32 devices in a mesh: seq: 4 (over z), exp: 8 (over y, x, core).
Axes of the slice: x: 2, y: 2, z: 4, core: 2. Of those that a mesh axis runs over, the one named last changes fastest.
Arguments:
- inputs: bfloat16 [8, 512, 4096], P('exp', 'seq'), may hold values from -6 to 6
- b_proj: bfloat16 [8, 512, 128], P('exp', 'seq'), may hold values from -0.046875 to 0.046875
- c_proj: bfloat16 [8, 512, 128], P('exp', 'seq'), may hold values from -6 to 6
- log_decay: float32 [8, 32, 512], P('exp', None, 'seq'), may hold values from -1.1 to 0, as said below
- doc_lengths: int32 [8, 6], P('exp'), may hold values from 1 to 256, 512 in all within a row
- expert_ids: int32 [8, 512, 2], P('exp', 'seq'), may hold values from 0 to 7, all different within a row; in each aligned block of 128 rows (0 to 127, 128 to 255, ..., all dimensions but the last counted through in order) at most 48 rows name the same one
- gate_weights: float32 [8, 512, 2], P('exp', 'seq'), may hold values from 0.2 to 1
- w_up: bfloat16 [8, 4096, 1024], P('exp'), may hold values from -0.09375 to 0.09375
- w_down: bfloat16 [8, 1024, 4096], P('exp'), may hold values from -0.1875 to 0.1875
- cotangent: bfloat16 [8, 512, 4096], P('exp', 'seq'), may hold values from -6 to 6
Outputs:
- output: bfloat16 [8, 512, 4096], P('exp', 'seq')
- input_grad: bfloat16 [8, 512, 4096], P('exp', 'seq')
The draws below stay inside these ranges and needn't reach their ends.
Inputs may be any that keep to these rules, and one draw needn't show every extreme that they name: `log_decay`: log of a decay factor, below zero. `doc_lengths`: each sequence's document lengths sum to 512. `expert_ids`: two different experts a position; among the 128 positions of one device no expert is named more than 48 times, a bound that some block reaches.
All inputs are finite; a program needn't handle non-finite values.
Results may differ from the reference program's by a relative error of at most 0.013.
Values may be sent and summed in bfloat16 or wider, within the bound.
No kernel may reach another device: no remote copies, remote signals or barrier semaphores. Data moves between devices by JAX's collectives and lax.ppermute only.
A program may use at most 128 MiB of HBM per device.

```python
import math
import jax
import jax.numpy as jnp
import numpy as np
from jax import lax

D = 4096
H = 32
P_SIZE = 128
N = 128
HID = 1024
BLOCK = 128
DOCS = 6
TOK_DEV = 128
STREAM_TOTAL = 8
STREAM_SPAN = 512
EXPERTS = 8
CAP = 48
N_SEQ = 4
N_EXP = 8


def draw_log_decay(key, part):
    stochastic_seed_array = jax.random.split(key, 7)
    fast_share = 0.5
    head_pick = jax.random.uniform(stochastic_seed_array[0], (STREAM_TOTAL, H, 1))
    fast_rate = jnp.exp(jax.random.uniform(stochastic_seed_array[1], (STREAM_TOTAL, H, 1), minval=math.log(0.046), maxval=math.log(0.077)))
    slow_rate = jnp.exp(jax.random.uniform(stochastic_seed_array[2], (STREAM_TOTAL, H, 1), minval=math.log(0.05), maxval=math.log(0.4))) / STREAM_SPAN
    resting_frequency = jnp.where(head_pick < fast_share, fast_rate, slow_rate)
    each_chip_multiplier = jnp.exp(jax.random.uniform(stochastic_seed_array[3], (STREAM_TOTAL, H, STREAM_SPAN // TOK_DEV), minval=-0.693, maxval=0.693))
    each_chip_multiplier = jnp.repeat(each_chip_multiplier, TOK_DEV, axis=2)
    storage_unit_multiplier = jnp.exp(jax.random.uniform(stochastic_seed_array[4], (STREAM_TOTAL, H, STREAM_SPAN), minval=-0.693, maxval=0.693))
    spike_location = jax.random.randint(stochastic_seed_array[5], (STREAM_TOTAL, 2, 1), 0, STREAM_SPAN)
    spike_amplitude = jax.random.uniform(stochastic_seed_array[6], (STREAM_TOTAL, 2, 1), minval=math.log(0.5), maxval=math.log(0.8))
    element_offsets = jnp.arange(STREAM_SPAN, dtype=jnp.int32)[None, None, :]
    spike_attenuation = jnp.sum(jnp.where(spike_location == element_offsets, spike_amplitude, 0.0), axis=1)
    return (spike_attenuation[:, None, :] - resting_frequency * each_chip_multiplier * storage_unit_multiplier).astype(jnp.float32)


def steps_of(own_key, dims, pieces, smallest, high):
    def one(dim, shards_of):
        steps = jax.random.uniform(jax.random.fold_in(jax.random.fold_in(own_key, 6), dim), (shards_of,), jnp.float32, smallest / len(pieces), high / len(pieces))
        return jnp.repeat(jnp.exp(steps), dims[dim] // shards_of).reshape((-1,) + (1,) * (len(dims) - dim - 1))

    gain = one(*pieces[0])
    for cut in pieces[1:]:
        gain = gain * one(*cut)
    return gain


def profile(number_of, total, most, lean):
    portions = [(1 << 20) // math.isqrt(rank ** lean) + 1 for rank in range(2, number_of + 1)]
    surplus, counts = total - most - (number_of - 1), [1] * (number_of - 1)
    while surplus > 0:
        movable = [i for i in range(number_of - 1) if counts[i] < most]
        pool, remaining = sum([portions[i] for i in movable]), surplus
        for i in movable:
            addition = min(most - counts[i], max(1, remaining * portions[i] // pool), surplus)
            counts[i] = counts[i] + addition
            surplus = surplus - addition
    return np.array([most] + counts)


def ragged(key, amount, total, bound, slope):
    if amount == 2:
        one = jax.random.randint(key, (), max(1, total - bound), min(bound, total - 1) + 1)
        return jnp.stack([one, total - one])
    sizes = jnp.asarray(profile(amount, total, bound, slope), jnp.int32)
    pairs = (amount - 1) // 2
    giver, taker = sizes[1:1 + 2 * pairs:2], sizes[2:2 + 2 * pairs:2]
    room = jnp.minimum(giver - 1, bound - taker)
    moved = jax.random.randint(jax.random.fold_in(key, 1), (pairs,), 0, 1 << 20) % (room + 1)
    sizes = sizes.at[1:1 + 2 * pairs:2].set(giver - moved).at[2:2 + 2 * pairs:2].set(taker + moved)
    return sizes[jax.random.permutation(jax.random.fold_in(key, 2), amount)]


def deal_out(key, own, number, rows, amount, top, bound, slope):
    ranking = jax.random.permutation(key, amount)
    crowded, common = portions_of(amount, rows * top, bound, slope, True), portions_of(amount, rows * top, bound, slope, False)
    places = jnp.arange(amount)

    def named(sizes, offset_by):
        used = int((sizes > 0).sum())
        fixed = max(1, used // 4)
        shifted = fixed + (places - fixed + offset_by * (used - fixed)) % max(1, amount - fixed)
        return jnp.zeros((amount,), jnp.int32).at[ranking[jnp.where(places < fixed, places, shifted)]].set(jnp.asarray(sizes, jnp.int32))

    sizes = jnp.where(number % 4 == 0, named(crowded, number // 4), named(common, number - number // 4 - 1))
    mixed = jax.random.permutation(jax.random.fold_in(own, 3), amount)
    source_of, taker = mixed[0:amount // 2 * 2:2], mixed[1:amount // 2 * 2:2]
    slack = jnp.minimum(sizes[source_of] - 1, bound - sizes[taker]) // 2
    slack = jnp.where((source_of == ranking[0]) | (taker == ranking[0]) | (sizes[taker] == 0), 0, jnp.maximum(slack, 0))
    shifted = jax.random.randint(jax.random.fold_in(own, 4), (amount // 2,), 0, 1 << 20) % (slack + 1)
    sizes = sizes.at[source_of].add(-shifted).at[taker].add(shifted)
    members = jnp.searchsorted(jnp.cumsum(sizes), jnp.arange(rows * top), side="right").astype(jnp.int32)
    table = members.reshape(top, rows).T
    table = table[jax.random.permutation(jax.random.fold_in(own, 1), rows)]
    offset_by = jax.random.randint(jax.random.fold_in(own, 2), (rows, 1), 0, top)
    return jnp.take_along_axis(table, (jnp.arange(top)[None, :] + offset_by) % top, axis=1)


def portions_of(count, total, bound, skew, full):
    weights = [(1 << 20) // math.isqrt(standing ** skew) + 1 for standing in range(1, count + 1)]
    largest = bound if full else min(bound, max(-(-total // count), total * weights[0] // sum(weights)))
    least = 1 if total - largest >= count - 1 else 0
    given, surplus = [largest] + [least] * (count - 1), total - largest - least * (count - 1)
    while surplus > 0:
        free = [i for i in range(1, count) if given[i] < largest] or [i for i in range(1, count) if given[i] < bound]
        mass, remaining = sum([weights[i] for i in free]), surplus
        for i in free:
            extra = min(bound - given[i], max(1, remaining * weights[i] // mass), surplus)
            given[i] = given[i] + extra
            surplus = surplus - extra
    return np.array(given)


def bell_draw(key, dims, scale, most, pieces=(), kind=jnp.bfloat16):
    gain = steps_of(key, dims, pieces, -0.22, 0.18) if pieces else 1.0
    drawn = jax.random.normal(key, dims, jnp.float32) * scale * gain
    return jnp.minimum(jnp.maximum(drawn, -most), most).astype(kind)


def setup_inputs(seed: int = 0) -> dict:
    streams_of = jax.random.split(jax.random.key(seed), 11)
    inputs = bell_draw(streams_of[0], (STREAM_TOTAL, STREAM_SPAN, D), 1.0, 6.0, ((0, 8), (1, 4)))
    b_proj = bell_draw(streams_of[1], (STREAM_TOTAL, STREAM_SPAN, N), (N * BLOCK) ** -0.5, 0.046875, ((0, 8), (1, 4)))
    c_proj = bell_draw(streams_of[2], (STREAM_TOTAL, STREAM_SPAN, N), 1.0, 6.0, ((0, 8), (1, 4)))
    log_decay = draw_log_decay(jax.random.fold_in(streams_of[10], 71), 0)
    doc_lengths = jax.vmap(lambda own: ragged(own, DOCS, STREAM_SPAN, STREAM_SPAN // 2, 1))(jax.random.split(streams_of[4], STREAM_TOTAL)).reshape((STREAM_TOTAL, DOCS)).astype(jnp.int32)
    expert_ids_keys = jax.random.split(jax.random.fold_in(streams_of[5], 1), STREAM_TOTAL * STREAM_SPAN // TOK_DEV)
    expert_ids_turns = jax.random.permutation(jax.random.fold_in(streams_of[5], 3), STREAM_TOTAL * STREAM_SPAN // TOK_DEV)
    expert_ids = jax.vmap(lambda own, number: deal_out(jax.random.fold_in(streams_of[5], 2), own, number, TOK_DEV, EXPERTS, 2, CAP, 2))(expert_ids_keys, expert_ids_turns).reshape((STREAM_TOTAL, STREAM_SPAN, 2))
    gate_weights = jnp.clip(0.2 + 0.8 * jax.random.uniform(streams_of[6], (STREAM_TOTAL, STREAM_SPAN, 2), jnp.float32) ** steps_of(streams_of[6], (STREAM_TOTAL, STREAM_SPAN, 2), ((0, 8), (1, 4)), -0.2, 0.2), 0.2, 1.0)
    w_up = bell_draw(streams_of[7], (EXPERTS, D, HID), D ** -0.5, 0.09375, ((0, 8),))
    w_down = bell_draw(streams_of[8], (EXPERTS, HID, D), HID ** -0.5, 0.1875, ((0, 8),))
    cotangent = bell_draw(streams_of[9], (STREAM_TOTAL, STREAM_SPAN, D), 1.0, 6.0, ((0, 8), (1, 4)))
    return dict(inputs=inputs, b_proj=b_proj, c_proj=c_proj, log_decay=log_decay, doc_lengths=doc_lengths, expert_ids=expert_ids, gate_weights=gate_weights, w_up=w_up, w_down=w_down, cotangent=cotangent)


EPSILON = 1e-06
HIGHEST_PREC = lax.Precision.HIGHEST

def doc_index(starts, element_offsets):
    return lax.optimization_barrier(jnp.sum((starts[None, :] <= element_offsets[:, None]).astype(jnp.int32), axis=1)) - 1

def chain_states(retained, terms, backward):
    block_count = retained.shape[0]

    def advance(index, carry):
        state, stored = carry
        where_now = block_count - 1 - index if backward else index
        stored = lax.dynamic_update_index_in_dim(stored, state, where_now, 0)
        decay_now = lax.dynamic_index_in_dim(retained, where_now, 0, keepdims=False)
        term_now = lax.dynamic_index_in_dim(terms, where_now, 0, keepdims=False)
        state = decay_now[:, None, None] * state + term_now
        return (state, stored)
    start_state = jnp.zeros_like(terms[0])
    _, stored = lax.fori_loop(0, block_count, advance, (start_state, jnp.zeros_like(terms)))
    return stored

def block_terms(x_blocks, b_blocks, c_blocks, log_blocks, doc_of, doc_before):
    span_len = log_blocks.shape[2]
    cumulative = jnp.cumsum(log_blocks, axis=2)
    lower = jnp.arange(span_len)[:, None] >= jnp.arange(span_len)[None, :]
    same_doc = (doc_of[:, :, None] == doc_of[:, None, :]) & lower[None]
    spread = cumulative[:, :, :, None] - cumulative[:, :, None, :]
    decay_pairs = jnp.where(same_doc[:, None], jnp.exp(jnp.minimum(spread, 0.0)), 0.0)
    scores = jnp.einsum('ktn,ksn->kts', c_blocks.astype(jnp.float32), b_blocks.astype(jnp.float32), precision=HIGHEST_PREC)
    mixing = (decay_pairs * scores[:, None]).astype(jnp.bfloat16)
    opened = (doc_of == doc_before[:, None]).astype(jnp.float32)
    tail_mask = (doc_of == doc_of[:, -1:]).astype(jnp.float32)
    last_cum = cumulative[:, :, -1:]
    c_weighted = (opened[:, None, :, None] * jnp.exp(cumulative)[..., None] * c_blocks[:, None].astype(jnp.float32)).astype(jnp.bfloat16)
    b_weighted = (tail_mask[:, None, :, None] * jnp.exp(last_cum - cumulative)[..., None] * b_blocks[:, None].astype(jnp.float32)).astype(jnp.bfloat16)
    retained = opened[:, -1:] * jnp.exp(last_cum[:, :, 0])
    local_state = jnp.einsum('kshp,khsn->khpn', x_blocks.astype(jnp.float32), b_weighted.astype(jnp.float32), precision=HIGHEST_PREC)
    return (mixing, c_weighted, b_weighted, retained, local_state)

def sequence_blocks(x_seq, b_seq, c_seq, log_seq, lengths):
    block_count = STREAM_SPAN // BLOCK
    starts = (jnp.cumsum(lengths) - lengths).astype(jnp.int32)
    doc_of = doc_index(starts, jnp.arange(STREAM_SPAN, dtype=jnp.int32)).reshape(block_count, BLOCK)
    doc_before = doc_index(starts, jnp.arange(block_count, dtype=jnp.int32) * BLOCK - 1)
    x_blocks = x_seq.reshape(block_count, BLOCK, H, P_SIZE)
    log_blocks = log_seq.reshape(H, block_count, BLOCK).transpose(1, 0, 2)
    terms = block_terms(x_blocks, b_seq.reshape(block_count, BLOCK, N), c_seq.reshape(block_count, BLOCK, N), log_blocks, doc_of, doc_before)
    return (x_blocks, terms)

def sequence_forward(x_seq, b_seq, c_seq, log_seq, lengths):
    x_blocks, terms = sequence_blocks(x_seq, b_seq, c_seq, log_seq, lengths)
    mixing, c_weighted, b_weighted, retained, local_state = terms
    state_in = chain_states(retained, local_state, False)
    inner = jnp.einsum('khts,kshp->kthp', mixing.astype(jnp.float32), x_blocks.astype(jnp.float32), precision=HIGHEST_PREC)
    carried = jnp.einsum('khpn,khtn->kthp', state_in, c_weighted.astype(jnp.float32), precision=HIGHEST_PREC)
    return (inner + carried).astype(jnp.bfloat16).reshape(STREAM_SPAN, D)

def sequence_backward(x_seq, b_seq, c_seq, log_seq, lengths, grad_seq):
    x_blocks, terms = sequence_blocks(x_seq, b_seq, c_seq, log_seq, lengths)
    mixing, c_weighted, b_weighted, retained, local_state = terms
    block_count = STREAM_SPAN // BLOCK
    grad_blocks = grad_seq.reshape(block_count, BLOCK, H, P_SIZE).astype(jnp.float32)
    sources = jnp.einsum('kthp,khtn->khpn', grad_blocks, c_weighted.astype(jnp.float32), precision=HIGHEST_PREC)
    state_after = chain_states(retained, sources, True)
    inner = jnp.einsum('khts,kthp->kshp', mixing.astype(jnp.float32), grad_blocks, precision=HIGHEST_PREC)
    carried = jnp.einsum('khpn,khsn->kshp', state_after, b_weighted.astype(jnp.float32), precision=HIGHEST_PREC)
    return (inner + carried).astype(jnp.bfloat16).reshape(STREAM_SPAN, D)

def expert_rows(rows_in, rows_grad, expert_up, expert_down):
    pre_act = jnp.dot(rows_in, expert_up, preferred_element_type=jnp.float32)
    gate_sig = jax.nn.sigmoid(pre_act)
    activated = (pre_act * gate_sig).astype(jnp.bfloat16)
    expert_out = jnp.dot(activated, expert_down, preferred_element_type=jnp.float32).astype(jnp.bfloat16)
    back_hidden = jnp.dot(rows_grad, expert_down.T, preferred_element_type=jnp.float32)
    pre_grad = (back_hidden * gate_sig * (1.0 + pre_act * (1.0 - gate_sig))).astype(jnp.bfloat16)
    expert_grad = jnp.dot(pre_grad, expert_up.T, preferred_element_type=jnp.float32).astype(jnp.bfloat16)
    return (expert_out, expert_grad)

def reference(inputs, b_proj, c_proj, log_decay, doc_lengths, expert_ids, gate_weights, w_up, w_down, cotangent):
    resid = jnp.stack([sequence_forward(inputs[s], b_proj[s], c_proj[s], log_decay[s], doc_lengths[s]) for s in range(STREAM_TOTAL)])
    resid_rows = resid.reshape(-1, D).astype(jnp.float32)
    scale_rows = lax.rsqrt(lax.optimization_barrier(jnp.mean(resid_rows * resid_rows, axis=1, keepdims=True)) + EPSILON)
    normed = resid_rows * scale_rows
    mixed_in = normed.astype(jnp.bfloat16)
    grad_rows = cotangent.reshape(-1, D)
    expert_flat = expert_ids.reshape(-1)
    weight_flat = gate_weights.reshape(-1)
    slot_total = expert_flat.shape[0]
    row_bound = CAP * N_EXP * N_SEQ

    def per_expert(accumulated, expert_number):
        picked_rows = jnp.nonzero(expert_flat == expert_number, size=row_bound, fill_value=slot_total)[0].astype(jnp.int32)
        valid_rows = picked_rows < slot_total
        token_rows = jnp.where(valid_rows, picked_rows // 2, 0)
        weight_pick = jnp.where(valid_rows, weight_flat[jnp.minimum(picked_rows, slot_total - 1)], 0.0)[:, None]
        expert_out, expert_grad = expert_rows(mixed_in[token_rows], grad_rows[token_rows], w_up[expert_number], w_down[expert_number])
        moe_sum = accumulated[0].at[token_rows].add(weight_pick * expert_out.astype(jnp.float32))
        grad_sum = accumulated[1].at[token_rows].add(weight_pick * expert_grad.astype(jnp.float32))
        return ((moe_sum, grad_sum), None)
    zero_rows = jnp.zeros_like(resid_rows)
    (moe_rows, dmixed), _ = lax.scan(per_expert, (zero_rows, zero_rows), jnp.arange(EXPERTS, dtype=jnp.int32))
    output = (resid_rows + moe_rows).astype(jnp.bfloat16).reshape(STREAM_TOTAL, STREAM_SPAN, D)
    dresid = (grad_rows.astype(jnp.float32) + scale_rows * (dmixed - normed * lax.optimization_barrier(jnp.mean(dmixed * normed, axis=1, keepdims=True)))).astype(jnp.bfloat16)
    dresid_seq = dresid.reshape(STREAM_TOTAL, STREAM_SPAN, D)
    input_grad = jnp.stack([sequence_backward(inputs[s], b_proj[s], c_proj[s], log_decay[s], doc_lengths[s], dresid_seq[s]) for s in range(STREAM_TOTAL)])
    return (output, input_grad)
```

```python
import functools

import jax
import jax.numpy as jnp
from jax import lax
from jax.experimental import pallas as pl
from jax.experimental.pallas import tpu as pltpu
from jax.sharding import PartitionSpec as P

EPSILON = 1e-06
F32 = jnp.float32
BF16 = jnp.bfloat16
HEADS_STEP = 8
VMEM_BYTES = 48 * 1024 * 1024
NT = (((1,), (1,)), ((), ()))


def dot(a, b):
    return jnp.dot(a, b, preferred_element_type=F32)


def dot_nt(a, b):
    return lax.dot_general(a, b, NT, preferred_element_type=F32)


def call(kernel, grid, in_specs, out_specs, out_shape, flops, nbytes, name, scratch=()):
    return pl.pallas_call(
        kernel,
        grid=grid,
        in_specs=in_specs,
        out_specs=out_specs,
        out_shape=out_shape,
        scratch_shapes=scratch,
        name=name,
        cost_estimate=pl.CostEstimate(flops=flops, bytes_accessed=nbytes, transcendentals=0),
        compiler_params=pltpu.CompilerParams(vmem_limit_bytes=VMEM_BYTES),
    )


def whole(shape):
    return pl.BlockSpec(shape, lambda i: (0,) * len(shape))


def columns(rows, width):
    return pl.BlockSpec((rows, width), lambda i: (0, i))


SMEM = pl.BlockSpec(memory_space=pltpu.SMEM)


def documents(meta, rows, size):
    count = meta.shape[0] - 1
    first = meta[count]
    along = first + lax.broadcasted_iota(jnp.int32, (1, size), 1)
    down = first + lax.broadcasted_iota(jnp.int32, (size, 1), 0)
    row = jnp.full((1, size), -1, jnp.int32)
    col = jnp.full((size, 1), -1, jnp.int32)
    before, last, start = jnp.int32(-1), jnp.int32(-1), jnp.int32(0)
    for i in range(count):
        row += (start <= along).astype(jnp.int32)
        col += (start <= down).astype(jnp.int32)
        before += (start <= first - 1).astype(jnp.int32)
        last += (start <= first + size - 1).astype(jnp.int32)
        start = start + meta[i]
    return row, col, before, last


def running(log_ref):
    size = log_ref.shape[1]
    upto = (
        lax.broadcasted_iota(jnp.int32, (size, size), 0)
        <= lax.broadcasted_iota(jnp.int32, (size, size), 1)
    ).astype(F32)
    return jnp.dot(
        log_ref[...], upto, precision=lax.Precision.HIGHEST, preferred_element_type=F32
    )


def head(h, size):
    return slice(h * size, (h + 1) * size)


def local_kernel(meta, log_ref, b_ref, x_ref, state_ref):
    size = log_ref.shape[1]
    cum = running(log_ref)
    row, _, _, last = documents(meta, cum.shape[0], size)
    tail = (row == last).astype(F32)
    weight = tail * jnp.exp(cum[:, size - 1 :] - cum)
    b_t = b_ref[...].astype(F32).T
    p = x_ref.shape[1] // cum.shape[0]
    for h in range(cum.shape[0]):
        b_weighted = (b_t * weight[h : h + 1, :]).astype(BF16)
        state_ref[:, head(h, p)] = dot(b_weighted, x_ref[:, head(h, p)]).astype(BF16)


def pair_mask(meta, size):
    row, col, before, last = documents(meta, size, size)
    later = lax.broadcasted_iota(jnp.int32, (size, size), 0)
    earlier = lax.broadcasted_iota(jnp.int32, (size, size), 1)
    return row, col, before, last, later, earlier


def inner_kernel(meta, log_ref, b_ref, c_ref, x_ref, out_ref):
    size = log_ref.shape[1]
    cum = running(log_ref)
    cum_t = cum.T
    row, col, _, _, down, along = pair_mask(meta, size)
    scores = jnp.where((row == col) & (down >= along), dot_nt(c_ref[...], b_ref[...]), 0.0)
    p = x_ref.shape[1] // cum.shape[0]
    for h in range(cum.shape[0]):
        spread = cum_t[:, h : h + 1] - cum[h : h + 1, :]
        pair = (jnp.exp(jnp.minimum(spread, 0.0)) * scores).astype(BF16)
        out_ref[:, head(h, p)] = dot(pair, x_ref[:, head(h, p)])


def inner_back_kernel(meta, log_ref, b_ref, c_ref, grad_ref, out_ref):
    size = log_ref.shape[1]
    cum = running(log_ref)
    cum_t = cum.T
    row, col, _, _, down, along = pair_mask(meta, size)
    scores = jnp.where((row == col) & (down <= along), dot_nt(b_ref[...], c_ref[...]), 0.0)
    p = grad_ref.shape[1] // cum.shape[0]
    for h in range(cum.shape[0]):
        spread = cum[h : h + 1, :] - cum_t[:, h : h + 1]
        pair = (jnp.exp(jnp.minimum(spread, 0.0)) * scores).astype(BF16)
        out_ref[:, head(h, p)] = dot(pair, grad_ref[:, head(h, p)])


def keep_kernel(meta, log_ref, state_ref, out_ref):
    size = log_ref.shape[1]
    total = jnp.exp(running(log_ref)[:, size - 1 :])
    _, _, before, last = documents(meta, 1, size)
    total = jnp.where(before == last, total, 0.0)
    p = state_ref.shape[1] // total.shape[0]
    for h in range(total.shape[0]):
        out_ref[:, head(h, p)] = (
            state_ref[:, head(h, p)].astype(F32) * total[h : h + 1, :]
        ).astype(BF16)


def resid_kernel(hops, meta, log_ref, c_ref, pick_ref, inner_ref, *refs):
    states, (resid_ref, sent_ref, scale_ref) = refs[:hops], refs[hops:]
    size = log_ref.shape[1]
    features = inner_ref.shape[1] * pl.num_programs(0)
    _, col, before, _ = documents(meta, size, size)
    weight = jnp.where(col == before, jnp.exp(running(log_ref).T), 0.0)
    p = inner_ref.shape[1] // log_ref.shape[0]
    squares = jnp.zeros((size, p), F32)
    for h in range(log_ref.shape[0]):
        carried = dot(c_ref[...], states[0][:, head(h, p)])
        for state in states[1:]:
            carried += dot(c_ref[...], state[:, head(h, p)])
        rows = (inner_ref[:, head(h, p)] + weight[:, h : h + 1] * carried).astype(BF16)
        resid_ref[:, head(h, p)] = rows
        squares += rows.astype(F32) * rows.astype(F32)
    sent_ref[...] = dot(pick_ref[...], resid_ref[...]).astype(BF16)
    squares = jnp.broadcast_to(jnp.sum(squares, axis=1, keepdims=True), scale_ref.shape)
    step = pl.program_id(0)

    @pl.when(step == 0)
    def _():
        scale_ref[...] = squares

    @pl.when(step > 0)
    def _():
        scale_ref[...] += squares

    @pl.when(step == pl.num_programs(0) - 1)
    def _():
        scale_ref[...] = lax.rsqrt(scale_ref[...] / features + EPSILON)


def dresid_kernel(meta, log_ref, c_ref, high_ref, low_ref, scale_ref, cot_ref, got_ref, dresid_ref, source_ref):
    size = log_ref.shape[1]
    row, _, before, _ = documents(meta, size, size)
    weight = jnp.where(row == before, jnp.exp(running(log_ref)), 0.0)
    c_t = c_ref[...].astype(F32).T
    got = got_ref[...]
    moved = dot(high_ref[...], got) + dot(low_ref[...], got)
    dresid_ref[...] = (cot_ref[...].astype(F32) + scale_ref[:, :1] * moved).astype(BF16)
    p = cot_ref.shape[1] // log_ref.shape[0]
    for h in range(log_ref.shape[0]):
        c_weighted = (c_t * weight[h : h + 1, :]).astype(BF16)
        source_ref[:, head(h, p)] = dot(c_weighted, dresid_ref[:, head(h, p)]).astype(BF16)


def grad_kernel(hops, meta, log_ref, b_ref, inner_ref, *refs):
    states, out_ref = refs[:hops], refs[hops]
    size = log_ref.shape[1]
    _, col, _, last = documents(meta, size, size)
    cum = running(log_ref)
    weight = jnp.where(col == last, jnp.exp(cum[:, size - 1 :] - cum).T, 0.0)
    p = inner_ref.shape[1] // log_ref.shape[0]
    for h in range(log_ref.shape[0]):
        carried = dot(b_ref[...], states[0][:, head(h, p)])
        for state in states[1:]:
            carried += dot(b_ref[...], state[:, head(h, p)])
        out_ref[:, head(h, p)] = (inner_ref[:, head(h, p)] + weight[:, h : h + 1] * carried).astype(BF16)


def output_kernel(high_ref, low_ref, resid_ref, got_ref, out_ref):
    got = got_ref[...]
    moved = dot(high_ref[...], got) + dot(low_ref[...], got)
    out_ref[...] = (resid_ref[...].astype(F32) + moved).astype(BF16)


def pick_kernel(experts, capacity, ids_ref, gate_ref, cot_ref, pick_ref, high_ref, low_ref, sent_ref):
    tokens = ids_ref.shape[1]

    @pl.when(pl.program_id(0) == 0)
    def _():
        expert = lax.broadcasted_iota(jnp.int32, (experts, tokens), 0)
        first, second = ids_ref[0:1, :] == expert, ids_ref[1:2, :] == expert
        named = (first | second).astype(F32)
        gate = jnp.where(first, gate_ref[0:1, :], 0.0) + jnp.where(second, gate_ref[1:2, :], 0.0)
        before = (
            lax.broadcasted_iota(jnp.int32, (tokens, tokens), 0)
            < lax.broadcasted_iota(jnp.int32, (tokens, tokens), 1)
        ).astype(BF16)
        rank = jnp.where(named > 0, dot(named.astype(BF16), before), -1.0)
        slot = lax.broadcasted_iota(jnp.int32, (capacity, tokens), 0).astype(F32)
        picks, gates = [], []
        for e in range(experts):
            pick = (rank[e : e + 1, :] == slot).astype(F32)
            picks.append(pick)
            gates.append(pick * gate[e : e + 1, :])
        pick_ref[...] = jnp.concatenate(picks, axis=0).astype(BF16)
        gates = jnp.concatenate(gates, axis=0).T
        high = gates.astype(BF16)
        high_ref[...] = high
        low_ref[...] = (gates - high.astype(F32)).astype(BF16)

    sent_ref[...] = dot(pick_ref[...], cot_ref[...]).astype(BF16)


def back_kernel(rows_ref, down_ref, back_ref):
    part = dot_nt(rows_ref[...], down_ref[...])

    @pl.when(pl.program_id(0) == 0)
    def _():
        back_ref[...] = part

    @pl.when(pl.program_id(0) > 0)
    def _():
        back_ref[...] += part


def up_kernel(rows_ref, up_ref, back_ref, act_ref, pre_grad_ref, along_ref, total, squares):
    step, steps = pl.program_id(0), pl.num_programs(0)
    features = rows_ref.shape[1] * steps
    part = dot(rows_ref[...], up_ref[...])
    rows = rows_ref[...].astype(F32)
    square = jnp.sum(rows * rows, axis=1, keepdims=True)

    @pl.when(step == 0)
    def _():
        total[...] = part
        squares[...] = jnp.broadcast_to(square, squares.shape)

    @pl.when(step > 0)
    def _():
        total[...] += part
        squares[...] += jnp.broadcast_to(square, squares.shape)

    @pl.when(step == steps - 1)
    def _():
        scale = lax.rsqrt(squares[:, :1] / features + EPSILON)
        pre = total[...] * scale
        gate = jax.nn.sigmoid(pre)
        act_ref[...] = (pre * gate).astype(BF16)
        pre_grad = (back_ref[...] * gate * (1.0 + pre * (1.0 - gate))).astype(BF16)
        pre_grad_ref[...] = pre_grad
        along = jnp.sum(pre_grad.astype(F32) * pre, axis=1, keepdims=True)
        along_ref[...] = jnp.broadcast_to(scale * along / features, along_ref.shape)


def expert_grad_kernel(pre_grad_ref, up_ref, rows_ref, along_ref, out_ref):
    out_ref[...] = (
        dot_nt(pre_grad_ref[...], up_ref[...]) - rows_ref[...].astype(F32) * along_ref[:, :1]
    ).astype(BF16)


def expert_out_kernel(act_ref, down_ref, out_ref):
    out_ref[...] = dot(act_ref[...], down_ref[...]).astype(BF16)


def exchange(rows, experts):
    parts = rows.reshape(experts, rows.shape[0] // experts, rows.shape[1])
    return lax.all_to_all(parts, "exp", split_axis=0, concat_axis=0, tiled=True).reshape(rows.shape)


def on_device(inputs, b_proj, c_proj, log_decay, doc_lengths, expert_ids, gate_weights, w_up, w_down, cotangent):
    tokens, features = inputs.shape[1:]
    heads = log_decay.shape[1]
    state = b_proj.shape[2]
    experts, blocks = lax.axis_size("exp"), lax.axis_size("seq")
    hidden = w_up.shape[2]
    capacity = 3 * tokens // experts
    slots = experts * capacity
    steps = heads // HEADS_STEP
    width = features // steps
    hops = max(1, blocks // 2)

    x, b, c, log, cot = inputs[0], b_proj[0], c_proj[0], log_decay[0], cotangent[0]
    up, down = w_up[0], w_down[0]
    meta = jnp.concatenate([doc_lengths[0], (lax.axis_index("seq") * tokens)[None].astype(jnp.int32)])

    log_spec = pl.BlockSpec((HEADS_STEP, tokens), lambda i: (i, 0))
    part, small = columns(tokens, width), whole((tokens, state))
    rows_f32 = jax.ShapeDtypeStruct((tokens, features), F32)
    rows_bf16 = jax.ShapeDtypeStruct((tokens, features), BF16)
    slots_bf16 = jax.ShapeDtypeStruct((slots, features), BF16)
    unit = tokens * features
    head_flops = 2 * tokens * unit

    pick, high, low, sent_cot = call(
        functools.partial(pick_kernel, experts, capacity),
        (steps,),
        [whole((2, tokens)), whole((2, tokens)), part],
        [whole((slots, tokens)), whole((tokens, slots)), whole((tokens, slots)), columns(slots, width)],
        [
            jax.ShapeDtypeStruct((slots, tokens), BF16),
            jax.ShapeDtypeStruct((tokens, slots), BF16),
            jax.ShapeDtypeStruct((tokens, slots), BF16),
            slots_bf16,
        ],
        2 * slots * unit,
        2 * (unit + slots * features),
        "pick_rows",
    )(expert_ids[0].T, gate_weights[0].T, cot)
    got_cot = exchange(sent_cot, experts)

    local = call(
        local_kernel, (steps,), [SMEM, log_spec, small, part], part, rows_bf16, head_flops, 4 * unit, "local_states"
    )(meta, log, b, x)

    keep = call(keep_kernel, (steps,), [SMEM, log_spec, part], part, rows_bf16, unit, 4 * unit, "keep_states")

    def passed(states, step):
        pairs = [(i, i + step) for i in range(blocks) if 0 <= i + step < blocks]
        arrived = [lax.ppermute(states, "seq", pairs)]
        for _ in range(hops - 1):
            arrived.append(lax.ppermute(keep(meta, log, arrived[-1]), "seq", pairs))
        return arrived

    states_in = passed(local, 1)
    inner = call(
        inner_kernel, (steps,), [SMEM, log_spec, small, small, part], part, rows_f32, 2 * head_flops, 6 * unit, "inner"
    )(meta, log, b, c, x)

    resid, sent_in, scale = call(
        functools.partial(resid_kernel, hops),
        (steps,),
        [SMEM, log_spec, small, whole((slots, tokens)), part] + [part] * hops,
        [part, columns(slots, width), whole((tokens, 128))],
        [rows_bf16, slots_bf16, jax.ShapeDtypeStruct((tokens, 128), F32)],
        hops * head_flops + 2 * slots * unit,
        (4 + 2 * hops + 2) * unit + 2 * slots * features,
        "resid",
    )(meta, log, c, pick, inner, *states_in)
    got_in = exchange(sent_in, experts)

    expert_flops = 2 * slots * features * hidden
    expert_bytes = 2 * features * (hidden + slots)
    chunk = features // 4
    slots_hidden = whole((slots, hidden))
    back = call(
        back_kernel,
        (4,),
        [columns(slots, chunk), columns(hidden, chunk)],
        slots_hidden,
        jax.ShapeDtypeStruct((slots, hidden), F32),
        expert_flops,
        expert_bytes,
        "back",
    )(got_cot, down)
    act, pre_grad, along = call(
        up_kernel,
        (4,),
        [columns(slots, chunk), pl.BlockSpec((chunk, hidden), lambda i: (i, 0)), slots_hidden],
        [slots_hidden, slots_hidden, whole((slots, 128))],
        [
            jax.ShapeDtypeStruct((slots, hidden), BF16),
            jax.ShapeDtypeStruct((slots, hidden), BF16),
            jax.ShapeDtypeStruct((slots, 128), F32),
        ],
        expert_flops,
        expert_bytes,
        "up",
        [pltpu.VMEM((slots, hidden), F32), pltpu.VMEM((slots, 128), F32)],
    )(got_in, up, back)
    expert_grad = call(
        expert_grad_kernel,
        (4,),
        [
            slots_hidden,
            pl.BlockSpec((chunk, hidden), lambda i: (i, 0)),
            columns(slots, chunk),
            whole((slots, 128)),
        ],
        columns(slots, chunk),
        slots_bf16,
        expert_flops,
        expert_bytes,
        "expert_grad",
    )(pre_grad, up, got_in, along)
    got_grad = exchange(expert_grad, experts)
    expert_out = call(
        expert_out_kernel,
        (4,),
        [slots_hidden, columns(hidden, chunk)],
        columns(slots, chunk),
        slots_bf16,
        expert_flops,
        expert_bytes,
        "expert_out",
    )(act, down)
    got_out = exchange(expert_out, experts)

    weights = [whole((tokens, slots))] * 2
    dresid, sources = call(
        dresid_kernel,
        (steps,),
        [SMEM, log_spec, small] + weights + [whole((tokens, 128)), part, columns(slots, width)],
        [part, part],
        [rows_bf16, rows_bf16],
        head_flops + 4 * slots * unit,
        6 * unit + 2 * slots * features,
        "dresid",
    )(meta, log, c, high, low, scale, cot, got_grad)
    states_after = passed(sources, -1)
    inner_back = call(
        inner_back_kernel,
        (steps,),
        [SMEM, log_spec, small, small, part],
        part,
        rows_f32,
        2 * head_flops,
        6 * unit,
        "inner_back",
    )(meta, log, b, c, dresid)
    input_grad = call(
        functools.partial(grad_kernel, hops),
        (steps,),
        [SMEM, log_spec, small, part] + [part] * hops,
        part,
        rows_bf16,
        hops * head_flops,
        (6 + 2 * hops) * unit,
        "input_grad",
    )(meta, log, b, inner_back, *states_after)
    output = call(
        output_kernel,
        (steps,),
        weights + [part, columns(slots, width)],
        part,
        rows_bf16,
        4 * slots * unit,
        4 * unit + 2 * slots * features,
        "output",
    )(high, low, resid, got_out)
    return (output[None], input_grad[None])


def solution(mesh):
    placed = (
        P("exp", "seq", None),
        P("exp", "seq", None),
        P("exp", "seq", None),
        P("exp", None, "seq"),
        P("exp", None),
        P("exp", "seq", None),
        P("exp", "seq", None),
        P("exp", None, None),
        P("exp", None, None),
        P("exp", "seq", None),
    )
    return jax.shard_map(
        on_device,
        mesh=mesh,
        in_specs=placed,
        out_specs=(P("exp", "seq", None), P("exp", "seq", None)),
        check_vma=False,
    )
```

```python
import functools

import jax
import jax.numpy as jnp
from jax import lax
from jax.experimental import pallas as pl
from jax.experimental.pallas import tpu as pltpu
from jax.sharding import PartitionSpec as P

EPSILON = 1e-06
F32 = jnp.float32
BF16 = jnp.bfloat16
CHUNKS = 2
VMEM_BYTES = 32 * 1024 * 1024
NT = (((1,), (1,)), ((), ()))


def dot(a, b):
    return jnp.dot(a, b, preferred_element_type=F32)


def dot_nt(a, b):
    return lax.dot_general(a, b, NT, preferred_element_type=F32)


def call(kernel, grid, in_specs, out_specs, out_shape, flops, nbytes, name, scratch=()):
    return pl.pallas_call(
        kernel,
        grid=grid,
        in_specs=in_specs,
        out_specs=out_specs,
        out_shape=out_shape,
        scratch_shapes=scratch,
        name=name,
        cost_estimate=pl.CostEstimate(flops=flops, bytes_accessed=nbytes, transcendentals=0),
        compiler_params=pltpu.CompilerParams(vmem_limit_bytes=VMEM_BYTES),
    )


def whole(shape):
    return pl.BlockSpec(shape, lambda i: (0,) * len(shape))


def columns(rows, width):
    return pl.BlockSpec((rows, width), lambda i: (0, i))


SMEM = pl.BlockSpec(memory_space=pltpu.SMEM)


def documents(meta, rows, size):
    count = meta.shape[0] - 1
    first = meta[count]
    along = first + lax.broadcasted_iota(jnp.int32, (1, size), 1)
    down = first + lax.broadcasted_iota(jnp.int32, (size, 1), 0)
    row = jnp.full((1, size), -1, jnp.int32)
    col = jnp.full((size, 1), -1, jnp.int32)
    before, last, start = jnp.int32(-1), jnp.int32(-1), jnp.int32(0)
    for i in range(count):
        row += (start <= along).astype(jnp.int32)
        col += (start <= down).astype(jnp.int32)
        before += (start <= first - 1).astype(jnp.int32)
        last += (start <= first + size - 1).astype(jnp.int32)
        start = start + meta[i]
    return row, col, before, last


def running(log_ref):
    size = log_ref.shape[1]
    upto = (
        lax.broadcasted_iota(jnp.int32, (size, size), 0)
        <= lax.broadcasted_iota(jnp.int32, (size, size), 1)
    ).astype(F32)
    return jnp.dot(
        log_ref[...], upto, precision=lax.Precision.HIGHEST, preferred_element_type=F32
    )


def head(h, size):
    return slice(h * size, (h + 1) * size)


def local_kernel(meta, log_ref, b_ref, x_ref, state_ref):
    size = log_ref.shape[1]
    cum = running(log_ref)
    row, _, _, last = documents(meta, cum.shape[0], size)
    tail = (row == last).astype(F32)
    weight = tail * jnp.exp(cum[:, size - 1 :] - cum)
    b_t = b_ref[...].astype(F32).T
    p = x_ref.shape[1] // cum.shape[0]
    for h in range(cum.shape[0]):
        b_weighted = (b_t * weight[h : h + 1, :]).astype(BF16)
        state_ref[:, head(h, p)] = dot(b_weighted, x_ref[:, head(h, p)]).astype(BF16)


def pair_mask(meta, size):
    row, col, before, last = documents(meta, size, size)
    later = lax.broadcasted_iota(jnp.int32, (size, size), 0)
    earlier = lax.broadcasted_iota(jnp.int32, (size, size), 1)
    return row, col, before, last, later, earlier


def inner_kernel(meta, log_ref, b_ref, c_ref, x_ref, out_ref):
    size = log_ref.shape[1]
    cum = running(log_ref)
    cum_t = cum.T
    row, col, _, _, down, along = pair_mask(meta, size)
    scores = jnp.where((row == col) & (down >= along), dot_nt(c_ref[...], b_ref[...]), 0.0)
    p = x_ref.shape[1] // cum.shape[0]
    for h in range(cum.shape[0]):
        spread = cum_t[:, h : h + 1] - cum[h : h + 1, :]
        pair = (jnp.exp(jnp.minimum(spread, 0.0)) * scores).astype(BF16)
        out_ref[:, head(h, p)] = dot(pair, x_ref[:, head(h, p)])


def inner_back_kernel(meta, log_ref, b_ref, c_ref, grad_ref, out_ref):
    size = log_ref.shape[1]
    cum = running(log_ref)
    cum_t = cum.T
    row, col, _, _, down, along = pair_mask(meta, size)
    scores = jnp.where((row == col) & (down <= along), dot_nt(b_ref[...], c_ref[...]), 0.0)
    p = grad_ref.shape[1] // cum.shape[0]
    for h in range(cum.shape[0]):
        spread = cum[h : h + 1, :] - cum_t[:, h : h + 1]
        pair = (jnp.exp(jnp.minimum(spread, 0.0)) * scores).astype(BF16)
        out_ref[:, head(h, p)] = dot(pair, grad_ref[:, head(h, p)])


def keep_kernel(meta, log_ref, state_ref, out_ref):
    size = log_ref.shape[1]
    total = jnp.exp(running(log_ref)[:, size - 1 :])
    _, _, before, last = documents(meta, 1, size)
    total = jnp.where(before == last, total, 0.0)
    p = state_ref.shape[1] // total.shape[0]
    for h in range(total.shape[0]):
        out_ref[:, head(h, p)] = (
            state_ref[:, head(h, p)].astype(F32) * total[h : h + 1, :]
        ).astype(BF16)


def resid_kernel(hops, meta, log_ref, c_ref, inner_ref, *refs):
    states, (resid_ref, squares_ref) = refs[:hops], refs[hops:]
    size = log_ref.shape[1]
    _, col, before, _ = documents(meta, size, size)
    weight = jnp.where(col == before, jnp.exp(running(log_ref).T), 0.0)
    p = inner_ref.shape[1] // log_ref.shape[0]
    squares = jnp.zeros((size, p), F32)
    for h in range(log_ref.shape[0]):
        carried = dot(c_ref[...], states[0][:, head(h, p)])
        for state in states[1:]:
            carried += dot(c_ref[...], state[:, head(h, p)])
        rows = (inner_ref[:, head(h, p)] + weight[:, h : h + 1] * carried).astype(BF16)
        resid_ref[:, head(h, p)] = rows
        squares += rows.astype(F32) * rows.astype(F32)
    squares_ref[...] = jnp.broadcast_to(jnp.sum(squares, axis=1, keepdims=True), squares_ref.shape)


def combined(weights_ref, pieces):
    total = dot(weights_ref[0], pieces[0][...])
    for i, piece in enumerate(pieces[1:]):
        total += dot(weights_ref[i + 1], piece[...])
    return total


def relay_kernel(weights_ref, *refs):
    pieces, out_ref = refs[:-1], refs[-1]
    out_ref[...] = combined(weights_ref, pieces).astype(BF16)


def dresid_kernel(chunks, features, meta, log_ref, c_ref, weights_ref, cot_ref, *refs):
    squares, refs = refs[:chunks], refs[chunks:]
    moved_refs, (dresid_ref, source_ref) = refs[:-2], refs[-2:]
    size = log_ref.shape[1]
    row, _, before, _ = documents(meta, size, size)
    weight = jnp.where(row == before, jnp.exp(running(log_ref)), 0.0)
    c_t = c_ref[...].astype(F32).T
    total = squares[0][...]
    for part in squares[1:]:
        total = total + part[...]
    scale = lax.rsqrt(total[:, :1] / features + EPSILON)
    count = weights_ref.shape[0]
    moved = combined(weights_ref, moved_refs[:count])
    for arrived in moved_refs[count:]:
        moved += arrived[...].astype(F32)
    dresid_ref[...] = (cot_ref[...].astype(F32) + scale * moved).astype(BF16)
    p = cot_ref.shape[1] // log_ref.shape[0]
    for h in range(log_ref.shape[0]):
        c_weighted = (c_t * weight[h : h + 1, :]).astype(BF16)
        source_ref[:, head(h, p)] = dot(c_weighted, dresid_ref[:, head(h, p)]).astype(BF16)


def grad_kernel(hops, meta, log_ref, b_ref, inner_ref, *refs):
    states, out_ref = refs[:hops], refs[-1]
    size = log_ref.shape[1]
    _, col, _, last = documents(meta, size, size)
    cum = running(log_ref)
    weight = jnp.where(col == last, jnp.exp(cum[:, size - 1 :] - cum).T, 0.0)
    p = inner_ref.shape[1] // log_ref.shape[0]
    for h in range(log_ref.shape[0]):
        carried = dot(b_ref[...], states[0][:, head(h, p)])
        for state in states[1:]:
            carried += dot(b_ref[...], state[:, head(h, p)])
        out_ref[:, head(h, p)] = (inner_ref[:, head(h, p)] + weight[:, h : h + 1] * carried).astype(BF16)


def output_kernel(weights_ref, resid_ref, *refs):
    out_ref = refs[-1]
    count = weights_ref.shape[0]
    moved = combined(weights_ref, refs[:count])
    for arrived in refs[count : len(refs) - 1]:
        if arrived.shape == out_ref.shape:
            moved += arrived[...].astype(F32)
    out_ref[...] = (resid_ref[...].astype(F32) + moved).astype(BF16)


def picks_of(table, me, experts, capacity):
    tokens = table.shape[1]
    offset = lax.broadcasted_iota(jnp.int32, (experts, tokens), 0)
    first = (table[0:1, :].astype(jnp.int32) ^ me) == offset
    second = (table[1:2, :].astype(jnp.int32) ^ me) == offset
    named = (first | second).astype(F32)
    gate = jnp.where(first, table[2:3, :], 0.0) + jnp.where(second, table[3:4, :], 0.0)
    before = (
        lax.broadcasted_iota(jnp.int32, (tokens, tokens), 0)
        < lax.broadcasted_iota(jnp.int32, (tokens, tokens), 1)
    ).astype(BF16)
    rank = jnp.where(named > 0, dot(named.astype(BF16), before), -1.0)
    slot = lax.broadcasted_iota(jnp.int32, (capacity, tokens), 0).astype(F32)
    picks = [(rank[e : e + 1, :] == slot).astype(F32) for e in range(experts)]
    return picks, [pick * gate[e : e + 1, :] for e, pick in enumerate(picks)]


def direct_pick_kernel(experts, capacity, table_ref, pick_ref, weights_ref):
    picks, gated = picks_of(table_ref[...], 0, experts, capacity)
    pick_ref[...] = jnp.concatenate(picks, axis=0).astype(BF16)
    weights_ref[0] = jnp.concatenate(gated, axis=0).T.astype(BF16)


def relay_pick_kernel(experts, capacity, kinds, me_ref, own_ref, *refs):
    tables, outs = refs[: len(kinds)], refs[len(kinds) :]
    me = me_ref[0]
    picks, gated = picks_of(own_ref[...], me, experts, capacity)
    none = jnp.zeros_like(picks[0])
    for (_, offsets), table_ref, (pick_ref, own_weights_ref, relay_weights_ref) in zip(
        kinds, tables, (outs[:3], outs[3:])
    ):
        other_picks, other_gated = picks_of(table_ref[...], me, experts, capacity)
        for i, o in enumerate(offsets):
            pick_ref[i, 0] = picks[o].astype(BF16)
            pick_ref[i, 1] = other_picks[o].astype(BF16)
            own_weights_ref[i] = jnp.concatenate([gated[o], none], axis=0).T.astype(BF16)
            relay_weights_ref[i] = jnp.concatenate([none, other_gated[o]], axis=0).T.astype(BF16)


def gather_kernel(pick_ref, own_ref, other_ref, *outs):
    capacity = pick_ref.shape[2]
    for i, out in enumerate(outs):
        out[:capacity, :] = dot(pick_ref[i, 0], own_ref[...]).astype(BF16)
        out[capacity:, :] = dot(pick_ref[i, 1], other_ref[...]).astype(BF16)


def direct_gather_kernel(pick_ref, own_ref, out_ref):
    out_ref[...] = dot(pick_ref[...], own_ref[...]).astype(BF16)


def assemble(plan, pieces, rows):
    for piece, at, to, count in plan:
        rows[to : to + count, :] = pieces[piece][at : at + count, :]


def back_kernel(plans, *refs):
    counts = [max(b[0] for b in plan) + 1 for plan in plans]
    pieces, (down_ref, back_ref, rows) = refs[: sum(counts)], refs[sum(counts) :]
    step, each = pl.program_id(0), pl.num_programs(0) // len(plans)
    for k, plan in enumerate(plans):
        mine = pieces[sum(counts[:k]) : sum(counts[: k + 1])]

        @pl.when(step // each == k)
        def _(plan=plan, mine=mine):
            assemble(plan, mine, rows)

    part = dot_nt(rows[...], down_ref[...])

    @pl.when(step == 0)
    def _():
        back_ref[...] = part

    @pl.when(step > 0)
    def _():
        back_ref[...] += part


def up_first_kernel(plan, *refs):
    pieces, (up_ref, total_ref, squares_ref, rows) = refs[:-4], refs[-4:]
    assemble(plan, pieces, rows)
    part = dot(rows[...], up_ref[...])
    values = rows[...].astype(F32)
    square = jnp.broadcast_to(jnp.sum(values * values, axis=1, keepdims=True), squares_ref.shape)

    @pl.when(pl.program_id(0) == 0)
    def _():
        total_ref[...] = part
        squares_ref[...] = square

    @pl.when(pl.program_id(0) > 0)
    def _():
        total_ref[...] += part
        squares_ref[...] += square


def up_last_kernel(plan, features, *refs):
    count = max(b[0] for b in plan) + 1
    pieces = refs[:count]
    up_ref, before_ref, before_squares_ref, back_ref, act_ref, pre_grad_ref, along_ref, total, squares, rows = refs[count:]
    step, steps = pl.program_id(0), pl.num_programs(0)
    assemble(plan, pieces, rows)
    part = dot(rows[...], up_ref[...])
    values = rows[...].astype(F32)
    square = jnp.broadcast_to(jnp.sum(values * values, axis=1, keepdims=True), squares.shape)

    @pl.when(step == 0)
    def _():
        total[...] = before_ref[...] + part
        squares[...] = before_squares_ref[...] + square

    @pl.when(step > 0)
    def _():
        total[...] += part
        squares[...] += square

    @pl.when(step == steps - 1)
    def _():
        scale = lax.rsqrt(squares[:, :1] / features + EPSILON)
        pre = total[...] * scale
        gate = jax.nn.sigmoid(pre)
        act_ref[...] = (pre * gate).astype(BF16)
        pre_grad = (back_ref[...] * gate * (1.0 + pre * (1.0 - gate))).astype(BF16)
        pre_grad_ref[...] = pre_grad
        along = jnp.sum(pre_grad.astype(F32) * pre, axis=1, keepdims=True)
        along_ref[...] = jnp.broadcast_to(scale * along / features, along_ref.shape)


def expert_grad_kernel(plan, pre_grad_ref, up_ref, along_ref, *refs):
    count = len(refs) // 2
    total = dot_nt(pre_grad_ref[...], up_ref[...])
    for piece, at, to, size in plan:
        rows = refs[piece][at : at + size, :].astype(F32)
        refs[count + piece][at : at + size, :] = (
            total[to : to + size, :] - rows * along_ref[to : to + size, :1]
        ).astype(BF16)


def expert_out_kernel(plan, act_ref, down_ref, *outs):
    total = dot(act_ref[...], down_ref[...])
    for piece, at, to, size in plan:
        outs[piece][at : at + size, :] = total[to : to + size, :].astype(BF16)


def on_device(inputs, b_proj, c_proj, log_decay, doc_lengths, expert_ids, gate_weights, w_up, w_down, cotangent):
    tokens, features = inputs.shape[1:]
    heads = log_decay.shape[1]
    state = b_proj.shape[2]
    experts, blocks = lax.axis_size("exp"), lax.axis_size("seq")
    hidden = w_up.shape[2]
    capacity = 3 * tokens // experts
    slots = experts * capacity
    width = features // CHUNKS
    hops = max(1, blocks // 2)
    relayed = experts == 8
    kinds = ((2, (0, 1, 4, 5)), (4, (0, 1, 2, 3)))

    x, b, c, log, cot = inputs[0], b_proj[0], c_proj[0], log_decay[0], cotangent[0]
    up, down = w_up[0], w_down[0]
    meta = jnp.concatenate([doc_lengths[0], (lax.axis_index("seq") * tokens)[None].astype(jnp.int32)])

    def log_spec(k):
        return pl.BlockSpec((heads // CHUNKS, tokens), lambda i: (k, 0))

    def chunk(k, rows=tokens):
        return pl.BlockSpec((rows, width), lambda i: (0, k))

    def shape(rows, columns, kind=BF16):
        return jax.ShapeDtypeStruct((rows, columns), kind)

    small, part = whole((tokens, state)), whole((tokens, width))
    unit = tokens * width
    head_flops = 2 * tokens * unit

    def offset(a, k):
        return lax.ppermute(a, "exp", [(i, i ^ k) for i in range(experts)])

    def passed(states, step, k):
        pairs = [(i, i + step) for i in range(blocks) if 0 <= i + step < blocks]
        arrived = [lax.ppermute(states, "seq", pairs)]
        for _ in range(hops - 1):
            kept = call(
                keep_kernel, (1,), [SMEM, log_spec(k), part], part, shape(tokens, width), unit, 4 * unit, "keep_states"
            )(meta, log, arrived[-1])
            arrived.append(lax.ppermute(kept, "seq", pairs))
        return arrived

    states_in, local = [], None
    for k in range(CHUNKS):
        local = call(
            local_kernel,
            (1,),
            [SMEM, log_spec(k), small, chunk(k)],
            part,
            shape(tokens, width),
            head_flops,
            4 * unit,
            "local_states",
        )(meta, log, b, x)
        states_in.append(passed(local, 1, k))

    table = jnp.concatenate([expert_ids[0].T.astype(F32), gate_weights[0].T], axis=0)
    table, cot, _ = lax.optimization_barrier((table, cot, local))
    if relayed:
        plans = [
            [
                block
                for i, o in enumerate(offsets)
                for block in ((i, 0, o * capacity, capacity), (i, capacity, (o ^ by) * capacity, capacity))
            ]
            for by, offsets in kinds
        ]
        pieces_of = [[2 * capacity] * 4] * 2
        pick_shape = (4, 2, capacity, tokens)
        weight_shape = (4, tokens, 2 * capacity)
        outs = [pick_shape, weight_shape, weight_shape] * 2
        me = lax.axis_index("exp").astype(jnp.int32)[None]
        found = call(
            functools.partial(relay_pick_kernel, experts, capacity, kinds),
            (1,),
            [SMEM] + [whole((4, tokens))] * 3,
            [whole(s) for s in outs],
            [jax.ShapeDtypeStruct(s, BF16) for s in outs],
            6 * experts * tokens * tokens,
            4 * slots * tokens,
            "pick_rows",
        )(me, table, *[offset(table, by) for by, _ in kinds])
        picks, own_weights, relay_weights = found[0::3], found[1::3], found[2::3]
    else:
        plans = [[(0, 0, 0, slots)]] * 2
        pieces_of = [[slots]] * 2
        pick, weights = call(
            functools.partial(direct_pick_kernel, experts, capacity),
            (1,),
            [whole((4, tokens))],
            [whole((slots, tokens)), whole((1, tokens, slots))],
            [shape(slots, tokens), jax.ShapeDtypeStruct((1, tokens, slots), BF16)],
            2 * experts * tokens * tokens,
            4 * slots * tokens,
            "pick_rows",
        )(table)
        picks, own_weights = [pick] * 2, [weights] * 2

    def piece_specs(kind):
        return [whole((rows, width)) for rows in pieces_of[kind]]

    def piece_shapes(kind):
        return [shape(rows, width) for rows in pieces_of[kind]]

    def switch(pieces):
        parts = pieces[0].reshape(experts, capacity, width)
        return [lax.all_to_all(parts, "exp", split_axis=0, concat_axis=0, tiled=True).reshape(slots, width)]

    def to_experts(rows, k, spec):
        kind = k % 2
        cost = (2 * slots * unit, 2 * (unit + slots * width))
        if not relayed:
            sent = call(
                direct_gather_kernel, (1,), [whole((slots, tokens)), spec], piece_specs(kind), piece_shapes(kind), *cost, "gather"
            )(picks[kind], rows)
            return switch(sent)
        by, offsets = kinds[kind]
        chunk_rows = rows if rows.shape[1] == width else rows[:, k * width : (k + 1) * width]
        other = offset(chunk_rows, by)
        sent = call(
            gather_kernel,
            (1,),
            [whole(picks[kind].shape), part, part],
            piece_specs(kind),
            piece_shapes(kind),
            *cost,
            "gather",
        )(picks[kind], chunk_rows, other)
        return [piece if o == 0 else offset(piece, o) for piece, o in zip(sent, offsets)]

    def to_positions(pieces, k):
        kind = k % 2
        if not relayed:
            return switch(pieces)
        by, offsets = kinds[kind]
        pieces = [piece if o == 0 else offset(piece, o) for piece, o in zip(pieces, offsets)]
        relay = call(
            relay_kernel,
            (1,),
            [whole(relay_weights[kind].shape)] + piece_specs(kind),
            part,
            shape(tokens, width),
            2 * slots * unit,
            2 * (unit + slots * width),
            "relay",
        )(relay_weights[kind], *pieces)
        return pieces + [offset(relay, by)]

    def moved_specs(kind):
        return piece_specs(kind) + ([part] if relayed else [])

    got_cot = [to_experts(cot, k, chunk(k)) for k in range(CHUNKS)]

    inner = call(
        inner_kernel,
        (CHUNKS,),
        [SMEM, pl.BlockSpec((heads // CHUNKS, tokens), lambda i: (i, 0)), small, small, columns(tokens, width)],
        columns(tokens, width),
        shape(tokens, features, F32),
        2 * CHUNKS * head_flops,
        6 * CHUNKS * unit,
        "inner",
    )(meta, log, b, c, x)

    resid, squares, got_in = [], [], []
    for k in range(CHUNKS):
        rows, square = call(
            functools.partial(resid_kernel, hops),
            (1,),
            [SMEM, log_spec(k), small, chunk(k)] + [part] * hops,
            [part, whole((tokens, 128))],
            [shape(tokens, width), shape(tokens, 128, F32)],
            hops * head_flops,
            (6 + 2 * hops) * unit,
            "resid",
        )(meta, log, c, inner, *states_in[k])
        resid.append(rows)
        squares.append(square)
        got_in.append(to_experts(rows, k, part))

    each = 2
    step = width // each
    chunk_flops = 2 * slots * width * hidden
    chunk_bytes = 2 * width * (hidden + slots)
    slots_hidden = whole((slots, hidden))

    def step_specs(kind, first=0):
        return [
            pl.BlockSpec((rows, step), lambda i: (0, jnp.clip(i - first, 0, each - 1))) for rows in pieces_of[kind]
        ]

    back = call(
        functools.partial(back_kernel, [plans[k % 2] for k in range(CHUNKS)]),
        (each * CHUNKS,),
        [spec for k in range(CHUNKS) for spec in step_specs(k % 2, each * k)] + [columns(hidden, step)],
        slots_hidden,
        shape(slots, hidden, F32),
        CHUNKS * chunk_flops,
        CHUNKS * chunk_bytes,
        "back",
        [pltpu.VMEM((slots, step), BF16)],
    )(*[piece for pieces in got_cot for piece in pieces], down)

    def up_spec(k):
        return pl.BlockSpec((step, hidden), lambda i: (each * k + i, 0))

    slots_small = whole((slots, 128))
    total, total_squares = call(
        functools.partial(up_first_kernel, plans[0]),
        (each,),
        step_specs(0) + [up_spec(0)],
        [slots_hidden, slots_small],
        [shape(slots, hidden, F32), shape(slots, 128, F32)],
        chunk_flops,
        chunk_bytes,
        "up_first",
        [pltpu.VMEM((slots, step), BF16)],
    )(*got_in[0], up)
    act, pre_grad, along = call(
        functools.partial(up_last_kernel, plans[1], features),
        (each,),
        step_specs(1) + [up_spec(1), slots_hidden, slots_small, slots_hidden],
        [slots_hidden, slots_hidden, slots_small],
        [shape(slots, hidden), shape(slots, hidden), shape(slots, 128, F32)],
        chunk_flops,
        chunk_bytes,
        "up_last",
        [pltpu.VMEM((slots, hidden), F32), pltpu.VMEM((slots, 128), F32), pltpu.VMEM((slots, step), BF16)],
    )(*got_in[1], up, total, total_squares, back)

    got_grad = []
    for k in range(CHUNKS):
        kind = k % 2
        expert_grad = call(
            functools.partial(expert_grad_kernel, plans[kind]),
            (each,),
            [slots_hidden, up_spec(k), slots_small] + step_specs(kind),
            step_specs(kind),
            piece_shapes(kind),
            chunk_flops,
            chunk_bytes,
            "expert_grad",
        )(pre_grad, up, along, *got_in[k])
        got_grad.append(to_positions(expert_grad, k))
    got_out = []
    for k in range(CHUNKS):
        kind = k % 2
        expert_out = call(
            functools.partial(expert_out_kernel, plans[kind]),
            (each,),
            [slots_hidden, pl.BlockSpec((hidden, step), lambda i, k=k: (0, each * k + i))],
            step_specs(kind),
            piece_shapes(kind),
            chunk_flops,
            chunk_bytes,
            "expert_out",
        )(act, down)
        got_out.append(to_positions(expert_out, k))

    def weights_spec(kind):
        return whole(own_weights[kind].shape)

    dresid, states_after = [], []
    for k in range(CHUNKS):
        kind = k % 2
        grad, source = call(
            functools.partial(dresid_kernel, CHUNKS, features),
            (1,),
            [SMEM, log_spec(k), small, weights_spec(kind), chunk(k)]
            + [whole((tokens, 128))] * CHUNKS
            + moved_specs(kind),
            [part, part],
            [shape(tokens, width)] * 2,
            head_flops + 2 * slots * unit,
            6 * unit + 2 * slots * width,
            "dresid",
        )(meta, log, c, own_weights[kind], cotangent[0], *squares, *got_grad[k])
        dresid.append(grad)
        states_after.append(passed(source, -1, k))

    into = chunk
    anywhere = pl.BlockSpec(memory_space=pl.ANY)

    def placed(kernel, k, in_specs, operands, earlier, flops, nbytes, name):
        more = [] if earlier is None else [earlier]
        return pl.pallas_call(
            kernel,
            grid=(1,),
            in_specs=in_specs + [anywhere] * len(more),
            out_specs=into(k),
            out_shape=shape(tokens, features),
            input_output_aliases={len(operands): 0} if more else {},
            name=name,
            cost_estimate=pl.CostEstimate(flops=flops, bytes_accessed=nbytes, transcendentals=0),
            compiler_params=pltpu.CompilerParams(vmem_limit_bytes=VMEM_BYTES),
        )(*operands, *more)

    input_grad = output = None
    for k in range(CHUNKS):
        inner_back = call(
            inner_back_kernel,
            (1,),
            [SMEM, log_spec(k), small, small, part],
            part,
            shape(tokens, width, F32),
            2 * head_flops,
            6 * unit,
            "inner_back",
        )(meta, log, b, c, dresid[k])
        input_grad = placed(
            functools.partial(grad_kernel, hops),
            k,
            [SMEM, log_spec(k), small, part] + [part] * hops,
            [meta, log, b, inner_back, *states_after[k]],
            input_grad,
            hops * head_flops,
            (6 + 2 * hops) * unit,
            "input_grad",
        )
    for k in range(CHUNKS):
        kind = k % 2
        output = placed(
            output_kernel,
            k,
            [weights_spec(kind), part] + moved_specs(kind),
            [own_weights[kind], resid[k], *got_out[k]],
            output,
            2 * slots * unit,
            4 * unit + 2 * slots * width,
            "output",
        )
    return (output[None], input_grad[None])


def solution(mesh):
    placed = (
        P("exp", "seq", None),
        P("exp", "seq", None),
        P("exp", "seq", None),
        P("exp", None, "seq"),
        P("exp", None),
        P("exp", "seq", None),
        P("exp", "seq", None),
        P("exp", None, None),
        P("exp", None, None),
        P("exp", "seq", None),
    )
    return jax.shard_map(
        on_device,
        mesh=mesh,
        in_specs=placed,
        out_specs=(P("exp", "seq", None), P("exp", "seq", None)),
        check_vma=False,
    )
```

```python
import functools

import jax
import jax.numpy as jnp
from jax import lax
from jax.experimental import pallas as pl
from jax.experimental.pallas import tpu as pltpu
from jax.sharding import PartitionSpec as P

EPSILON = 1e-06
F32 = jnp.float32
BF16 = jnp.bfloat16
CHUNKS = 2
VMEM_BYTES = 32 * 1024 * 1024
NT = (((1,), (1,)), ((), ()))


def dot(a, b):
    return jnp.dot(a, b, preferred_element_type=F32)


def dot_nt(a, b):
    return lax.dot_general(a, b, NT, preferred_element_type=F32)


def call(kernel, grid, in_specs, out_specs, out_shape, flops, nbytes, name, scratch=(), after=(), aliases=None):
    count, more = len(in_specs), len(after)

    def body(*refs):
        kernel(*refs[:count], *refs[count + more :])

    called = pl.pallas_call(
        body,
        grid=grid,
        in_specs=list(in_specs) + [pl.BlockSpec(memory_space=pl.ANY)] * more,
        out_specs=out_specs,
        out_shape=out_shape,
        scratch_shapes=scratch,
        input_output_aliases=aliases or {},
        name=name,
        cost_estimate=pl.CostEstimate(flops=flops, bytes_accessed=nbytes, transcendentals=0),
        compiler_params=pltpu.CompilerParams(vmem_limit_bytes=VMEM_BYTES),
    )
    return lambda *operands: called(*operands, *after)


def whole(shape):
    return pl.BlockSpec(shape, lambda i: (0,) * len(shape))


def columns(rows, width):
    return pl.BlockSpec((rows, width), lambda i: (0, i))


SMEM = pl.BlockSpec(memory_space=pltpu.SMEM)


def documents(meta, rows, size):
    count = meta.shape[0] - 1
    first = meta[count]
    along = first + lax.broadcasted_iota(jnp.int32, (1, size), 1)
    down = first + lax.broadcasted_iota(jnp.int32, (size, 1), 0)
    row = jnp.full((1, size), -1, jnp.int32)
    col = jnp.full((size, 1), -1, jnp.int32)
    before, last, start = jnp.int32(-1), jnp.int32(-1), jnp.int32(0)
    for i in range(count):
        row += (start <= along).astype(jnp.int32)
        col += (start <= down).astype(jnp.int32)
        before += (start <= first - 1).astype(jnp.int32)
        last += (start <= first + size - 1).astype(jnp.int32)
        start = start + meta[i]
    return row, col, before, last


def running(log_ref):
    size = log_ref.shape[1]
    upto = (
        lax.broadcasted_iota(jnp.int32, (size, size), 0)
        <= lax.broadcasted_iota(jnp.int32, (size, size), 1)
    ).astype(F32)
    return jnp.dot(
        log_ref[...], upto, precision=lax.Precision.HIGHEST, preferred_element_type=F32
    )


def head(h, size):
    return slice(h * size, (h + 1) * size)


def local_kernel(meta, log_ref, b_ref, x_ref, cot_ref, state_ref, chunk_ref):
    chunk_ref[...] = cot_ref[...]
    size = log_ref.shape[1]
    cum = running(log_ref)
    row, _, _, last = documents(meta, cum.shape[0], size)
    tail = (row == last).astype(F32)
    weight = tail * jnp.exp(cum[:, size - 1 :] - cum)
    b_t = b_ref[...].astype(F32).T
    p = x_ref.shape[1] // cum.shape[0]
    for h in range(cum.shape[0]):
        b_weighted = (b_t * weight[h : h + 1, :]).astype(BF16)
        state_ref[:, head(h, p)] = dot(b_weighted, x_ref[:, head(h, p)]).astype(BF16)


def pair_mask(meta, size):
    row, col, before, last = documents(meta, size, size)
    later = lax.broadcasted_iota(jnp.int32, (size, size), 0)
    earlier = lax.broadcasted_iota(jnp.int32, (size, size), 1)
    return row, col, before, last, later, earlier


def inner_kernel(meta, log_ref, b_ref, c_ref, x_ref, out_ref):
    size = log_ref.shape[1]
    cum = running(log_ref)
    cum_t = cum.T
    row, col, _, _, down, along = pair_mask(meta, size)
    scores = jnp.where((row == col) & (down >= along), dot_nt(c_ref[...], b_ref[...]), 0.0)
    p = x_ref.shape[1] // cum.shape[0]
    for h in range(cum.shape[0]):
        spread = cum_t[:, h : h + 1] - cum[h : h + 1, :]
        pair = (jnp.exp(jnp.minimum(spread, 0.0)) * scores).astype(BF16)
        out_ref[:, head(h, p)] = dot(pair, x_ref[:, head(h, p)])


def inner_back_kernel(meta, log_ref, b_ref, c_ref, grad_ref, out_ref):
    size = log_ref.shape[1]
    cum = running(log_ref)
    cum_t = cum.T
    row, col, _, _, down, along = pair_mask(meta, size)
    scores = jnp.where((row == col) & (down <= along), dot_nt(b_ref[...], c_ref[...]), 0.0)
    p = grad_ref.shape[1] // cum.shape[0]
    for h in range(cum.shape[0]):
        spread = cum[h : h + 1, :] - cum_t[:, h : h + 1]
        pair = (jnp.exp(jnp.minimum(spread, 0.0)) * scores).astype(BF16)
        out_ref[:, head(h, p)] = dot(pair, grad_ref[:, head(h, p)])


def keep_kernel(meta, log_ref, state_ref, out_ref):
    size = log_ref.shape[1]
    total = jnp.exp(running(log_ref)[:, size - 1 :])
    _, _, before, last = documents(meta, 1, size)
    total = jnp.where(before == last, total, 0.0)
    p = state_ref.shape[1] // total.shape[0]
    for h in range(total.shape[0]):
        out_ref[:, head(h, p)] = (
            state_ref[:, head(h, p)].astype(F32) * total[h : h + 1, :]
        ).astype(BF16)


def resid_kernel(hops, meta, log_ref, c_ref, inner_ref, *refs):
    states, (resid_ref, squares_ref) = refs[:hops], refs[hops:]
    size = log_ref.shape[1]
    _, col, before, _ = documents(meta, size, size)
    weight = jnp.where(col == before, jnp.exp(running(log_ref).T), 0.0)
    p = inner_ref.shape[1] // log_ref.shape[0]
    squares = jnp.zeros((size, p), F32)
    for h in range(log_ref.shape[0]):
        carried = dot(c_ref[...], states[0][:, head(h, p)])
        for state in states[1:]:
            carried += dot(c_ref[...], state[:, head(h, p)])
        rows = (inner_ref[:, head(h, p)] + weight[:, h : h + 1] * carried).astype(BF16)
        resid_ref[:, head(h, p)] = rows
        squares += rows.astype(F32) * rows.astype(F32)
    squares_ref[...] = jnp.broadcast_to(jnp.sum(squares, axis=1, keepdims=True), squares_ref.shape)


def combined(weights_ref, pieces):
    total = dot(weights_ref[0], pieces[0][...])
    for i, piece in enumerate(pieces[1:]):
        total += dot(weights_ref[i + 1], piece[...])
    return total


def relay_kernel(weights_ref, *refs):
    pieces, out_ref = refs[:-1], refs[-1]
    out_ref[...] = combined(weights_ref, pieces).astype(BF16)


def dresid_kernel(chunks, features, meta, log_ref, c_ref, weights_ref, cot_ref, *refs):
    squares, refs = refs[:chunks], refs[chunks:]
    moved_refs, (dresid_ref, source_ref) = refs[:-2], refs[-2:]
    size = log_ref.shape[1]
    row, _, before, _ = documents(meta, size, size)
    weight = jnp.where(row == before, jnp.exp(running(log_ref)), 0.0)
    c_t = c_ref[...].astype(F32).T
    total = squares[0][...]
    for part in squares[1:]:
        total = total + part[...]
    scale = lax.rsqrt(total[:, :1] / features + EPSILON)
    count = weights_ref.shape[0]
    moved = combined(weights_ref, moved_refs[:count])
    for arrived in moved_refs[count:]:
        moved += arrived[...].astype(F32)
    dresid_ref[...] = (cot_ref[...].astype(F32) + scale * moved).astype(BF16)
    p = cot_ref.shape[1] // log_ref.shape[0]
    for h in range(log_ref.shape[0]):
        c_weighted = (c_t * weight[h : h + 1, :]).astype(BF16)
        source_ref[:, head(h, p)] = dot(c_weighted, dresid_ref[:, head(h, p)]).astype(BF16)


def grad_kernel(hops, meta, log_ref, b_ref, inner_ref, *refs):
    states, out_ref = refs[:hops], refs[-1]
    size = log_ref.shape[1]
    _, col, _, last = documents(meta, size, size)
    cum = running(log_ref)
    weight = jnp.where(col == last, jnp.exp(cum[:, size - 1 :] - cum).T, 0.0)
    p = inner_ref.shape[1] // log_ref.shape[0]
    for h in range(log_ref.shape[0]):
        carried = dot(b_ref[...], states[0][:, head(h, p)])
        for state in states[1:]:
            carried += dot(b_ref[...], state[:, head(h, p)])
        out_ref[:, head(h, p)] = (inner_ref[:, head(h, p)] + weight[:, h : h + 1] * carried).astype(BF16)


def output_kernel(weights_ref, resid_ref, *refs):
    out_ref = refs[-1]
    count = weights_ref.shape[0]
    moved = combined(weights_ref, refs[:count])
    for arrived in refs[count : len(refs) - 1]:
        if arrived.shape == out_ref.shape:
            moved += arrived[...].astype(F32)
    out_ref[...] = (resid_ref[...].astype(F32) + moved).astype(BF16)


def picks_of(table, me, experts, capacity):
    tokens = table.shape[1]
    offset = lax.broadcasted_iota(jnp.int32, (experts, tokens), 0)
    first = (table[0:1, :].astype(jnp.int32) ^ me) == offset
    second = (table[1:2, :].astype(jnp.int32) ^ me) == offset
    named = (first | second).astype(F32)
    gate = jnp.where(first, table[2:3, :], 0.0) + jnp.where(second, table[3:4, :], 0.0)
    before = (
        lax.broadcasted_iota(jnp.int32, (tokens, tokens), 0)
        < lax.broadcasted_iota(jnp.int32, (tokens, tokens), 1)
    ).astype(BF16)
    rank = jnp.where(named > 0, dot(named.astype(BF16), before), -1.0)
    slot = lax.broadcasted_iota(jnp.int32, (capacity, tokens), 0).astype(F32)
    picks = [(rank[e : e + 1, :] == slot).astype(F32) for e in range(experts)]
    return picks, [pick * gate[e : e + 1, :] for e, pick in enumerate(picks)]


def direct_pick_kernel(experts, capacity, table_ref, pick_ref, weights_ref):
    picks, gated = picks_of(table_ref[...], 0, experts, capacity)
    pick_ref[...] = jnp.concatenate(picks, axis=0).astype(BF16)
    weights_ref[0] = jnp.concatenate(gated, axis=0).T.astype(BF16)


def relay_pick_kernel(experts, capacity, kinds, me_ref, own_ref, *refs):
    tables, outs = refs[: len(kinds)], refs[len(kinds) :]
    me = me_ref[0]
    picks, gated = picks_of(own_ref[...], me, experts, capacity)
    none = jnp.zeros_like(picks[0])
    for (_, offsets), table_ref, (pick_ref, own_weights_ref, relay_weights_ref) in zip(
        kinds, tables, (outs[:3], outs[3:])
    ):
        other_picks, other_gated = picks_of(table_ref[...], me, experts, capacity)
        for i, o in enumerate(offsets):
            pick_ref[i, 0] = picks[o].astype(BF16)
            pick_ref[i, 1] = other_picks[o].astype(BF16)
            own_weights_ref[i] = jnp.concatenate([gated[o], none], axis=0).T.astype(BF16)
            relay_weights_ref[i] = jnp.concatenate([none, other_gated[o]], axis=0).T.astype(BF16)


def gather_kernel(pick_ref, own_ref, other_ref, *outs):
    capacity = pick_ref.shape[2]
    for i, out in enumerate(outs):
        out[:capacity, :] = dot(pick_ref[i, 0], own_ref[...]).astype(BF16)
        out[capacity:, :] = dot(pick_ref[i, 1], other_ref[...]).astype(BF16)


def direct_gather_kernel(pick_ref, own_ref, out_ref):
    out_ref[...] = dot(pick_ref[...], own_ref[...]).astype(BF16)


def assemble(plan, pieces, rows):
    for piece, at, to, count in plan:
        rows[to : to + count, :] = pieces[piece][at : at + count, :]


def back_kernel(plans, *refs):
    counts = [max(b[0] for b in plan) + 1 for plan in plans]
    pieces, (down_ref, back_ref, rows) = refs[: sum(counts)], refs[sum(counts) :]
    step, each = pl.program_id(0), pl.num_programs(0) // len(plans)
    for k, plan in enumerate(plans):
        mine = pieces[sum(counts[:k]) : sum(counts[: k + 1])]

        @pl.when(step // each == k)
        def _(plan=plan, mine=mine):
            assemble(plan, mine, rows)

    part = dot_nt(rows[...], down_ref[...])

    @pl.when(step == 0)
    def _():
        back_ref[...] = part

    @pl.when(step > 0)
    def _():
        back_ref[...] += part


def up_first_kernel(plan, *refs):
    pieces, (up_ref, total_ref, squares_ref, rows) = refs[:-4], refs[-4:]
    assemble(plan, pieces, rows)
    part = dot(rows[...], up_ref[...])
    values = rows[...].astype(F32)
    square = jnp.broadcast_to(jnp.sum(values * values, axis=1, keepdims=True), squares_ref.shape)

    @pl.when(pl.program_id(0) == 0)
    def _():
        total_ref[...] = part
        squares_ref[...] = square

    @pl.when(pl.program_id(0) > 0)
    def _():
        total_ref[...] += part
        squares_ref[...] += square


def up_last_kernel(plan, features, *refs):
    count = max(b[0] for b in plan) + 1
    pieces = refs[:count]
    up_ref, before_ref, before_squares_ref, back_ref, act_ref, pre_grad_ref, along_ref, total, squares, rows = refs[count:]
    step, steps = pl.program_id(0), pl.num_programs(0)
    assemble(plan, pieces, rows)
    part = dot(rows[...], up_ref[...])
    values = rows[...].astype(F32)
    square = jnp.broadcast_to(jnp.sum(values * values, axis=1, keepdims=True), squares.shape)

    @pl.when(step == 0)
    def _():
        total[...] = before_ref[...] + part
        squares[...] = before_squares_ref[...] + square

    @pl.when(step > 0)
    def _():
        total[...] += part
        squares[...] += square

    @pl.when(step == steps - 1)
    def _():
        scale = lax.rsqrt(squares[:, :1] / features + EPSILON)
        pre = total[...] * scale
        gate = jax.nn.sigmoid(pre)
        act_ref[...] = (pre * gate).astype(BF16)
        pre_grad = (back_ref[...] * gate * (1.0 + pre * (1.0 - gate))).astype(BF16)
        pre_grad_ref[...] = pre_grad
        along = jnp.sum(pre_grad.astype(F32) * pre, axis=1, keepdims=True)
        along_ref[...] = jnp.broadcast_to(scale * along / features, along_ref.shape)


def expert_grad_kernel(plan, pre_grad_ref, up_ref, along_ref, *refs):
    count = len(refs) // 2
    total = dot_nt(pre_grad_ref[...], up_ref[...])
    for piece, at, to, size in plan:
        rows = refs[piece][at : at + size, :].astype(F32)
        refs[count + piece][at : at + size, :] = (
            total[to : to + size, :] - rows * along_ref[to : to + size, :1]
        ).astype(BF16)


def expert_out_kernel(plan, act_ref, down_ref, *outs):
    total = dot(act_ref[...], down_ref[...])
    for piece, at, to, size in plan:
        outs[piece][at : at + size, :] = total[to : to + size, :].astype(BF16)


def on_device(inputs, b_proj, c_proj, log_decay, doc_lengths, expert_ids, gate_weights, w_up, w_down, cotangent):
    tokens, features = inputs.shape[1:]
    heads = log_decay.shape[1]
    state = b_proj.shape[2]
    experts, blocks = lax.axis_size("exp"), lax.axis_size("seq")
    hidden = w_up.shape[2]
    capacity = 3 * tokens // experts
    slots = experts * capacity
    width = features // CHUNKS
    hops = max(1, blocks // 2)
    relayed = experts == 8
    kinds = ((2, (0, 1, 4, 5)), (4, (0, 1, 2, 3)))

    x, b, c, log, cot = inputs[0], b_proj[0], c_proj[0], log_decay[0], cotangent[0]
    up, down = w_up[0], w_down[0]
    meta = jnp.concatenate([doc_lengths[0], (lax.axis_index("seq") * tokens)[None].astype(jnp.int32)])

    def log_spec(k):
        return pl.BlockSpec((heads // CHUNKS, tokens), lambda i: (k, 0))

    def chunk(k, rows=tokens):
        return pl.BlockSpec((rows, width), lambda i: (0, k))

    def shape(rows, columns, kind=BF16):
        return jax.ShapeDtypeStruct((rows, columns), kind)

    small, part = whole((tokens, state)), whole((tokens, width))
    unit = tokens * width
    head_flops = 2 * tokens * unit

    def offset(a, k):
        return lax.ppermute(a, "exp", [(i, i ^ k) for i in range(experts)])

    def hop(states, step):
        return lax.ppermute(states, "seq", [(i, i + step) for i in range(blocks) if 0 <= i + step < blocks])

    def hop_on(arrived, step, k, after):
        for _ in range(hops - 1):
            kept = call(
                keep_kernel,
                (1,),
                [SMEM, log_spec(k), part],
                part,
                shape(tokens, width),
                unit,
                4 * unit,
                "keep_states",
                after=after,
            )(meta, log, arrived[-1])
            arrived = arrived + [hop(kept, step)]
        return arrived, kept

    states_in, cots = [], []
    for k in range(CHUNKS):
        local, cot_chunk = call(
            local_kernel,
            (1,),
            [SMEM, log_spec(k), small, chunk(k), chunk(k)],
            [part, part],
            [shape(tokens, width)] * 2,
            head_flops,
            8 * unit,
            "local_states",
        )(meta, log, b, x, cot)
        states_in.append([hop(local, 1)])
        cots.append(cot_chunk)

    table = jnp.concatenate([expert_ids[0].T.astype(F32), gate_weights[0].T], axis=0)
    if relayed:
        plans = [
            [
                block
                for i, o in enumerate(offsets)
                for block in ((i, 0, o * capacity, capacity), (i, capacity, (o ^ by) * capacity, capacity))
            ]
            for by, offsets in kinds
        ]
        pieces_of = [[2 * capacity] * 4] * 2
        pick_shape = (4, 2, capacity, tokens)
        weight_shape = (4, tokens, 2 * capacity)
        outs = [pick_shape, weight_shape, weight_shape] * 2
        me = lax.axis_index("exp").astype(jnp.int32)[None]
        found = call(
            functools.partial(relay_pick_kernel, experts, capacity, kinds),
            (1,),
            [SMEM] + [whole((4, tokens))] * 3,
            [whole(s) for s in outs],
            [jax.ShapeDtypeStruct(s, BF16) for s in outs],
            6 * experts * tokens * tokens,
            4 * slots * tokens,
            "pick_rows",
        )(me, table, *[offset(table, by) for by, _ in kinds])
        picks, own_weights, relay_weights = found[0::3], found[1::3], found[2::3]
    else:
        plans = [[(0, 0, 0, slots)]] * 2
        pieces_of = [[slots]] * 2
        pick, weights = call(
            functools.partial(direct_pick_kernel, experts, capacity),
            (1,),
            [whole((4, tokens))],
            [whole((slots, tokens)), whole((1, tokens, slots))],
            [shape(slots, tokens), jax.ShapeDtypeStruct((1, tokens, slots), BF16)],
            2 * experts * tokens * tokens,
            4 * slots * tokens,
            "pick_rows",
        )(table)
        picks, own_weights = [pick] * 2, [weights] * 2

    def piece_specs(kind):
        return [whole((rows, width)) for rows in pieces_of[kind]]

    def piece_shapes(kind):
        return [shape(rows, width) for rows in pieces_of[kind]]

    def switch(pieces):
        parts = pieces[0].reshape(experts, capacity, width)
        return [lax.all_to_all(parts, "exp", split_axis=0, concat_axis=0, tiled=True).reshape(slots, width)]

    def to_experts(rows, k, other, after=()):
        kind = k % 2
        cost = (2 * slots * unit, 2 * (unit + slots * width))
        if not relayed:
            sent = call(
                direct_gather_kernel,
                (1,),
                [whole((slots, tokens)), part],
                piece_specs(kind),
                piece_shapes(kind),
                *cost,
                "gather",
                after=after,
            )(picks[kind], rows)
            return sent, switch(sent)
        _, offsets = kinds[kind]
        sent = call(
            gather_kernel,
            (1,),
            [whole(picks[kind].shape), part, part],
            piece_specs(kind),
            piece_shapes(kind),
            *cost,
            "gather",
            after=after,
        )(picks[kind], rows, other)
        return sent, [piece if o == 0 else offset(piece, o) for piece, o in zip(sent, offsets)]

    def other_of(rows, k):
        return offset(rows, kinds[k % 2][0]) if relayed else None

    def to_positions(pieces, k, after=()):
        kind = k % 2
        if not relayed:
            arrived = switch(pieces)
            return arrived[0], arrived
        by, offsets = kinds[kind]
        pieces = [piece if o == 0 else offset(piece, o) for piece, o in zip(pieces, offsets)]
        relay = call(
            relay_kernel,
            (1,),
            [whole(relay_weights[kind].shape)] + piece_specs(kind),
            part,
            shape(tokens, width),
            2 * slots * unit,
            2 * (unit + slots * width),
            "relay",
            after=after,
        )(relay_weights[kind], *pieces)
        return relay, pieces + [offset(relay, by)]

    def moved_specs(kind):
        return piece_specs(kind) + ([part] if relayed else [])

    other_cots = [other_of(cots[k], k) for k in range(CHUNKS)]
    inner = call(
        inner_kernel,
        (CHUNKS,),
        [SMEM, pl.BlockSpec((heads // CHUNKS, tokens), lambda i: (i, 0)), small, small, columns(tokens, width)],
        columns(tokens, width),
        shape(tokens, features, F32),
        2 * CHUNKS * head_flops,
        6 * CHUNKS * unit,
        "inner",
    )(meta, log, b, c, x)
    states_in[0], kept = hop_on(states_in[0], 1, 0, [inner, picks[0]])
    got_cot, sent = [], kept
    for k in range(CHUNKS):
        (sent, *_), pieces = to_experts(cots[k], k, other_cots[k], [sent])
        got_cot.append(pieces)
    states_in[1], kept = hop_on(states_in[1], 1, 1, [sent])

    resid, squares, others = [], [], []
    for k in range(CHUNKS):
        rows, square = call(
            functools.partial(resid_kernel, hops),
            (1,),
            [SMEM, log_spec(k), small, chunk(k)] + [part] * hops,
            [part, whole((tokens, 128))],
            [shape(tokens, width), shape(tokens, 128, F32)],
            hops * head_flops,
            (6 + 2 * hops) * unit,
            "resid",
        )(meta, log, c, inner, *states_in[k])
        resid.append(rows)
        squares.append(square)
        others.append(other_of(rows, k))
    (sent, *_), pieces = to_experts(resid[0], 0, others[0], [resid[1]])
    got_in = [pieces]

    each = 2
    step = width // each
    chunk_flops = 2 * slots * width * hidden
    chunk_bytes = 2 * width * (hidden + slots)
    slots_hidden = whole((slots, hidden))

    def step_specs(kind, first=0):
        return [
            pl.BlockSpec((rows, step), lambda i: (0, jnp.clip(i - first, 0, each - 1))) for rows in pieces_of[kind]
        ]

    back = call(
        functools.partial(back_kernel, [plans[k % 2] for k in range(CHUNKS)]),
        (each * CHUNKS,),
        [spec for k in range(CHUNKS) for spec in step_specs(k % 2, each * k)] + [columns(hidden, step)],
        slots_hidden,
        shape(slots, hidden, F32),
        CHUNKS * chunk_flops,
        CHUNKS * chunk_bytes,
        "back",
        [pltpu.VMEM((slots, step), BF16)],
        after=[sent],
    )(*[piece for pieces in got_cot for piece in pieces], down)
    _, pieces = to_experts(resid[1], 1, others[1], [back])
    got_in.append(pieces)

    def up_spec(k):
        return pl.BlockSpec((step, hidden), lambda i: (each * k + i, 0))

    slots_small = whole((slots, 128))
    total, total_squares = call(
        functools.partial(up_first_kernel, plans[0]),
        (each,),
        step_specs(0) + [up_spec(0)],
        [slots_hidden, slots_small],
        [shape(slots, hidden, F32), shape(slots, 128, F32)],
        chunk_flops,
        chunk_bytes,
        "up_first",
        [pltpu.VMEM((slots, step), BF16)],
    )(*got_in[0], up)
    act, pre_grad, along = call(
        functools.partial(up_last_kernel, plans[1], features),
        (each,),
        step_specs(1) + [up_spec(1), slots_hidden, slots_small, slots_hidden],
        [slots_hidden, slots_hidden, slots_small],
        [shape(slots, hidden), shape(slots, hidden), shape(slots, 128, F32)],
        chunk_flops,
        chunk_bytes,
        "up_last",
        [pltpu.VMEM((slots, hidden), F32), pltpu.VMEM((slots, 128), F32), pltpu.VMEM((slots, step), BF16)],
    )(*got_in[1], up, total, total_squares, back)

    got_grad = []
    for k in range(CHUNKS):
        kind = k % 2
        expert_grad = call(
            functools.partial(expert_grad_kernel, plans[kind]),
            (each,),
            [slots_hidden, up_spec(k), slots_small] + step_specs(kind),
            step_specs(kind),
            piece_shapes(kind),
            chunk_flops,
            chunk_bytes,
            "expert_grad",
        )(pre_grad, up, along, *got_in[k])
        relay, pieces = to_positions(expert_grad, k)
        got_grad.append(pieces)
    outs, last = [], relay
    for k in range(CHUNKS):
        kind = k % 2
        expert_out = call(
            functools.partial(expert_out_kernel, plans[kind]),
            (each,),
            [slots_hidden, pl.BlockSpec((hidden, step), lambda i, k=k: (0, each * k + i))],
            step_specs(kind),
            piece_shapes(kind),
            chunk_flops,
            chunk_bytes,
            "expert_out",
            after=[last],
        )(act, down)
        outs.append(expert_out)
        last = expert_out[0]

    def weights_spec(kind):
        return whole(own_weights[kind].shape)

    dresid, states_after = [], []
    for k in range(CHUNKS):
        kind = k % 2
        grad, source = call(
            functools.partial(dresid_kernel, CHUNKS, features),
            (1,),
            [SMEM, log_spec(k), small, weights_spec(kind), chunk(k)]
            + [whole((tokens, 128))] * CHUNKS
            + moved_specs(kind),
            [part, part],
            [shape(tokens, width)] * 2,
            head_flops + 2 * slots * unit,
            6 * unit + 2 * slots * width,
            "dresid",
            after=[last],
        )(meta, log, c, own_weights[kind], cot, *squares, *got_grad[k])
        dresid.append(grad)
        states_after.append([hop(source, -1)])
        last = grad

    inner_back = [
        call(
            inner_back_kernel,
            (1,),
            [SMEM, log_spec(k), small, small, part],
            part,
            shape(tokens, width, F32),
            2 * head_flops,
            6 * unit,
            "inner_back",
            after=[last],
        )(meta, log, b, c, dresid[k])
        for k in range(CHUNKS)
    ]
    states_after[0], last = hop_on(states_after[0], -1, 0, inner_back)
    got_out = []
    for k in range(CHUNKS):
        last, pieces = to_positions(outs[k], k, [last])
        got_out.append(pieces)
    states_after[1], last = hop_on(states_after[1], -1, 1, [last])

    def placed(kernel, k, in_specs, operands, earlier, after, flops, nbytes, name):
        more = [] if earlier is None else [earlier]
        return call(
            kernel,
            (1,),
            in_specs + [pl.BlockSpec(memory_space=pl.ANY)] * len(more),
            chunk(k),
            shape(tokens, features),
            flops,
            nbytes,
            name,
            after=after,
            aliases={len(operands): 0} if more else {},
        )(*operands, *more)

    def input_grads(k, earlier, after):
        return placed(
            functools.partial(grad_kernel, hops),
            k,
            [SMEM, log_spec(k), small, part] + [part] * hops,
            [meta, log, b, inner_back[k], *states_after[k]],
            earlier,
            after,
            hops * head_flops,
            (6 + 2 * hops) * unit,
            "input_grad",
        )

    input_grad, output = input_grads(0, None, [last]), None
    for k in range(CHUNKS):
        kind = k % 2
        output = placed(
            output_kernel,
            k,
            [weights_spec(kind), part] + moved_specs(kind),
            [own_weights[kind], resid[k], *got_out[k]],
            output,
            [input_grad] if output is None else [],
            2 * slots * unit,
            4 * unit + 2 * slots * width,
            "output",
        )
    input_grad = input_grads(1, input_grad, [output])
    return (output[None], input_grad[None])


def solution(mesh):
    placed = (
        P("exp", "seq", None),
        P("exp", "seq", None),
        P("exp", "seq", None),
        P("exp", None, "seq"),
        P("exp", None),
        P("exp", "seq", None),
        P("exp", "seq", None),
        P("exp", None, None),
        P("exp", None, None),
        P("exp", "seq", None),
    )
    return jax.shard_map(
        on_device,
        mesh=mesh,
        in_specs=placed,
        out_specs=(P("exp", "seq", None), P("exp", "seq", None)),
        check_vma=False,
    )
```

```python
import functools

import jax
import jax.numpy as jnp
from jax import lax
from jax.experimental import pallas as pl
from jax.experimental.pallas import tpu as pltpu
from jax.sharding import PartitionSpec as P

EPSILON = 1e-06
F32 = jnp.float32
BF16 = jnp.bfloat16
CHUNKS = 2
VMEM_BYTES = 32 * 1024 * 1024
NT = (((1,), (1,)), ((), ()))


def dot(a, b):
    return jnp.dot(a, b, preferred_element_type=F32)


def dot_nt(a, b):
    return lax.dot_general(a, b, NT, preferred_element_type=F32)


def call(kernel, grid, in_specs, out_specs, out_shape, flops, nbytes, name, scratch=(), after=(), aliases=None):
    count, more = len(in_specs), len(after)

    def body(*refs):
        kernel(*refs[:count], *refs[count + more :])

    called = pl.pallas_call(
        body,
        grid=grid,
        in_specs=list(in_specs) + [pl.BlockSpec(memory_space=pl.ANY)] * more,
        out_specs=out_specs,
        out_shape=out_shape,
        scratch_shapes=scratch,
        input_output_aliases=aliases or {},
        name=name,
        cost_estimate=pl.CostEstimate(flops=flops, bytes_accessed=nbytes, transcendentals=0),
        compiler_params=pltpu.CompilerParams(vmem_limit_bytes=VMEM_BYTES),
    )
    return lambda *operands: called(*operands, *after)


def whole(shape):
    return pl.BlockSpec(shape, lambda i: (0,) * len(shape))


def columns(rows, width):
    return pl.BlockSpec((rows, width), lambda i: (0, i))


SMEM = pl.BlockSpec(memory_space=pltpu.SMEM)


def documents(meta, rows, size):
    count = meta.shape[0] - 1
    first = meta[count]
    along = first + lax.broadcasted_iota(jnp.int32, (1, size), 1)
    down = first + lax.broadcasted_iota(jnp.int32, (size, 1), 0)
    row = jnp.full((1, size), -1, jnp.int32)
    col = jnp.full((size, 1), -1, jnp.int32)
    before, last, start = jnp.int32(-1), jnp.int32(-1), jnp.int32(0)
    for i in range(count):
        row += (start <= along).astype(jnp.int32)
        col += (start <= down).astype(jnp.int32)
        before += (start <= first - 1).astype(jnp.int32)
        last += (start <= first + size - 1).astype(jnp.int32)
        start = start + meta[i]
    return row, col, before, last


def running(log_ref):
    size = log_ref.shape[1]
    upto = (
        lax.broadcasted_iota(jnp.int32, (size, size), 0)
        <= lax.broadcasted_iota(jnp.int32, (size, size), 1)
    ).astype(F32)
    return jnp.dot(
        log_ref[...], upto, precision=lax.Precision.HIGHEST, preferred_element_type=F32
    )


def head(h, size):
    return slice(h * size, (h + 1) * size)


def local_kernel(meta, log_ref, b_ref, x_ref, state_ref):
    size = log_ref.shape[1]
    cum = running(log_ref)
    row, _, _, last = documents(meta, cum.shape[0], size)
    tail = (row == last).astype(F32)
    weight = tail * jnp.exp(cum[:, size - 1 :] - cum)
    b_t = b_ref[...].astype(F32).T
    p = x_ref.shape[1] // cum.shape[0]
    for h in range(cum.shape[0]):
        b_weighted = (b_t * weight[h : h + 1, :]).astype(BF16)
        state_ref[:, head(h, p)] = dot(b_weighted, x_ref[:, head(h, p)]).astype(BF16)


def pair_mask(meta, size):
    row, col, before, last = documents(meta, size, size)
    later = lax.broadcasted_iota(jnp.int32, (size, size), 0)
    earlier = lax.broadcasted_iota(jnp.int32, (size, size), 1)
    return row, col, before, last, later, earlier


def inner_kernel(meta, log_ref, b_ref, c_ref, x_ref, out_ref):
    size = log_ref.shape[1]
    cum = running(log_ref)
    cum_t = cum.T
    row, col, _, _, down, along = pair_mask(meta, size)
    scores = jnp.where((row == col) & (down >= along), dot_nt(c_ref[...], b_ref[...]), 0.0)
    p = x_ref.shape[1] // cum.shape[0]
    for h in range(cum.shape[0]):
        spread = cum_t[:, h : h + 1] - cum[h : h + 1, :]
        pair = (jnp.exp(jnp.minimum(spread, 0.0)) * scores).astype(BF16)
        out_ref[:, head(h, p)] = dot(pair, x_ref[:, head(h, p)])


def inner_back_kernel(meta, log_ref, b_ref, c_ref, grad_ref, out_ref):
    size = log_ref.shape[1]
    cum = running(log_ref)
    cum_t = cum.T
    row, col, _, _, down, along = pair_mask(meta, size)
    scores = jnp.where((row == col) & (down <= along), dot_nt(b_ref[...], c_ref[...]), 0.0)
    p = grad_ref.shape[1] // cum.shape[0]
    for h in range(cum.shape[0]):
        spread = cum[h : h + 1, :] - cum_t[:, h : h + 1]
        pair = (jnp.exp(jnp.minimum(spread, 0.0)) * scores).astype(BF16)
        out_ref[:, head(h, p)] = dot(pair, grad_ref[:, head(h, p)])


def keep_kernel(meta, log_ref, state_ref, out_ref):
    size = log_ref.shape[1]
    total = jnp.exp(running(log_ref)[:, size - 1 :])
    _, _, before, last = documents(meta, 1, size)
    total = jnp.where(before == last, total, 0.0)
    p = state_ref.shape[1] // total.shape[0]
    for h in range(total.shape[0]):
        out_ref[:, head(h, p)] = (
            state_ref[:, head(h, p)].astype(F32) * total[h : h + 1, :]
        ).astype(BF16)


def resid_kernel(hops, meta, log_ref, c_ref, inner_ref, *refs):
    states, (resid_ref, squares_ref) = refs[:hops], refs[hops:]
    size = log_ref.shape[1]
    _, col, before, _ = documents(meta, size, size)
    weight = jnp.where(col == before, jnp.exp(running(log_ref).T), 0.0)
    p = inner_ref.shape[1] // log_ref.shape[0]
    squares = jnp.zeros((size, p), F32)
    for h in range(log_ref.shape[0]):
        carried = dot(c_ref[...], states[0][:, head(h, p)])
        for state in states[1:]:
            carried += dot(c_ref[...], state[:, head(h, p)])
        rows = (inner_ref[:, head(h, p)] + weight[:, h : h + 1] * carried).astype(BF16)
        resid_ref[:, head(h, p)] = rows
        squares += rows.astype(F32) * rows.astype(F32)
    squares_ref[...] = jnp.broadcast_to(jnp.sum(squares, axis=1, keepdims=True), squares_ref.shape)


def combined(weights_ref, pieces):
    total = dot(weights_ref[0], pieces[0][...])
    for i, piece in enumerate(pieces[1:]):
        total += dot(weights_ref[i + 1], piece[...])
    return total


def relay_kernel(weights_ref, *refs):
    pieces, out_ref = refs[:-1], refs[-1]
    out_ref[...] = combined(weights_ref, pieces).astype(BF16)


def dresid_kernel(chunks, features, meta, log_ref, c_ref, weights_ref, cot_ref, *refs):
    squares, refs = refs[:chunks], refs[chunks:]
    moved_refs, (dresid_ref, source_ref) = refs[:-2], refs[-2:]
    size = log_ref.shape[1]
    row, _, before, _ = documents(meta, size, size)
    weight = jnp.where(row == before, jnp.exp(running(log_ref)), 0.0)
    c_t = c_ref[...].astype(F32).T
    total = squares[0][...]
    for part in squares[1:]:
        total = total + part[...]
    scale = lax.rsqrt(total[:, :1] / features + EPSILON)
    count = weights_ref.shape[0]
    moved = combined(weights_ref, moved_refs[:count])
    for arrived in moved_refs[count:]:
        moved += arrived[...].astype(F32)
    dresid_ref[...] = (cot_ref[...].astype(F32) + scale * moved).astype(BF16)
    p = cot_ref.shape[1] // log_ref.shape[0]
    for h in range(log_ref.shape[0]):
        c_weighted = (c_t * weight[h : h + 1, :]).astype(BF16)
        source_ref[:, head(h, p)] = dot(c_weighted, dresid_ref[:, head(h, p)]).astype(BF16)


def grad_kernel(hops, meta, log_ref, b_ref, inner_ref, *refs):
    states, out_ref = refs[:hops], refs[-1]
    size = log_ref.shape[1]
    _, col, _, last = documents(meta, size, size)
    cum = running(log_ref)
    weight = jnp.where(col == last, jnp.exp(cum[:, size - 1 :] - cum).T, 0.0)
    p = inner_ref.shape[1] // log_ref.shape[0]
    for h in range(log_ref.shape[0]):
        carried = dot(b_ref[...], states[0][:, head(h, p)])
        for state in states[1:]:
            carried += dot(b_ref[...], state[:, head(h, p)])
        out_ref[:, head(h, p)] = (inner_ref[:, head(h, p)] + weight[:, h : h + 1] * carried).astype(BF16)


def output_kernel(weights_ref, got_ref, *refs):
    resid, out_ref = refs[:-1], refs[-1]
    width = resid[0].shape[1]
    for k, rows in enumerate(resid):
        at = slice(k * width, (k + 1) * width)
        out_ref[:, at] = (rows[...].astype(F32) + dot(weights_ref[...], got_ref[:, at])).astype(BF16)


def picks_of(table, me, experts, capacity):
    tokens = table.shape[1]
    offset = lax.broadcasted_iota(jnp.int32, (experts, tokens), 0)
    first = (table[0:1, :].astype(jnp.int32) ^ me) == offset
    second = (table[1:2, :].astype(jnp.int32) ^ me) == offset
    named = (first | second).astype(F32)
    gate = jnp.where(first, table[2:3, :], 0.0) + jnp.where(second, table[3:4, :], 0.0)
    before = (
        lax.broadcasted_iota(jnp.int32, (tokens, tokens), 0)
        < lax.broadcasted_iota(jnp.int32, (tokens, tokens), 1)
    ).astype(BF16)
    rank = jnp.where(named > 0, dot(named.astype(BF16), before), -1.0)
    slot = lax.broadcasted_iota(jnp.int32, (capacity, tokens), 0).astype(F32)
    picks = [(rank[e : e + 1, :] == slot).astype(F32) for e in range(experts)]
    return picks, [pick * gate[e : e + 1, :] for e, pick in enumerate(picks)]


def direct_pick_kernel(experts, capacity, table_ref, cot_ref, pick_ref, weights_ref, sent_ref):
    picks, gated = picks_of(table_ref[...], 0, experts, capacity)
    pick = jnp.concatenate(picks, axis=0).astype(BF16)
    pick_ref[...] = pick
    weights_ref[...] = jnp.concatenate(gated, axis=0).T.astype(BF16)
    sent_ref[...] = dot(pick, cot_ref[...]).astype(BF16)


def relay_pick_kernel(experts, capacity, kinds, me_ref, own_ref, *refs):
    tables, outs = refs[: len(kinds)], refs[len(kinds) :]
    me = me_ref[0]
    picks, gated = picks_of(own_ref[...], me, experts, capacity)
    none = jnp.zeros_like(picks[0])
    for (_, offsets), table_ref, (pick_ref, own_weights_ref, relay_weights_ref) in zip(
        kinds, tables, (outs[:3], outs[3:])
    ):
        other_picks, other_gated = picks_of(table_ref[...], me, experts, capacity)
        for i, o in enumerate(offsets):
            pick_ref[i, 0] = picks[o].astype(BF16)
            pick_ref[i, 1] = other_picks[o].astype(BF16)
            own_weights_ref[i] = jnp.concatenate([gated[o], none], axis=0).T.astype(BF16)
            relay_weights_ref[i] = jnp.concatenate([none, other_gated[o]], axis=0).T.astype(BF16)


def gather_kernel(pick_ref, own_ref, other_ref, *outs):
    capacity = pick_ref.shape[2]
    for i, out in enumerate(outs):
        out[:capacity, :] = dot(pick_ref[i, 0], own_ref[...]).astype(BF16)
        out[capacity:, :] = dot(pick_ref[i, 1], other_ref[...]).astype(BF16)


def direct_gather_kernel(pick_ref, own_ref, out_ref):
    out_ref[...] = dot(pick_ref[...], own_ref[...]).astype(BF16)


def assemble(plan, pieces, rows):
    for piece, at, to, count in plan:
        rows[to : to + count, :] = pieces[piece][at : at + count, :]


def back_kernel(capacity, me_ref, rows_ref, down_ref, back_ref, total):
    step = pl.program_id(0)
    part = dot_nt(rows_ref[...], down_ref[...])

    @pl.when(step == 0)
    def _():
        total[...] = part

    @pl.when(step > 0)
    def _():
        total[...] += part

    @pl.when(step == pl.num_programs(0) - 1)
    def _():
        for i in range(total.shape[0] // capacity):
            to = pl.multiple_of((i ^ me_ref[0]) * capacity, 8)
            back_ref[pl.ds(to, capacity), :] = total[i * capacity : (i + 1) * capacity, :]


def up_first_kernel(plan, *refs):
    pieces, (up_ref, total_ref, squares_ref, rows) = refs[:-4], refs[-4:]
    assemble(plan, pieces, rows)
    part = dot(rows[...], up_ref[...])
    values = rows[...].astype(F32)
    square = jnp.broadcast_to(jnp.sum(values * values, axis=1, keepdims=True), squares_ref.shape)

    @pl.when(pl.program_id(0) == 0)
    def _():
        total_ref[...] = part
        squares_ref[...] = square

    @pl.when(pl.program_id(0) > 0)
    def _():
        total_ref[...] += part
        squares_ref[...] += square


def up_last_kernel(plan, features, *refs):
    count = max(b[0] for b in plan) + 1
    pieces = refs[:count]
    up_ref, before_ref, before_squares_ref, back_ref, act_ref, pre_grad_ref, along_ref, total, squares, rows = refs[count:]
    step, steps = pl.program_id(0), pl.num_programs(0)
    assemble(plan, pieces, rows)
    part = dot(rows[...], up_ref[...])
    values = rows[...].astype(F32)
    square = jnp.broadcast_to(jnp.sum(values * values, axis=1, keepdims=True), squares.shape)

    @pl.when(step == 0)
    def _():
        total[...] = before_ref[...] + part
        squares[...] = before_squares_ref[...] + square

    @pl.when(step > 0)
    def _():
        total[...] += part
        squares[...] += square

    @pl.when(step == steps - 1)
    def _():
        scale = lax.rsqrt(squares[:, :1] / features + EPSILON)
        pre = total[...] * scale
        gate = jax.nn.sigmoid(pre)
        act_ref[...] = (pre * gate).astype(BF16)
        pre_grad = (back_ref[...] * gate * (1.0 + pre * (1.0 - gate))).astype(BF16)
        pre_grad_ref[...] = pre_grad
        along = jnp.sum(pre_grad.astype(F32) * pre, axis=1, keepdims=True)
        along_ref[...] = jnp.broadcast_to(scale * along / features, along_ref.shape)


def expert_grad_kernel(plan, pre_grad_ref, up_ref, along_ref, *refs):
    count = len(refs) // 2
    total = dot_nt(pre_grad_ref[...], up_ref[...])
    for piece, at, to, size in plan:
        rows = refs[piece][at : at + size, :].astype(F32)
        refs[count + piece][at : at + size, :] = (
            total[to : to + size, :] - rows * along_ref[to : to + size, :1]
        ).astype(BF16)


def expert_out_kernel(capacity, me_ref, act_ref, down_ref, out_ref):
    total = dot(act_ref[...], down_ref[...]).astype(BF16)
    for i in range(total.shape[0] // capacity):
        to = pl.multiple_of((i ^ me_ref[0]) * capacity, 8)
        out_ref[pl.ds(to, capacity), :] = total[i * capacity : (i + 1) * capacity, :]


def on_device(inputs, b_proj, c_proj, log_decay, doc_lengths, expert_ids, gate_weights, w_up, w_down, cotangent):
    tokens, features = inputs.shape[1:]
    heads = log_decay.shape[1]
    state = b_proj.shape[2]
    experts, blocks = lax.axis_size("exp"), lax.axis_size("seq")
    hidden = w_up.shape[2]
    capacity = 3 * tokens // experts
    slots = experts * capacity
    width = features // CHUNKS
    hops = max(1, blocks // 2)
    relayed = experts == 8
    kinds = ((2, (0, 1, 4, 5)), (4, (0, 1, 2, 3)))

    x, b, c, log, cot = inputs[0], b_proj[0], c_proj[0], log_decay[0], cotangent[0]
    up, down = w_up[0], w_down[0]
    meta = jnp.concatenate([doc_lengths[0], (lax.axis_index("seq") * tokens)[None].astype(jnp.int32)])

    def log_spec(k):
        return pl.BlockSpec((heads // CHUNKS, tokens), lambda i: (k, 0))

    def chunk(k, rows=tokens):
        return pl.BlockSpec((rows, width), lambda i: (0, k))

    def shape(rows, columns, kind=BF16):
        return jax.ShapeDtypeStruct((rows, columns), kind)

    small, part = whole((tokens, state)), whole((tokens, width))
    unit = tokens * width
    head_flops = 2 * tokens * unit

    def offset(a, k):
        return lax.ppermute(a, "exp", [(i, i ^ k) for i in range(experts)])

    def hop(states, step):
        return lax.ppermute(states, "seq", [(i, i + step) for i in range(blocks) if 0 <= i + step < blocks])

    def hop_on(arrived, step, k, after):
        for _ in range(hops - 1):
            kept = call(
                keep_kernel,
                (1,),
                [SMEM, log_spec(k), part],
                part,
                shape(tokens, width),
                unit,
                4 * unit,
                "keep_states",
                after=after,
            )(meta, log, arrived[-1])
            arrived = arrived + [hop(kept, step)]
        return arrived, kept

    states_in, near = [], []
    for k in range(CHUNKS):
        local = call(
            local_kernel,
            (1,),
            [SMEM, log_spec(k), small, chunk(k)],
            part,
            shape(tokens, width),
            head_flops,
            4 * unit,
            "local_states",
            after=near,
        )(meta, log, b, x)
        states_in.append([hop(local, 1)])
        near = [local]

    table = jnp.concatenate([expert_ids[0].T.astype(F32), gate_weights[0].T], axis=0)
    me = (lax.axis_index("exp") if relayed else jnp.zeros((), jnp.int32)).astype(jnp.int32)[None]
    pick, weights, sent_cot = call(
        functools.partial(direct_pick_kernel, experts, capacity),
        (1,),
        [whole((4, tokens)), whole((tokens, features))],
        [whole((slots, tokens)), whole((tokens, slots)), whole((slots, features))],
        [shape(slots, tokens), shape(tokens, slots), shape(slots, features)],
        2 * slots * tokens * features,
        2 * (slots + tokens) * features,
        "pick_rows",
        after=near,
    )(table, cot)

    def switch(rows):
        parts = rows.reshape(experts, capacity, rows.shape[1])
        return lax.all_to_all(parts, "exp", split_axis=0, concat_axis=0, tiled=True).reshape(rows.shape)

    got_cot = switch(sent_cot)
    if relayed:
        plans = [
            [
                block
                for i, o in enumerate(offsets)
                for block in ((i, 0, o * capacity, capacity), (i, capacity, (o ^ by) * capacity, capacity))
            ]
            for by, offsets in kinds
        ]
        pieces_of = [[2 * capacity] * 4] * 2
        pick_shape = (4, 2, capacity, tokens)
        weight_shape = (4, tokens, 2 * capacity)
        outs = [pick_shape, weight_shape, weight_shape] * 2
        found = call(
            functools.partial(relay_pick_kernel, experts, capacity, kinds),
            (1,),
            [SMEM] + [whole((4, tokens))] * 3,
            [whole(s) for s in outs],
            [jax.ShapeDtypeStruct(s, BF16) for s in outs],
            6 * experts * tokens * tokens,
            4 * slots * tokens,
            "pick_relayed",
        )(me, table, *[offset(table, by) for by, _ in kinds])
        picks, own_weights, relay_weights = found[0::3], found[1::3], found[2::3]
    else:
        plans = [[(0, 0, 0, slots)]] * 2
        pieces_of = [[slots]] * 2
        picks, own_weights = [pick] * 2, [weights[None]] * 2

    def piece_specs(kind):
        return [whole((rows, width)) for rows in pieces_of[kind]]

    def piece_shapes(kind):
        return [shape(rows, width) for rows in pieces_of[kind]]

    def to_experts(rows, k, other, after=()):
        kind = k % 2
        cost = (2 * slots * unit, 2 * (unit + slots * width))
        if not relayed:
            sent = call(
                direct_gather_kernel,
                (1,),
                [whole((slots, tokens)), part],
                piece_specs(kind),
                piece_shapes(kind),
                *cost,
                "gather",
                after=after,
            )(picks[kind], rows)
            return sent, [switch(sent[0])]
        _, offsets = kinds[kind]
        sent = call(
            gather_kernel,
            (1,),
            [whole(picks[kind].shape), part, part],
            piece_specs(kind),
            piece_shapes(kind),
            *cost,
            "gather",
            after=after,
        )(picks[kind], rows, other)
        return sent, [piece if o == 0 else offset(piece, o) for piece, o in zip(sent, offsets)]

    def other_of(rows, k):
        return offset(rows, kinds[k % 2][0]) if relayed else None

    def to_positions(pieces, k, after=()):
        kind = k % 2
        if not relayed:
            arrived = [switch(pieces[0])]
            return arrived[0], arrived
        by, offsets = kinds[kind]
        pieces = [piece if o == 0 else offset(piece, o) for piece, o in zip(pieces, offsets)]
        relay = call(
            relay_kernel,
            (1,),
            [whole(relay_weights[kind].shape)] + piece_specs(kind),
            part,
            shape(tokens, width),
            2 * slots * unit,
            2 * (unit + slots * width),
            "relay",
            after=after,
        )(relay_weights[kind], *pieces)
        return relay, pieces + [offset(relay, by)]

    def moved_specs(kind):
        return piece_specs(kind) + ([part] if relayed else [])

    inner = call(
        inner_kernel,
        (CHUNKS,),
        [SMEM, pl.BlockSpec((heads // CHUNKS, tokens), lambda i: (i, 0)), small, small, columns(tokens, width)],
        columns(tokens, width),
        shape(tokens, features, F32),
        2 * CHUNKS * head_flops,
        6 * CHUNKS * unit,
        "inner",
        after=[sent_cot],
    )(meta, log, b, c, x)
    states_in[0], kept = hop_on(states_in[0], 1, 0, [inner, picks[0]])
    states_in[1], _ = hop_on(states_in[1], 1, 1, [] if kept is None else [kept])

    resid, squares, others = [], [], []
    for k in range(CHUNKS):
        rows, square = call(
            functools.partial(resid_kernel, hops),
            (1,),
            [SMEM, log_spec(k), small, chunk(k)] + [part] * hops,
            [part, whole((tokens, 128))],
            [shape(tokens, width), shape(tokens, 128, F32)],
            hops * head_flops,
            (6 + 2 * hops) * unit,
            "resid",
        )(meta, log, c, inner, *states_in[k])
        resid.append(rows)
        squares.append(square)
        others.append(other_of(rows, k))
    (sent, *_), pieces = to_experts(resid[0], 0, others[0], [resid[1]])
    got_in = [pieces]

    each = 2
    step = width // each
    chunk_flops = 2 * slots * width * hidden
    chunk_bytes = 2 * width * (hidden + slots)
    slots_hidden = whole((slots, hidden))

    def step_specs(kind, first=0):
        return [
            pl.BlockSpec((rows, step), lambda i: (0, jnp.clip(i - first, 0, each - 1))) for rows in pieces_of[kind]
        ]

    back = call(
        functools.partial(back_kernel, capacity),
        (4,),
        [SMEM, columns(slots, features // 4), columns(hidden, features // 4)],
        slots_hidden,
        shape(slots, hidden, F32),
        CHUNKS * chunk_flops,
        CHUNKS * chunk_bytes,
        "back",
        [pltpu.VMEM((slots, hidden), F32)],
        after=[sent],
    )(me, got_cot, down)
    _, pieces = to_experts(resid[1], 1, others[1], [back])
    got_in.append(pieces)

    def up_spec(k):
        return pl.BlockSpec((step, hidden), lambda i: (each * k + i, 0))

    slots_small = whole((slots, 128))
    total, total_squares = call(
        functools.partial(up_first_kernel, plans[0]),
        (each,),
        step_specs(0) + [up_spec(0)],
        [slots_hidden, slots_small],
        [shape(slots, hidden, F32), shape(slots, 128, F32)],
        chunk_flops,
        chunk_bytes,
        "up_first",
        [pltpu.VMEM((slots, step), BF16)],
    )(*got_in[0], up)
    act, pre_grad, along = call(
        functools.partial(up_last_kernel, plans[1], features),
        (each,),
        step_specs(1) + [up_spec(1), slots_hidden, slots_small, slots_hidden],
        [slots_hidden, slots_hidden, slots_small],
        [shape(slots, hidden), shape(slots, hidden), shape(slots, 128, F32)],
        chunk_flops,
        chunk_bytes,
        "up_last",
        [pltpu.VMEM((slots, hidden), F32), pltpu.VMEM((slots, 128), F32), pltpu.VMEM((slots, step), BF16)],
    )(*got_in[1], up, total, total_squares, back)

    got_grad = []
    for k in range(CHUNKS):
        kind = k % 2
        expert_grad = call(
            functools.partial(expert_grad_kernel, plans[kind]),
            (each,),
            [slots_hidden, up_spec(k), slots_small] + step_specs(kind),
            step_specs(kind),
            piece_shapes(kind),
            chunk_flops,
            chunk_bytes,
            "expert_grad",
        )(pre_grad, up, along, *got_in[k])
        relay, pieces = to_positions(expert_grad, k)
        got_grad.append(pieces)
    expert_out = call(
        functools.partial(expert_out_kernel, capacity),
        (4,),
        [SMEM, slots_hidden, columns(hidden, features // 4)],
        columns(slots, features // 4),
        shape(slots, features),
        CHUNKS * chunk_flops,
        CHUNKS * chunk_bytes,
        "expert_out",
        after=[relay],
    )(me, act, down)
    got_out = switch(expert_out)
    last = expert_out

    def weights_spec(kind):
        return whole(own_weights[kind].shape)

    dresid, states_after = [], []
    for k in range(CHUNKS):
        kind = k % 2
        grad, source = call(
            functools.partial(dresid_kernel, CHUNKS, features),
            (1,),
            [SMEM, log_spec(k), small, weights_spec(kind), chunk(k)]
            + [whole((tokens, 128))] * CHUNKS
            + moved_specs(kind),
            [part, part],
            [shape(tokens, width)] * 2,
            head_flops + 2 * slots * unit,
            6 * unit + 2 * slots * width,
            "dresid",
            after=[last],
        )(meta, log, c, own_weights[kind], cot, *squares, *got_grad[k])
        dresid.append(grad)
        states_after.append([hop(source, -1)])
        last = grad

    inner_back = [
        call(
            inner_back_kernel,
            (1,),
            [SMEM, log_spec(k), small, small, part],
            part,
            shape(tokens, width, F32),
            2 * head_flops,
            6 * unit,
            "inner_back",
            after=[last],
        )(meta, log, b, c, dresid[k])
        for k in range(CHUNKS)
    ]
    states_after[0], last = hop_on(states_after[0], -1, 0, inner_back)
    states_after[1], last = hop_on(states_after[1], -1, 1, [last])

    def placed(kernel, k, in_specs, operands, earlier, after, flops, nbytes, name):
        more = [] if earlier is None else [earlier]
        return call(
            kernel,
            (1,),
            in_specs + [pl.BlockSpec(memory_space=pl.ANY)] * len(more),
            chunk(k),
            shape(tokens, features),
            flops,
            nbytes,
            name,
            after=after,
            aliases={len(operands): 0} if more else {},
        )(*operands, *more)

    def input_grads(k, earlier, after):
        return placed(
            functools.partial(grad_kernel, hops),
            k,
            [SMEM, log_spec(k), small, part] + [part] * hops,
            [meta, log, b, inner_back[k], *states_after[k]],
            earlier,
            after,
            hops * head_flops,
            (6 + 2 * hops) * unit,
            "input_grad",
        )

    input_grad = input_grads(0, None, [last])
    output = call(
        output_kernel,
        (1,),
        [whole((tokens, slots)), whole((slots, features))] + [part] * CHUNKS,
        whole((tokens, features)),
        shape(tokens, features),
        2 * slots * tokens * features,
        2 * (slots + 2 * tokens) * features,
        "output",
        after=[input_grad],
    )(weights, got_out, *resid)
    input_grad = input_grads(1, input_grad, [output])
    return (output[None], input_grad[None])


def solution(mesh):
    placed = (
        P("exp", "seq", None),
        P("exp", "seq", None),
        P("exp", "seq", None),
        P("exp", None, "seq"),
        P("exp", None),
        P("exp", "seq", None),
        P("exp", "seq", None),
        P("exp", None, None),
        P("exp", None, None),
        P("exp", "seq", None),
    )
    return jax.shard_map(
        on_device,
        mesh=mesh,
        in_specs=placed,
        out_specs=(P("exp", "seq", None), P("exp", "seq", None)),
        check_vma=False,
    )
```

```python
import functools

import jax
import jax.numpy as jnp
from jax import lax
from jax.experimental import pallas as pl
from jax.experimental.pallas import tpu as pltpu
from jax.sharding import PartitionSpec as P

EPSILON = 1e-06
F32 = jnp.float32
BF16 = jnp.bfloat16
CHUNKS = 2
VMEM_BYTES = 32 * 1024 * 1024
VMEM_ALL = 60 * 1024 * 1024
NT = (((1,), (1,)), ((), ()))


def dot(a, b):
    return jnp.dot(a, b, preferred_element_type=F32)


def dot_nt(a, b):
    return lax.dot_general(a, b, NT, preferred_element_type=F32)


def call(kernel, grid, in_specs, out_specs, out_shape, flops, nbytes, name, scratch=(), after=(), aliases=None, vmem=VMEM_BYTES):
    count, more = len(in_specs), len(after)

    def body(*refs):
        kernel(*refs[:count], *refs[count + more :])

    called = pl.pallas_call(
        body,
        grid=grid,
        in_specs=list(in_specs) + [pl.BlockSpec(memory_space=pl.ANY)] * more,
        out_specs=out_specs,
        out_shape=out_shape,
        scratch_shapes=scratch,
        input_output_aliases=aliases or {},
        name=name,
        cost_estimate=pl.CostEstimate(flops=flops, bytes_accessed=nbytes, transcendentals=0),
        compiler_params=pltpu.CompilerParams(vmem_limit_bytes=vmem),
    )
    return lambda *operands: called(*operands, *after)


def whole(shape):
    return pl.BlockSpec(shape, lambda i: (0,) * len(shape))


def columns(rows, width):
    return pl.BlockSpec((rows, width), lambda i: (0, i))


anywhere = pl.BlockSpec(memory_space=pl.ANY)
SMEM = pl.BlockSpec(memory_space=pltpu.SMEM)


def documents(meta, size, shift=0):
    count = meta.shape[0] - 1
    first = meta[count] + shift * size
    along = first + lax.broadcasted_iota(jnp.int32, (1, size), 1)
    down = first + lax.broadcasted_iota(jnp.int32, (size, 1), 0)
    row = jnp.full((1, size), -1, jnp.int32)
    col = jnp.full((size, 1), -1, jnp.int32)
    before, last, start = jnp.int32(-1), jnp.int32(-1), jnp.int32(0)
    for i in range(count):
        row += (start <= along).astype(jnp.int32)
        col += (start <= down).astype(jnp.int32)
        before += (start <= first - 1).astype(jnp.int32)
        last += (start <= first + size - 1).astype(jnp.int32)
        start = start + meta[i]
    return row, col, before, last


def running(log_ref):
    size = log_ref.shape[1]
    upto = (
        lax.broadcasted_iota(jnp.int32, (size, size), 0)
        <= lax.broadcasted_iota(jnp.int32, (size, size), 1)
    ).astype(F32)
    return jnp.dot(
        log_ref[...], upto, precision=lax.Precision.HIGHEST, preferred_element_type=F32
    )


def head(h, size):
    return slice(h * size, (h + 1) * size)


def local_kernel(meta, log_ref, b_ref, x_ref, state_ref):
    size = log_ref.shape[1]
    cum = running(log_ref)
    row, _, _, last = documents(meta, size)
    tail = (row == last).astype(F32)
    weight = tail * jnp.exp(cum[:, size - 1 :] - cum)
    b_t = b_ref[...].astype(F32).T
    p = x_ref.shape[1] // cum.shape[0]
    for h in range(cum.shape[0]):
        b_weighted = (b_t * weight[h : h + 1, :]).astype(BF16)
        state_ref[:, head(h, p)] = dot(b_weighted, x_ref[:, head(h, p)]).astype(BF16)


def pair_mask(meta, size):
    row, col, before, last = documents(meta, size)
    later = lax.broadcasted_iota(jnp.int32, (size, size), 0)
    earlier = lax.broadcasted_iota(jnp.int32, (size, size), 1)
    return row, col, before, last, later, earlier


def inner_kernel(meta, log_ref, b_ref, c_ref, x_ref, out_ref):
    size = log_ref.shape[1]
    cum = running(log_ref)
    cum_t = cum.T
    row, col, _, _, down, along = pair_mask(meta, size)
    scores = jnp.where((row == col) & (down >= along), dot_nt(c_ref[...], b_ref[...]), 0.0)
    p = x_ref.shape[1] // cum.shape[0]
    for h in range(cum.shape[0]):
        spread = cum_t[:, h : h + 1] - cum[h : h + 1, :]
        pair = (jnp.exp(jnp.minimum(spread, 0.0)) * scores).astype(BF16)
        out_ref[:, head(h, p)] = dot(pair, x_ref[:, head(h, p)])


def inner_back_kernel(meta, log_ref, b_ref, c_ref, grad_ref, out_ref):
    size = log_ref.shape[1]
    cum = running(log_ref)
    cum_t = cum.T
    row, col, _, _, down, along = pair_mask(meta, size)
    scores = jnp.where((row == col) & (down <= along), dot_nt(b_ref[...], c_ref[...]), 0.0)
    p = grad_ref.shape[1] // cum.shape[0]
    for h in range(cum.shape[0]):
        spread = cum[h : h + 1, :] - cum_t[:, h : h + 1]
        pair = (jnp.exp(jnp.minimum(spread, 0.0)) * scores).astype(BF16)
        out_ref[:, head(h, p)] = dot(pair, grad_ref[:, head(h, p)])


def keep_kernel(meta, log_ref, state_ref, out_ref):
    size = log_ref.shape[1]
    total = jnp.exp(running(log_ref)[:, size - 1 :])
    _, _, before, last = documents(meta, size)
    total = jnp.where(before == last, total, 0.0)
    p = state_ref.shape[1] // total.shape[0]
    for h in range(total.shape[0]):
        out_ref[:, head(h, p)] = (
            state_ref[:, head(h, p)].astype(F32) * total[h : h + 1, :]
        ).astype(BF16)


def prepare_kernel(b_ref, c_ref, log_ref, cot_ref, ids_ref, gates_ref, b_pack_ref, c_pack_ref, *chunks):
    chunks, both = chunks[:-1], chunks[-1]
    size = ids_ref.shape[1]
    width = chunks[0].shape[1] - size
    table = jnp.concatenate([ids_ref[...].astype(F32), gates_ref[...], jnp.zeros((size - 4, size), F32)], axis=0)
    table = table.T.astype(BF16)
    for k, chunk in enumerate(chunks):
        for ref, to in ((chunk, 0), (both, k * size)):
            ref[to : to + size, :width] = cot_ref[:, k * width : (k + 1) * width]
            ref[to : to + size, width:] = table
    rest, heads, at = log_ref[...], log_ref.shape[0], b_ref.shape[0]
    b_pack_ref[:at, :] = b_ref[...]
    c_pack_ref[:at, :] = c_ref[...]
    for _ in range(3):
        term = rest.astype(BF16)
        rest = rest - term.astype(F32)
        b_pack_ref[at : at + heads, :] = term
        c_pack_ref[at : at + heads, :] = term
        at += heads


def pass_kernel(ahead, chunk, meta, log_ref, near_ref, far_ref, rows_ref, state_ref, sent_ref):
    size, heads = log_ref.shape[1], log_ref.shape[0]
    half = size // 2
    _, _, before, last = documents(meta, size)
    near_row, _, _, _ = documents(meta, size, -1 if ahead else 1)
    far_row, _, _, _ = documents(meta, size, 1 if ahead else -1)
    total = jnp.where(before == last, jnp.exp(running(log_ref)[:, size - 1 :]), 0.0)
    terms = (near_ref.shape[0] - size) // 3
    near_log = jnp.zeros((heads, size), F32)
    for i in range(3):
        at = size + i * terms + chunk * heads
        near_log += near_ref[at : at + heads, :].astype(F32)
    cum = running(near_log)
    if ahead:
        weight = jnp.where(near_row == before, jnp.exp(cum[:, size - 1 :] - cum), 0.0)
        count = jnp.sum((far_row == last).astype(F32), axis=1, keepdims=True)
        rows, wanted = slice(half, size), slice(0, half)
    else:
        weight = jnp.where(near_row == last, jnp.exp(cum), 0.0)
        count = jnp.sum((far_row == before).astype(F32), axis=1, keepdims=True)
        rows, wanted = slice(0, half), slice(half, size)
    few = (count <= half).astype(F32)
    weight_t = weight.T
    near_t = near_ref[:size, :].astype(F32).T
    far = far_ref[wanted, :]
    width = rows_ref.shape[1]
    p = width // heads
    for h in range(heads):
        at = head(h, p)
        state = dot((near_t * weight[h : h + 1, :]).astype(BF16), rows_ref[:, at]).astype(BF16)
        state_ref[:, at] = state
        scale = total[h : h + 1, :]
        sums = dot(far, state) * (few * scale)
        scaled = rows_ref[rows, at].astype(F32) * (weight_t[rows, h : h + 1] * ((1.0 - few) * scale))
        sent_ref[:, at] = (sums + scaled).astype(BF16)
    sent_ref[:, width:] = near_ref[rows, :]


def spread_of(few, shift, mine, theirs):
    size, half = mine.shape[0], theirs.shape[0]
    down = lax.broadcasted_iota(jnp.int32, (size, half), 0)
    along = lax.broadcasted_iota(jnp.int32, (size, half), 1)
    same = (down == along + shift).astype(F32)
    return (few * same + (1.0 - few) * dot_nt(mine, theirs)).astype(BF16)


def carried_in(mine, spread, states, at):
    carried = dot(mine, states[0][:, at])
    if spread is not None:
        return carried + dot(spread, states[1][:, at])
    for state in states[1:]:
        carried += dot(mine, state[:, at])
    return carried


def resid_kernel(relayed, meta, log_ref, c_ref, inner_ref, *refs):
    states, (resid_ref, squares_ref) = refs[:-2], refs[-2:]
    size = log_ref.shape[1]
    row, col, before, _ = documents(meta, size)
    weight = jnp.where(col == before, jnp.exp(running(log_ref).T), 0.0)
    width = inner_ref.shape[1]
    p = width // log_ref.shape[0]
    spread = None
    if relayed:
        few = (jnp.sum((row == before).astype(F32), axis=1, keepdims=True) <= size // 2).astype(F32)
        spread = spread_of(few, 0, c_ref[...], states[2][...])
    squares = jnp.zeros((size, p), F32)
    for h in range(log_ref.shape[0]):
        carried = carried_in(c_ref[...], spread, states, head(h, p))
        rows = (inner_ref[:, head(h, p)] + weight[:, h : h + 1] * carried).astype(BF16)
        resid_ref[:, head(h, p)] = rows
        squares += rows.astype(F32) * rows.astype(F32)
    squares_ref[...] = jnp.broadcast_to(jnp.sum(squares, axis=1, keepdims=True), squares_ref.shape)


def combined(weights_ref, pieces):
    total = dot(weights_ref[0], pieces[0][...])
    for i, piece in enumerate(pieces[1:]):
        total += dot(weights_ref[i + 1], piece[...])
    return total


def relay_kernel(weights_ref, *refs):
    pieces, out_ref = refs[:-1], refs[-1]
    out_ref[...] = combined(weights_ref, pieces).astype(BF16)


def dresid_kernel(chunks, features, meta, log_ref, c_ref, weights_ref, cot_ref, *refs):
    squares, refs = refs[:chunks], refs[chunks:]
    count = weights_ref.shape[0]
    relayed = weights_ref.shape[0] > 1
    moved_refs, outs = (refs[:-1], refs[-1:]) if relayed else (refs[:-2], refs[-2:])
    dresid_ref = outs[0]
    size = log_ref.shape[1]
    row, _, before, _ = documents(meta, size)
    weight = jnp.where(row == before, jnp.exp(running(log_ref)), 0.0)
    c_t = c_ref[...].astype(F32).T
    total = squares[0][...]
    for part in squares[1:]:
        total = total + part[...]
    scale = lax.rsqrt(total[:, :1] / features + EPSILON)
    moved = combined(weights_ref, moved_refs[:count])
    for arrived in moved_refs[count:]:
        moved += arrived[...].astype(F32)
    dresid_ref[...] = (cot_ref[...].astype(F32) + scale * moved).astype(BF16)
    if relayed:
        return
    p = cot_ref.shape[1] // log_ref.shape[0]
    for h in range(log_ref.shape[0]):
        c_weighted = (c_t * weight[h : h + 1, :]).astype(BF16)
        outs[1][:, head(h, p)] = dot(c_weighted, dresid_ref[:, head(h, p)]).astype(BF16)


def grad_kernel(count, relayed, meta, log_ref, b_ref, inner_ref, *refs):
    states, out_ref = refs[:count], refs[-1]
    size = log_ref.shape[1]
    row, col, _, last = documents(meta, size)
    cum = running(log_ref)
    weight = jnp.where(col == last, jnp.exp(cum[:, size - 1 :] - cum).T, 0.0)
    width = inner_ref.shape[1]
    p = width // log_ref.shape[0]
    spread = None
    if relayed:
        few = (jnp.sum((row == last).astype(F32), axis=1, keepdims=True) <= size // 2).astype(F32)
        spread = spread_of(few, size // 2, b_ref[...], states[2][...])
    for h in range(log_ref.shape[0]):
        carried = carried_in(b_ref[...], spread, states, head(h, p))
        out_ref[:, head(h, p)] = (inner_ref[:, head(h, p)] + weight[:, h : h + 1] * carried).astype(BF16)


def output_kernel(weights_ref, resid_ref, *refs):
    out_ref = refs[-1]
    count = weights_ref.shape[0]
    moved = combined(weights_ref, refs[:count])
    for arrived in refs[count : len(refs) - 1]:
        if arrived.shape == out_ref.shape:
            moved += arrived[...].astype(F32)
    out_ref[...] = (resid_ref[...].astype(F32) + moved).astype(BF16)


def picks_of(table, me, experts, capacity):
    tokens = table.shape[1]
    offset = lax.broadcasted_iota(jnp.int32, (experts, tokens), 0)
    first = (table[0:1, :].astype(jnp.int32) ^ me) == offset
    second = (table[1:2, :].astype(jnp.int32) ^ me) == offset
    named = (first | second).astype(F32)
    gate = jnp.where(first, table[2:3, :], 0.0) + jnp.where(second, table[3:4, :], 0.0)
    before = (
        lax.broadcasted_iota(jnp.int32, (tokens, tokens), 0)
        < lax.broadcasted_iota(jnp.int32, (tokens, tokens), 1)
    ).astype(BF16)
    rank = jnp.where(named > 0, dot(named.astype(BF16), before), -1.0)
    slot = lax.broadcasted_iota(jnp.int32, (capacity, tokens), 0).astype(F32)
    picks = [(rank[e : e + 1, :] == slot).astype(F32) for e in range(experts)]
    return picks, [pick * gate[e : e + 1, :] for e, pick in enumerate(picks)]


def direct_pick_kernel(experts, capacity, table_ref, pick_ref, weights_ref):
    picks, gated = picks_of(table_ref[...], 0, experts, capacity)
    pick_ref[...] = jnp.concatenate(picks, axis=0).astype(BF16)
    weights_ref[0] = jnp.concatenate(gated, axis=0).T.astype(BF16)


def relay_pick_kernel(experts, capacity, kinds, me_ref, own_ref, *refs):
    tables, outs = refs[: len(kinds)], refs[len(kinds) :]
    me = me_ref[0]
    picks, gated = picks_of(own_ref[...].astype(F32).T, me, experts, capacity)
    none = jnp.zeros_like(picks[0])
    for (_, offsets), table_ref, (pick_ref, own_weights_ref, relay_weights_ref) in zip(
        kinds, tables, (outs[:3], outs[3:])
    ):
        other_picks, other_gated = picks_of(table_ref[...].astype(F32).T, me, experts, capacity)
        for i, o in enumerate(offsets):
            pick_ref[i, 0] = picks[o].astype(BF16)
            pick_ref[i, 1] = other_picks[o].astype(BF16)
            own_weights_ref[i] = jnp.concatenate([gated[o], none], axis=0).T.astype(BF16)
            relay_weights_ref[i] = jnp.concatenate([none, other_gated[o]], axis=0).T.astype(BF16)


def side_pick_kernel(experts, capacity, kinds, me_ref, own_ref, sibling_ref, *refs):
    tables, outs = refs[:4], refs[4:]
    mine = [picks_of(t[...].astype(F32).T, me_ref[0], experts, capacity) for t in (own_ref, sibling_ref)]
    for k, (_, partner) in enumerate(kinds):
        near = [picks_of(t[...].astype(F32).T, me_ref[0], experts, capacity) for t in tables[2 * k : 2 * k + 2]]
        pick_ref, gated_ref = outs[2 * k : 2 * k + 2]
        for source, (picks, gated) in enumerate((mine[0], near[0], mine[1], near[1])):
            for e, to in enumerate((0, partner)):
                pick_ref[e, source] = picks[to].astype(BF16)
                gated_ref[e, source] = gated[to]


def side_weights_kernel(*refs):
    for gated_ref, weights_ref in zip(refs[:2], refs[2:]):
        for e in range(2):
            for source in range(4):
                weights_ref[source, e] = gated_ref[e, source].T.astype(BF16)


def side_gather_kernel(*refs):
    picks, rows, outs = refs[:2], (refs[2:6], refs[6:10]), (refs[10:12], refs[12:14])
    capacity = picks[0].shape[2]
    for e in (1, 0):
        for k in range(2):
            for source in range(4):
                at = slice(source * capacity, (source + 1) * capacity)
                outs[k][e][at, :] = dot(picks[k][e, source], rows[k][source][...]).astype(BF16)


def partial(weights_ref, pieces, source):
    slots = weights_ref.shape[3]
    rows = slice(source * slots, (source + 1) * slots)
    total = dot(weights_ref[source, 0], pieces[0][rows, :])
    for e, piece in enumerate(pieces[1:]):
        total += dot(weights_ref[source, e + 1], piece[rows, :])
    return total


def side_sums_kernel(*refs):
    weights, pieces, relayed_ref, own_ref = refs[:2], (refs[2:4], refs[4:6]), refs[6], refs[7]
    size = weights[0].shape[2]
    for ref, source in ((relayed_ref, 3), (own_ref, 2)):
        for k in range(2):
            ref[k * size : (k + 1) * size, :] = partial(weights[k], pieces[k], source).astype(BF16)


def side_relay_kernel(*refs):
    weights, pieces, arrived, outs = refs[:2], (refs[2:4], refs[4:6]), refs[6], refs[7:]
    size = weights[0].shape[2]
    for k in range(2):
        total = partial(weights[k], pieces[k], 1) + arrived[k * size : (k + 1) * size, :].astype(F32)
        outs[k][...] = total.astype(BF16)


def side_output_kernel(first_weights, second_weights, first_resid, second_resid, *refs):
    out_ref, refs = refs[-1], refs[:-1]
    count, width = len(refs) // 2, first_resid.shape[1]
    for k, (weights, resid) in enumerate(((first_weights, first_resid), (second_weights, second_resid))):
        terms = refs[k * count : (k + 1) * count]
        sums = partial(weights, terms[:2], 0)
        for arrived in terms[2:]:
            sums += arrived[...].astype(F32)
        out_ref[:, k * width : (k + 1) * width] = (resid[...].astype(F32) + sums).astype(BF16)


def hold_kernel(*refs):
    pass


def gather_kernel(pick_ref, own_ref, other_ref, *outs):
    capacity = pick_ref.shape[2]
    for i, out in enumerate(outs):
        out[:capacity, :] = dot(pick_ref[i, 0], own_ref[...]).astype(BF16)
        out[capacity:, :] = dot(pick_ref[i, 1], other_ref[...]).astype(BF16)


def direct_gather_kernel(pick_ref, own_ref, out_ref):
    out_ref[...] = dot(pick_ref[...], own_ref[...]).astype(BF16)


def assemble(plan, pieces, rows):
    for piece, at, to, count in plan:
        rows[to : to + count, :] = pieces[piece][at : at + count, :]


def back_kernel(plans, *refs):
    counts = [max(b[0] for b in plan) + 1 for plan in plans]
    pieces, (down_ref, back_ref, rows) = refs[: sum(counts)], refs[sum(counts) :]
    step, each = pl.program_id(0), pl.num_programs(0) // len(plans)
    for k, plan in enumerate(plans):
        mine = pieces[sum(counts[:k]) : sum(counts[: k + 1])]

        @pl.when(step // each == k)
        def _(plan=plan, mine=mine):
            assemble(plan, mine, rows)

    part = dot_nt(rows[...], down_ref[...])

    @pl.when(step == 0)
    def _():
        back_ref[...] = part

    @pl.when(step > 0)
    def _():
        back_ref[...] += part


def up_first_kernel(plan, *refs):
    pieces, (up_ref, total_ref, squares_ref, rows) = refs[:-4], refs[-4:]
    assemble(plan, pieces, rows)
    part = dot(rows[...], up_ref[...])
    values = rows[...].astype(F32)
    square = jnp.broadcast_to(jnp.sum(values * values, axis=1, keepdims=True), squares_ref.shape)

    @pl.when(pl.program_id(0) == 0)
    def _():
        total_ref[...] = part
        squares_ref[...] = square

    @pl.when(pl.program_id(0) > 0)
    def _():
        total_ref[...] += part
        squares_ref[...] += square


def up_last_kernel(plan, features, *refs):
    count = max(b[0] for b in plan) + 1
    pieces = refs[:count]
    up_ref, before_ref, before_squares_ref, back_ref, act_ref, pre_grad_ref, along_ref, total, squares, rows = refs[count:]
    step, steps = pl.program_id(0), pl.num_programs(0)
    assemble(plan, pieces, rows)
    part = dot(rows[...], up_ref[...])
    values = rows[...].astype(F32)
    square = jnp.broadcast_to(jnp.sum(values * values, axis=1, keepdims=True), squares.shape)

    @pl.when(step == 0)
    def _():
        total[...] = before_ref[...] + part
        squares[...] = before_squares_ref[...] + square

    @pl.when(step > 0)
    def _():
        total[...] += part
        squares[...] += square

    @pl.when(step == steps - 1)
    def _():
        scale = lax.rsqrt(squares[:, :1] / features + EPSILON)
        pre = total[...] * scale
        gate = jax.nn.sigmoid(pre)
        act_ref[...] = (pre * gate).astype(BF16)
        pre_grad = (back_ref[...] * gate * (1.0 + pre * (1.0 - gate))).astype(BF16)
        pre_grad_ref[...] = pre_grad
        along = jnp.sum(pre_grad.astype(F32) * pre, axis=1, keepdims=True)
        along_ref[...] = jnp.broadcast_to(scale * along / features, along_ref.shape)


def expert_grad_kernel(plan, pre_grad_ref, up_ref, along_ref, *refs):
    count = len(refs) // 2
    total = dot_nt(pre_grad_ref[...], up_ref[...])
    for piece, at, to, size in plan:
        rows = refs[piece][at : at + size, :].astype(F32)
        refs[count + piece][at : at + size, :] = (
            total[to : to + size, :] - rows * along_ref[to : to + size, :1]
        ).astype(BF16)


def expert_out_kernel(plan, act_ref, down_ref, *outs):
    total = dot(act_ref[...], down_ref[...])
    for piece, at, to, size in plan:
        outs[piece][at : at + size, :] = total[to : to + size, :].astype(BF16)


def on_device(inputs, b_proj, c_proj, log_decay, doc_lengths, expert_ids, gate_weights, w_up, w_down, cotangent):
    tokens, features = inputs.shape[1:]
    heads = log_decay.shape[1]
    state = b_proj.shape[2]
    experts, blocks = lax.axis_size("exp"), lax.axis_size("seq")
    hidden = w_up.shape[2]
    capacity = 3 * tokens // experts
    slots = experts * capacity
    width = features // CHUNKS
    hops = max(1, blocks // 2)
    relayed = experts == 8 and hops == 2
    kinds = ((2, (0, 1, 4, 5)), (4, (0, 1, 2, 3)))

    x, b, c, log, cot = inputs[0], b_proj[0], c_proj[0], log_decay[0], cotangent[0]
    up, down = w_up[0], w_down[0]
    meta = jnp.concatenate([doc_lengths[0], (lax.axis_index("seq") * tokens)[None].astype(jnp.int32)])

    def log_spec(k):
        return pl.BlockSpec((heads // CHUNKS, tokens), lambda i: (k, 0))

    def chunk(k, rows=tokens):
        return pl.BlockSpec((rows, width), lambda i: (0, k))

    def shape(rows, columns, kind=BF16):
        return jax.ShapeDtypeStruct((rows, columns), kind)

    small, part = whole((tokens, state)), whole((tokens, width))
    unit = tokens * width
    head_flops = 2 * tokens * unit

    def offset(a, k):
        return lax.ppermute(a, "exp", [(i, i ^ k) for i in range(experts)])

    def hop(states, step):
        return lax.ppermute(states, "seq", [(i, i + step) for i in range(blocks) if 0 <= i + step < blocks])

    def hop_on(arrived, spec, step, k, after):
        if relayed:
            near, far = (b_pack, c_pack) if step > 0 else (c_pack, b_pack)
            wide = arrived.shape[1]
            taken, sent = call(
                functools.partial(pass_kernel, step > 0, k),
                (1,),
                [SMEM, whole((heads, tokens)) if wide == features else log_spec(k), whole(near.shape), small, spec],
                [whole((tokens, wide)), whole((tokens // 2, wide + state))],
                [shape(tokens, wide), shape(tokens // 2, wide + state)],
                2 * head_flops,
                5 * unit,
                "pass_states",
                after=after,
            )(meta, log, near, far, arrived)
            passed = hop(sent, step)
            return [taken, passed, passed], sent
        arrived = [arrived]
        for _ in range(hops - 1):
            kept = call(
                keep_kernel,
                (1,),
                [SMEM, log_spec(k), part],
                part,
                shape(tokens, width),
                unit,
                4 * unit,
                "keep_states",
                after=after,
            )(meta, log, arrived[-1])
            arrived = arrived + [hop(kept, step)]
        return arrived, kept

    if relayed:
        moving = hop(x, 1)
        pack = (tokens + 3 * heads, state)
        b_pack, c_pack, *cots, cot_both = call(
            prepare_kernel,
            (1,),
            [small, small, whole((heads, tokens)), whole((tokens, features)), whole((2, tokens)), whole((2, tokens))],
            [whole(pack)] * 2 + [whole((tokens, width + 128))] * CHUNKS + [whole((2 * tokens, width + 128))],
            [shape(*pack)] * 2 + [shape(tokens, width + 128)] * CHUNKS + [shape(2 * tokens, width + 128)],
            0,
            4 * tokens * features,
            "prepare",
            vmem=VMEM_ALL,
        )(b, c, log, cot, expert_ids[0].T, gate_weights[0].T)
        b_pack, c_pack = hop(b_pack, 1), hop(c_pack, -1)
    else:
        moving = []
        for k in range(CHUNKS):
            local = call(
                local_kernel,
                (1,),
                [SMEM, log_spec(k), small, chunk(k)],
                part,
                shape(tokens, width),
                head_flops,
                4 * unit,
                "local_states",
            )(meta, log, b, x)
            moving.append(hop(local, 1))
        cots = [cot[:, k * width : (k + 1) * width] for k in range(CHUNKS)]

    if relayed:
        plans = [
            [
                block
                for i, o in enumerate(offsets)
                for block in ((i, 0, o * capacity, capacity), (i, capacity, (o ^ by) * capacity, capacity))
            ]
            for by, offsets in kinds
        ]
        pieces_of = [[2 * capacity] * 4] * 2
        pick_shape = (4, 2, capacity, tokens)
        weight_shape = (4, tokens, 2 * capacity)
        outs = [pick_shape, weight_shape, weight_shape] * 2
        me = lax.axis_index("exp").astype(jnp.int32)[None]
        other_cots = [offset(rows, by) for rows, (by, _) in zip(cots, kinds)]
        found = call(
            functools.partial(relay_pick_kernel, experts, capacity, kinds),
            (1,),
            [SMEM] + [pl.BlockSpec((tokens, 128), lambda i: (0, width // 128))] * 3,
            [whole(s) for s in outs],
            [jax.ShapeDtypeStruct(s, BF16) for s in outs],
            6 * experts * tokens * tokens,
            4 * slots * tokens,
            "pick_rows",
        )(me, cots[0], *other_cots)
        picks, own_weights, relay_weights = found[0::3], found[1::3], found[2::3]
    else:
        table = jnp.concatenate([expert_ids[0].T.astype(F32), gate_weights[0].T], axis=0)
        other_cots = [None] * CHUNKS
        plans = [[(0, 0, 0, slots)]] * 2
        pieces_of = [[slots]] * 2
        pick, weights = call(
            functools.partial(direct_pick_kernel, experts, capacity),
            (1,),
            [whole((4, tokens))],
            [whole((slots, tokens)), whole((1, tokens, slots))],
            [shape(slots, tokens), jax.ShapeDtypeStruct((1, tokens, slots), BF16)],
            2 * experts * tokens * tokens,
            4 * slots * tokens,
            "pick_rows",
        )(table)
        picks, own_weights = [pick] * 2, [weights] * 2

    def piece_specs(kind):
        return [whole((rows, width)) for rows in pieces_of[kind]]

    def piece_shapes(kind):
        return [shape(rows, width) for rows in pieces_of[kind]]

    def switch(pieces):
        parts = pieces[0].reshape(experts, capacity, width)
        return [lax.all_to_all(parts, "exp", split_axis=0, concat_axis=0, tiled=True).reshape(slots, width)]

    def to_experts(rows, k, other, after=()):
        kind = k % 2
        cost = (2 * slots * unit, 2 * (unit + slots * width))
        if not relayed:
            sent = call(
                direct_gather_kernel,
                (1,),
                [whole((slots, tokens)), part],
                piece_specs(kind),
                piece_shapes(kind),
                *cost,
                "gather",
                after=after,
            )(picks[kind], rows)
            return sent, switch(sent)
        _, offsets = kinds[kind]
        sent = call(
            gather_kernel,
            (1,),
            [whole(picks[kind].shape), part, part],
            piece_specs(kind),
            piece_shapes(kind),
            *cost,
            "gather",
            after=after,
        )(picks[kind], rows, other)
        return sent, [piece if o == 0 else offset(piece, o) for piece, o in zip(sent, offsets)]

    def other_of(rows, k):
        return offset(rows, kinds[k % 2][0]) if relayed else None

    def to_positions(pieces, k, after=()):
        kind = k % 2
        if not relayed:
            arrived = switch(pieces)
            return arrived[0], arrived
        by, offsets = kinds[kind]
        pieces = [piece if o == 0 else offset(piece, o) for piece, o in zip(pieces, offsets)]
        relay = call(
            relay_kernel,
            (1,),
            [whole(relay_weights[kind].shape)] + piece_specs(kind),
            part,
            shape(tokens, width),
            2 * slots * unit,
            2 * (unit + slots * width),
            "relay",
            after=after,
        )(relay_weights[kind], *pieces)
        return relay, pieces + [offset(relay, by)]

    def moved_specs(kind):
        return piece_specs(kind) + ([part] if relayed else [])

    inner = call(
        inner_kernel,
        (CHUNKS,),
        [SMEM, pl.BlockSpec((heads // CHUNKS, tokens), lambda i: (i, 0)), small, small, columns(tokens, width)],
        columns(tokens, width),
        shape(tokens, features, F32),
        2 * CHUNKS * head_flops,
        6 * CHUNKS * unit,
        "inner",
    )(meta, log, b, c, x)
    if relayed:
        first_in, kept = hop_on(moving, whole((tokens, features)), 1, 0, [inner, picks[0]])
        second_in = first_in
    else:
        first_in, kept = hop_on(moving[0], part, 1, 0, [inner, picks[0]])
    if relayed:
        held = call(
            hold_kernel,
            (1,),
            [anywhere] * 2,
            [anywhere] * 2,
            [shape(tokens, width + 128)] * 2,
            0,
            0,
            "hold",
            after=[kept],
            aliases={0: 0, 1: 1},
        )(*other_cots)
        cot_sibling = offset(cot_both, 1)
        side_others = [offset(rows, 1) for rows in held]
        table_spec = pl.BlockSpec((tokens, 128), lambda i: (0, width // 128))
        side_kinds = ((2, 4), (4, 2))
        side_plans = [
            [
                (e, j * capacity, (to ^ source) * capacity, capacity)
                for e, to in enumerate((0, partner))
                for j, source in enumerate((0, by, 1, by ^ 1))
            ]
            for by, partner in side_kinds
        ]
        side_shape, side_weight_shape = (2, 4, capacity, tokens), (4, 2, tokens, capacity)
        found = call(
            functools.partial(side_pick_kernel, experts, capacity, side_kinds),
            (1,),
            [SMEM] + [table_spec] * 6,
            [whole(side_shape)] * 4,
            [jax.ShapeDtypeStruct(side_shape, kind) for kind in (BF16, F32)] * 2,
            12 * experts * tokens * tokens,
            8 * slots * tokens,
            "side_picks",
        )(me, cots[0], cot_sibling, held[0], side_others[0], held[1], side_others[1])
        side_picks, side_gated = found[0::2], found[1::2]
        side_spec = whole((4 * capacity, width))
        both = [pl.BlockSpec((tokens, width), lambda i, k=k: (k, 0)) for k in range(2)]
        sent = call(
            side_gather_kernel,
            (1,),
            [whole(side_shape)] * 2 + [spec for k in range(2) for spec in (part, part, both[k], part)],
            [side_spec] * 4,
            [shape(4 * capacity, width)] * 4,
            4 * slots * unit,
            8 * slots * width,
            "side_gather",
            after=[kept],
        )(*side_picks, *[r for k in range(2) for r in (cots[k], held[k], cot_sibling, side_others[k])])
        got_cot = [[sent[2 * k], offset(sent[2 * k + 1], side_kinds[k][1])] for k in range(2)]
        sent = sent[1]
        early = [[], [pieces[1] for pieces in got_cot]]
    else:
        got_cot, sent, early = [], kept, [[], []]
        for k in range(CHUNKS):
            (sent, *_), pieces = to_experts(cots[k], k, other_cots[k], [sent])
            got_cot.append(pieces)
    if not relayed:
        second_in, _ = hop_on(moving[1], part, 1, 1, [sent])
    states_in = [first_in, second_in]


    def states_specs(k, w):
        if not relayed:
            return [part] * hops
        return [
            chunk(k),
            chunk(k, tokens // 2),
            pl.BlockSpec((tokens // 2, state), lambda i: (0, w // state)),
        ]

    resid, squares, others = [], [], []
    for k in range(CHUNKS):
        rows, square = call(
            functools.partial(resid_kernel, relayed),
            (1,),
            [SMEM, log_spec(k), small, chunk(k)] + states_specs(k, features),
            [part, whole((tokens, 128))],
            [shape(tokens, width), shape(tokens, 128, F32)],
            hops * head_flops,
            (6 + 2 * hops) * unit,
            "resid",
            after=early[k],
        )(meta, log, c, inner, *states_in[k])
        resid.append(rows)
        squares.append(square)
        others.append(other_of(rows, k))

    each = 2
    step = width // each
    chunk_flops = 2 * slots * width * hidden
    chunk_bytes = 2 * width * (hidden + slots)
    slots_hidden = whole((slots, hidden))

    def step_specs(kind, first=0):
        return [
            pl.BlockSpec((rows, step), lambda i: (0, jnp.clip(i - first, 0, each - 1))) for rows in pieces_of[kind]
        ]

    if relayed:
        cot_plans = side_plans
        cot_specs = [
            pl.BlockSpec((4 * capacity, step), lambda i, k=k: (0, jnp.clip(i - each * k, 0, each - 1)))
            for k in range(CHUNKS)
            for _ in range(2)
        ]
    else:
        cot_plans = [plans[k % 2] for k in range(CHUNKS)]
        cot_specs = [spec for k in range(CHUNKS) for spec in step_specs(k % 2, each * k)]
    back = call(
        functools.partial(back_kernel, cot_plans),
        (each * CHUNKS,),
        cot_specs + [columns(hidden, step)],
        slots_hidden,
        shape(slots, hidden, F32),
        CHUNKS * chunk_flops,
        CHUNKS * chunk_bytes,
        "back",
        [pltpu.VMEM((slots, step), BF16)],
        after=[resid[1]],
    )(*[piece for pieces in got_cot for piece in pieces], down)
    (sent, *_), pieces = to_experts(resid[0], 0, others[0], [back])
    got_in = [pieces]
    _, pieces = to_experts(resid[1], 1, others[1], [sent])
    got_in.append(pieces)

    def up_spec(k):
        return pl.BlockSpec((step, hidden), lambda i: (each * k + i, 0))

    slots_small = whole((slots, 128))
    total, total_squares = call(
        functools.partial(up_first_kernel, plans[0]),
        (each,),
        step_specs(0) + [up_spec(0)],
        [slots_hidden, slots_small],
        [shape(slots, hidden, F32), shape(slots, 128, F32)],
        chunk_flops,
        chunk_bytes,
        "up_first",
        [pltpu.VMEM((slots, step), BF16)],
    )(*got_in[0], up)
    act, pre_grad, along = call(
        functools.partial(up_last_kernel, plans[1], features),
        (each,),
        step_specs(1) + [up_spec(1), slots_hidden, slots_small, slots_hidden],
        [slots_hidden, slots_hidden, slots_small],
        [shape(slots, hidden), shape(slots, hidden), shape(slots, 128, F32)],
        chunk_flops,
        chunk_bytes,
        "up_last",
        [pltpu.VMEM((slots, hidden), F32), pltpu.VMEM((slots, 128), F32), pltpu.VMEM((slots, step), BF16)],
    )(*got_in[1], up, total, total_squares, back)

    got_grad, grads, last = [], [], []
    for k in range(CHUNKS):
        kind = k % 2
        expert_grad = call(
            functools.partial(expert_grad_kernel, plans[kind]),
            (each,),
            [slots_hidden, up_spec(k), slots_small] + step_specs(kind),
            step_specs(kind),
            piece_shapes(kind),
            chunk_flops,
            chunk_bytes,
            "expert_grad",
            after=last,
        )(pre_grad, up, along, *got_in[k])
        last = expert_grad[:1]
        grads.append(expert_grad)
    outs = []
    for k in range(CHUNKS):
        kind = k % 2
        expert_out = call(
            functools.partial(expert_out_kernel, side_plans[k] if relayed else plans[kind]),
            (each,),
            [slots_hidden, pl.BlockSpec((hidden, step), lambda i, k=k: (0, each * k + i))],
            [pl.BlockSpec((4 * capacity, step), lambda i: (0, i))] * 2 if relayed else step_specs(kind),
            [shape(4 * capacity, width)] * 2 if relayed else piece_shapes(kind),
            chunk_flops,
            chunk_bytes,
            "expert_out",
            after=last,
        )(act, down)
        outs.append(expert_out)
        last = expert_out[:1]

    for k in range(CHUNKS):
        relay, pieces = to_positions(grads[k], k, last)
        got_grad.append(pieces)
        last = [relay]
    last = relay

    def weights_spec(kind):
        return whole(own_weights[kind].shape)

    dresid, states_after = [], []
    for k in range(CHUNKS):
        kind = k % 2
        grads_here = call(
            functools.partial(dresid_kernel, CHUNKS, features),
            (1,),
            [SMEM, log_spec(k), small, weights_spec(kind), chunk(k)]
            + [whole((tokens, 128))] * CHUNKS
            + moved_specs(kind),
            [part] * (1 if relayed else 2),
            [shape(tokens, width)] * (1 if relayed else 2),
            head_flops + 2 * slots * unit,
            6 * unit + 2 * slots * width,
            "dresid",
            after=[last],
        )(meta, log, c, own_weights[kind], cot, *squares, *got_grad[k])
        dresid.append(grads_here[0])
        states_after.append(hop(grads_here[-1], -1))
        last = dresid[k]

    if relayed:
        states_after[0], last = hop_on(states_after[0], part, -1, 0, [last])
    inner_back = []
    for k in range(CHUNKS):
        last = call(
            inner_back_kernel,
            (1,),
            [SMEM, log_spec(k), small, small, part],
            part,
            shape(tokens, width, F32),
            2 * head_flops,
            6 * unit,
            "inner_back",
            after=[last],
        )(meta, log, b, c, dresid[k])
        inner_back.append(last)
    got_out = []
    if relayed:
        held = call(
            hold_kernel,
            (1,),
            [anywhere] * 2,
            [anywhere] * 2,
            [shape(4 * capacity, width)] * 2,
            0,
            0,
            "hold",
            after=[dresid[0]],
            aliases={0: 0, 1: 1},
        )(outs[0][1], outs[1][1])
        side_weights = call(
            side_weights_kernel,
            (1,),
            [whole(side_shape)] * 2,
            [whole(side_weight_shape)] * 2,
            [jax.ShapeDtypeStruct(side_weight_shape, BF16)] * 2,
            0,
            16 * slots * tokens,
            "side_weights",
            after=outs[0][:1],
        )(*side_gated)
        out_pieces = [[outs[k][0], offset(held[k], side_kinds[k][1])] for k in range(2)]
        states_after[1], last = hop_on(states_after[1], part, -1, 1, [last])
        operands = [*side_weights, *out_pieces[0], *out_pieces[1]]
        specs = [whole(side_weight_shape)] * 2 + [side_spec] * 4
        sums = call(
            side_sums_kernel,
            (1,),
            specs,
            [whole((2 * tokens, width))] * 2,
            [shape(2 * tokens, width)] * 2,
            4 * slots * unit,
            8 * slots * width,
            "side_sums",
            after=[last],
        )(*operands)
        sums_here = [offset(rows, 1) for rows in sums]
        sent = call(
            side_relay_kernel,
            (1,),
            specs + [whole((2 * tokens, width))],
            [part] * 2,
            [shape(tokens, width)] * 2,
            4 * slots * unit,
            8 * slots * width,
            "side_relay",
        )(*operands, sums_here[0])
        last = sent[0]
        relayed_sums = [offset(sent[k], side_kinds[k][0]) for k in range(2)]
    else:
        for k in range(CHUNKS):
            states_after[k], last = hop_on(states_after[k], part, -1, k, [last])
            last, pieces = to_positions(outs[k], k, [last])
            got_out.append(pieces)

    def placed(kernel, k, in_specs, operands, earlier, after, flops, nbytes, name):
        more = [] if earlier is None else [earlier]
        return call(
            kernel,
            (1,),
            in_specs + [pl.BlockSpec(memory_space=pl.ANY)] * len(more),
            chunk(k),
            shape(tokens, features),
            flops,
            nbytes,
            name,
            after=after,
            aliases={len(operands): 0} if more else {},
        )(*operands, *more)

    def input_grads(k, earlier, after):
        return placed(
            functools.partial(grad_kernel, 3 if relayed else hops, relayed),
            k,
            [SMEM, log_spec(k), small, part] + states_specs(0, width),
            [meta, log, b, inner_back[k], *states_after[k]],
            earlier,
            after,
            hops * head_flops,
            (6 + 2 * hops) * unit,
            "input_grad",
        )

    input_grad, output = input_grads(0, None, [last]), None
    if relayed:
        output = call(
            side_output_kernel,
            (1,),
            [whole(side_weight_shape)] * 2
            + [part] * 2
            + [spec for k in range(2) for spec in (side_spec, side_spec, both[k], part)],
            whole((tokens, features)),
            shape(tokens, features),
            2 * slots * unit,
            8 * unit + 4 * slots * width,
            "output",
            after=[input_grad],
        )(*side_weights, *resid, *[r for k in range(2) for r in (*out_pieces[k], sums_here[1], relayed_sums[k])])
    else:
        for k in range(CHUNKS):
            kind = k % 2
            output = placed(
                output_kernel,
                k,
                [weights_spec(kind), part] + moved_specs(kind),
                [own_weights[kind], resid[k], *got_out[k]],
                output,
                [input_grad] if output is None else [],
                2 * slots * unit,
                4 * unit + 2 * slots * width,
                "output",
            )
    input_grad = input_grads(1, input_grad, [output])
    return (output[None], input_grad[None])


def solution(mesh):
    placed = (
        P("exp", "seq", None),
        P("exp", "seq", None),
        P("exp", "seq", None),
        P("exp", None, "seq"),
        P("exp", None),
        P("exp", "seq", None),
        P("exp", "seq", None),
        P("exp", None, None),
        P("exp", None, None),
        P("exp", "seq", None),
    )
    return jax.shard_map(
        on_device,
        mesh=mesh,
        in_specs=placed,
        out_specs=(P("exp", "seq", None), P("exp", "seq", None)),
        check_vma=False,
    )
```

```python
import functools

import jax
import jax.numpy as jnp
from jax import lax
from jax.experimental import pallas as pl
from jax.experimental.pallas import tpu as pltpu
from jax.sharding import PartitionSpec as P

EPSILON = 1e-06
F32 = jnp.float32
BF16 = jnp.bfloat16
CHUNKS = 2
VMEM_BYTES = 32 * 1024 * 1024
VMEM_ALL = 60 * 1024 * 1024
NT = (((1,), (1,)), ((), ()))


def dot(a, b):
    return jnp.dot(a, b, preferred_element_type=F32)


def dot_nt(a, b):
    return lax.dot_general(a, b, NT, preferred_element_type=F32)


def call(kernel, grid, in_specs, out_specs, out_shape, flops, nbytes, name, scratch=(), after=(), aliases=None, vmem=VMEM_BYTES):
    count, more = len(in_specs), len(after)

    def body(*refs):
        kernel(*refs[:count], *refs[count + more :])

    called = pl.pallas_call(
        body,
        grid=grid,
        in_specs=list(in_specs) + [pl.BlockSpec(memory_space=pl.ANY)] * more,
        out_specs=out_specs,
        out_shape=out_shape,
        scratch_shapes=scratch,
        input_output_aliases=aliases or {},
        name=name,
        cost_estimate=pl.CostEstimate(flops=flops, bytes_accessed=nbytes, transcendentals=0),
        compiler_params=pltpu.CompilerParams(vmem_limit_bytes=vmem),
    )
    return lambda *operands: called(*operands, *after)


def whole(shape):
    return pl.BlockSpec(shape, lambda i: (0,) * len(shape))


def columns(rows, width):
    return pl.BlockSpec((rows, width), lambda i: (0, i))


anywhere = pl.BlockSpec(memory_space=pl.ANY)
SMEM = pl.BlockSpec(memory_space=pltpu.SMEM)


def documents(meta, size, shift=0):
    count = meta.shape[0] - 1
    first = meta[count] + shift * size
    along = first + lax.broadcasted_iota(jnp.int32, (1, size), 1)
    down = first + lax.broadcasted_iota(jnp.int32, (size, 1), 0)
    row = jnp.full((1, size), -1, jnp.int32)
    col = jnp.full((size, 1), -1, jnp.int32)
    before, last, start = jnp.int32(-1), jnp.int32(-1), jnp.int32(0)
    for i in range(count):
        row += (start <= along).astype(jnp.int32)
        col += (start <= down).astype(jnp.int32)
        before += (start <= first - 1).astype(jnp.int32)
        last += (start <= first + size - 1).astype(jnp.int32)
        start = start + meta[i]
    return row, col, before, last


def running(log_ref):
    size = log_ref.shape[1]
    upto = (
        lax.broadcasted_iota(jnp.int32, (size, size), 0)
        <= lax.broadcasted_iota(jnp.int32, (size, size), 1)
    ).astype(F32)
    return jnp.dot(
        log_ref[...], upto, precision=lax.Precision.HIGHEST, preferred_element_type=F32
    )


def head(h, size):
    return slice(h * size, (h + 1) * size)


def local_kernel(meta, log_ref, b_ref, x_ref, state_ref):
    size = log_ref.shape[1]
    cum = running(log_ref)
    row, _, _, last = documents(meta, size)
    tail = (row == last).astype(F32)
    weight = tail * jnp.exp(cum[:, size - 1 :] - cum)
    b_t = b_ref[...].astype(F32).T
    p = x_ref.shape[1] // cum.shape[0]
    for h in range(cum.shape[0]):
        b_weighted = (b_t * weight[h : h + 1, :]).astype(BF16)
        state_ref[:, head(h, p)] = dot(b_weighted, x_ref[:, head(h, p)]).astype(BF16)


def pair_mask(meta, size):
    row, col, before, last = documents(meta, size)
    later = lax.broadcasted_iota(jnp.int32, (size, size), 0)
    earlier = lax.broadcasted_iota(jnp.int32, (size, size), 1)
    return row, col, before, last, later, earlier


def inner_kernel(meta, log_ref, b_ref, c_ref, x_ref, out_ref):
    size = log_ref.shape[1]
    cum = running(log_ref)
    cum_t = cum.T
    row, col, _, _, down, along = pair_mask(meta, size)
    scores = jnp.where((row == col) & (down >= along), dot_nt(c_ref[...], b_ref[...]), 0.0)
    p = x_ref.shape[1] // cum.shape[0]
    for h in range(cum.shape[0]):
        spread = cum_t[:, h : h + 1] - cum[h : h + 1, :]
        pair = (jnp.exp(jnp.minimum(spread, 0.0)) * scores).astype(BF16)
        out_ref[:, head(h, p)] = dot(pair, x_ref[:, head(h, p)])


def inner_back_kernel(meta, log_ref, b_ref, c_ref, grad_ref, out_ref):
    size = log_ref.shape[1]
    cum = running(log_ref)
    cum_t = cum.T
    row, col, _, _, down, along = pair_mask(meta, size)
    scores = jnp.where((row == col) & (down <= along), dot_nt(b_ref[...], c_ref[...]), 0.0)
    p = grad_ref.shape[1] // cum.shape[0]
    for h in range(cum.shape[0]):
        spread = cum[h : h + 1, :] - cum_t[:, h : h + 1]
        pair = (jnp.exp(jnp.minimum(spread, 0.0)) * scores).astype(BF16)
        out_ref[:, head(h, p)] = dot(pair, grad_ref[:, head(h, p)])


def keep_kernel(meta, log_ref, state_ref, out_ref):
    size = log_ref.shape[1]
    total = jnp.exp(running(log_ref)[:, size - 1 :])
    _, _, before, last = documents(meta, size)
    total = jnp.where(before == last, total, 0.0)
    p = state_ref.shape[1] // total.shape[0]
    for h in range(total.shape[0]):
        out_ref[:, head(h, p)] = (
            state_ref[:, head(h, p)].astype(F32) * total[h : h + 1, :]
        ).astype(BF16)


def prepare_kernel(b_ref, c_ref, log_ref, cot_ref, ids_ref, gates_ref, b_pack_ref, c_pack_ref, *chunks):
    chunks, both = chunks[:-1], chunks[-1]
    size = ids_ref.shape[1]
    width = chunks[0].shape[1] - size
    table = jnp.concatenate([ids_ref[...].astype(F32), gates_ref[...], jnp.zeros((size - 4, size), F32)], axis=0)
    table = table.T.astype(BF16)
    for k, chunk in enumerate(chunks):
        for ref, to in ((chunk, 0), (both, k * size)):
            ref[to : to + size, :width] = cot_ref[:, k * width : (k + 1) * width]
            ref[to : to + size, width:] = table
    rest, heads, at = log_ref[...], log_ref.shape[0], b_ref.shape[0]
    b_pack_ref[:at, :] = b_ref[...]
    c_pack_ref[:at, :] = c_ref[...]
    for _ in range(3):
        term = rest.astype(BF16)
        rest = rest - term.astype(F32)
        b_pack_ref[at : at + heads, :] = term
        c_pack_ref[at : at + heads, :] = term
        at += heads


def pass_kernel(ahead, chunk, meta, log_ref, near_ref, far_ref, rows_ref, state_ref, sent_ref):
    size, heads = log_ref.shape[1], log_ref.shape[0]
    half = size // 2
    _, _, before, last = documents(meta, size)
    near_row, _, _, _ = documents(meta, size, -1 if ahead else 1)
    far_row, _, _, _ = documents(meta, size, 1 if ahead else -1)
    total = jnp.where(before == last, jnp.exp(running(log_ref)[:, size - 1 :]), 0.0)
    terms = (near_ref.shape[0] - size) // 3
    near_log = jnp.zeros((heads, size), F32)
    for i in range(3):
        at = size + i * terms + chunk * heads
        near_log += near_ref[at : at + heads, :].astype(F32)
    cum = running(near_log)
    if ahead:
        weight = jnp.where(near_row == before, jnp.exp(cum[:, size - 1 :] - cum), 0.0)
        count = jnp.sum((far_row == last).astype(F32), axis=1, keepdims=True)
        rows, wanted = slice(half, size), slice(0, half)
    else:
        weight = jnp.where(near_row == last, jnp.exp(cum), 0.0)
        count = jnp.sum((far_row == before).astype(F32), axis=1, keepdims=True)
        rows, wanted = slice(0, half), slice(half, size)
    few = (count <= half).astype(F32)
    weight_t = weight.T
    near_t = near_ref[:size, :].astype(F32).T
    far = far_ref[wanted, :]
    width = rows_ref.shape[1]
    p = width // heads
    for h in range(heads):
        at = head(h, p)
        state = dot((near_t * weight[h : h + 1, :]).astype(BF16), rows_ref[:, at]).astype(BF16)
        state_ref[:, at] = state
        scale = total[h : h + 1, :]
        sums = dot(far, state) * (few * scale)
        scaled = rows_ref[rows, at].astype(F32) * (weight_t[rows, h : h + 1] * ((1.0 - few) * scale))
        sent_ref[:, at] = (sums + scaled).astype(BF16)
    sent_ref[:, width:] = near_ref[rows, :]


def spread_of(few, shift, mine, theirs):
    size, half = mine.shape[0], theirs.shape[0]
    down = lax.broadcasted_iota(jnp.int32, (size, half), 0)
    along = lax.broadcasted_iota(jnp.int32, (size, half), 1)
    same = (down == along + shift).astype(F32)
    return (few * same + (1.0 - few) * dot_nt(mine, theirs)).astype(BF16)


def carried_in(mine, spread, states, at):
    carried = dot(mine, states[0][:, at])
    if spread is not None:
        return carried + dot(spread, states[1][:, at])
    for state in states[1:]:
        carried += dot(mine, state[:, at])
    return carried


def resid_kernel(relayed, meta, log_ref, c_ref, inner_ref, *refs):
    states, (resid_ref, squares_ref) = refs[:-2], refs[-2:]
    size = log_ref.shape[1]
    row, col, before, _ = documents(meta, size)
    weight = jnp.where(col == before, jnp.exp(running(log_ref).T), 0.0)
    width = inner_ref.shape[1]
    p = width // log_ref.shape[0]
    spread = None
    if relayed:
        few = (jnp.sum((row == before).astype(F32), axis=1, keepdims=True) <= size // 2).astype(F32)
        spread = spread_of(few, 0, c_ref[...], states[2][...])
    squares = jnp.zeros((size, p), F32)
    for h in range(log_ref.shape[0]):
        carried = carried_in(c_ref[...], spread, states, head(h, p))
        rows = (inner_ref[:, head(h, p)] + weight[:, h : h + 1] * carried).astype(BF16)
        resid_ref[:, head(h, p)] = rows
        squares += rows.astype(F32) * rows.astype(F32)
    squares_ref[...] = jnp.broadcast_to(jnp.sum(squares, axis=1, keepdims=True), squares_ref.shape)


def combined(weights_ref, pieces):
    total = dot(weights_ref[0], pieces[0][...])
    for i, piece in enumerate(pieces[1:]):
        total += dot(weights_ref[i + 1], piece[...])
    return total


def relay_kernel(weights_ref, *refs):
    pieces, out_ref = refs[:-1], refs[-1]
    out_ref[...] = combined(weights_ref, pieces).astype(BF16)


def dresid_kernel(chunks, features, meta, log_ref, c_ref, weights_ref, cot_ref, *refs):
    squares, refs = refs[:chunks], refs[chunks:]
    count = weights_ref.shape[0]
    relayed = weights_ref.shape[0] > 1
    moved_refs, outs = (refs[:-1], refs[-1:]) if relayed else (refs[:-2], refs[-2:])
    dresid_ref = outs[0]
    size = log_ref.shape[1]
    row, _, before, _ = documents(meta, size)
    weight = jnp.where(row == before, jnp.exp(running(log_ref)), 0.0)
    c_t = c_ref[...].astype(F32).T
    total = squares[0][...]
    for part in squares[1:]:
        total = total + part[...]
    scale = lax.rsqrt(total[:, :1] / features + EPSILON)
    moved = combined(weights_ref, moved_refs[:count])
    for arrived in moved_refs[count:]:
        moved += arrived[...].astype(F32)
    dresid_ref[...] = (cot_ref[...].astype(F32) + scale * moved).astype(BF16)
    if relayed:
        return
    p = cot_ref.shape[1] // log_ref.shape[0]
    for h in range(log_ref.shape[0]):
        c_weighted = (c_t * weight[h : h + 1, :]).astype(BF16)
        outs[1][:, head(h, p)] = dot(c_weighted, dresid_ref[:, head(h, p)]).astype(BF16)


def grad_kernel(count, relayed, meta, log_ref, b_ref, inner_ref, *refs):
    states, out_ref = refs[:count], refs[-1]
    size = log_ref.shape[1]
    row, col, _, last = documents(meta, size)
    cum = running(log_ref)
    weight = jnp.where(col == last, jnp.exp(cum[:, size - 1 :] - cum).T, 0.0)
    width = inner_ref.shape[1]
    p = width // log_ref.shape[0]
    spread = None
    if relayed:
        few = (jnp.sum((row == last).astype(F32), axis=1, keepdims=True) <= size // 2).astype(F32)
        spread = spread_of(few, size // 2, b_ref[...], states[2][...])
    for h in range(log_ref.shape[0]):
        carried = carried_in(b_ref[...], spread, states, head(h, p))
        out_ref[:, head(h, p)] = (inner_ref[:, head(h, p)] + weight[:, h : h + 1] * carried).astype(BF16)


def output_kernel(weights_ref, resid_ref, *refs):
    out_ref = refs[-1]
    count = weights_ref.shape[0]
    moved = combined(weights_ref, refs[:count])
    for arrived in refs[count : len(refs) - 1]:
        if arrived.shape == out_ref.shape:
            moved += arrived[...].astype(F32)
    out_ref[...] = (resid_ref[...].astype(F32) + moved).astype(BF16)


def picks_of(table, me, experts, capacity):
    tokens = table.shape[1]
    offset = lax.broadcasted_iota(jnp.int32, (experts, tokens), 0)
    first = (table[0:1, :].astype(jnp.int32) ^ me) == offset
    second = (table[1:2, :].astype(jnp.int32) ^ me) == offset
    named = (first | second).astype(F32)
    gate = jnp.where(first, table[2:3, :], 0.0) + jnp.where(second, table[3:4, :], 0.0)
    before = (
        lax.broadcasted_iota(jnp.int32, (tokens, tokens), 0)
        < lax.broadcasted_iota(jnp.int32, (tokens, tokens), 1)
    ).astype(BF16)
    rank = jnp.where(named > 0, dot(named.astype(BF16), before), -1.0)
    slot = lax.broadcasted_iota(jnp.int32, (capacity, tokens), 0).astype(F32)
    picks = [(rank[e : e + 1, :] == slot).astype(F32) for e in range(experts)]
    return picks, [pick * gate[e : e + 1, :] for e, pick in enumerate(picks)]


def direct_pick_kernel(experts, capacity, table_ref, pick_ref, weights_ref):
    picks, gated = picks_of(table_ref[...], 0, experts, capacity)
    pick_ref[...] = jnp.concatenate(picks, axis=0).astype(BF16)
    weights_ref[0] = jnp.concatenate(gated, axis=0).T.astype(BF16)


def relay_pick_kernel(experts, capacity, kinds, me_ref, own_ref, *refs):
    tables, outs = refs[: len(kinds)], refs[len(kinds) :]
    me = me_ref[0]
    picks, gated = picks_of(own_ref[...].astype(F32).T, me, experts, capacity)
    none = jnp.zeros_like(picks[0])
    for (_, offsets), table_ref, (pick_ref, own_weights_ref, relay_weights_ref) in zip(
        kinds, tables, (outs[:3], outs[3:])
    ):
        other_picks, other_gated = picks_of(table_ref[...].astype(F32).T, me, experts, capacity)
        for i, o in enumerate(offsets):
            pick_ref[i, 0] = picks[o].astype(BF16)
            pick_ref[i, 1] = other_picks[o].astype(BF16)
            own_weights_ref[i] = jnp.concatenate([gated[o], none], axis=0).T.astype(BF16)
            relay_weights_ref[i] = jnp.concatenate([none, other_gated[o]], axis=0).T.astype(BF16)


def side_pick_kernel(experts, capacity, kinds, me_ref, own_ref, sibling_ref, *refs):
    tables, outs = refs[:4], refs[4:]
    mine = [picks_of(t[...].astype(F32).T, me_ref[0], experts, capacity) for t in (own_ref, sibling_ref)]
    for k, (_, partner) in enumerate(kinds):
        near = [picks_of(t[...].astype(F32).T, me_ref[0], experts, capacity) for t in tables[2 * k : 2 * k + 2]]
        pick_ref, gated_ref = outs[2 * k : 2 * k + 2]
        for source, (picks, gated) in enumerate((mine[0], near[0], mine[1], near[1])):
            for e, to in enumerate((0, partner)):
                pick_ref[e, source] = picks[to].astype(BF16)
                gated_ref[e, source] = gated[to]


def side_weights_kernel(*refs):
    for gated_ref, weights_ref in zip(refs[:2], refs[2:]):
        for e in range(2):
            for source in range(4):
                weights_ref[source, e] = gated_ref[e, source].T.astype(BF16)


def side_gather_kernel(*refs):
    picks, rows, outs = refs[:2], (refs[2:6], refs[6:10]), (refs[10:12], refs[12:14])
    capacity = picks[0].shape[2]
    for e in (1, 0):
        for k in range(2):
            for source in range(4):
                at = slice(source * capacity, (source + 1) * capacity)
                outs[k][e][at, :] = dot(picks[k][e, source], rows[k][source][...]).astype(BF16)


def partial(weights_ref, pieces, source):
    slots = weights_ref.shape[3]
    rows = slice(source * slots, (source + 1) * slots)
    total = dot(weights_ref[source, 0], pieces[0][rows, :])
    for e, piece in enumerate(pieces[1:]):
        total += dot(weights_ref[source, e + 1], piece[rows, :])
    return total


def side_sums_kernel(*refs):
    weights, pieces, outs = refs[:2], (refs[2:4], refs[4:6]), refs[6:]
    for i, source in enumerate((3, 2)):
        for k in range(2):
            outs[2 * i + k][...] = partial(weights[k], pieces[k], source).astype(BF16)


def tick_kernel(out_ref):
    out_ref[...] = jnp.zeros_like(out_ref)


def side_relay_kernel(*refs):
    weights, pieces, arrived, outs = refs[:2], (refs[2:4], refs[4:6]), refs[6:8], refs[8:]
    for k in range(2):
        total = partial(weights[k], pieces[k], 1) + arrived[k][...].astype(F32)
        outs[k][...] = total.astype(BF16)


def side_output_kernel(first_weights, second_weights, first_resid, second_resid, *refs):
    out_ref, refs = refs[-1], refs[:-1]
    count, width = len(refs) // 2, first_resid.shape[1]
    for k, (weights, resid) in enumerate(((first_weights, first_resid), (second_weights, second_resid))):
        terms = refs[k * count : (k + 1) * count]
        sums = partial(weights, terms[:2], 0)
        for arrived in terms[2:]:
            sums += arrived[...].astype(F32)
        out_ref[:, k * width : (k + 1) * width] = (resid[...].astype(F32) + sums).astype(BF16)


def hold_kernel(*refs):
    pass


def gather_kernel(pick_ref, own_ref, other_ref, *outs):
    capacity = pick_ref.shape[2]
    for i, out in enumerate(outs):
        out[:capacity, :] = dot(pick_ref[i, 0], own_ref[...]).astype(BF16)
        out[capacity:, :] = dot(pick_ref[i, 1], other_ref[...]).astype(BF16)


def direct_gather_kernel(pick_ref, own_ref, out_ref):
    out_ref[...] = dot(pick_ref[...], own_ref[...]).astype(BF16)


def assemble(plan, pieces, rows):
    for piece, at, to, count in plan:
        rows[to : to + count, :] = pieces[piece][at : at + count, :]


def back_kernel(plans, *refs):
    counts = [max(b[0] for b in plan) + 1 for plan in plans]
    pieces, (down_ref, back_ref, rows) = refs[: sum(counts)], refs[sum(counts) :]
    step, each = pl.program_id(0), pl.num_programs(0) // len(plans)
    for k, plan in enumerate(plans):
        mine = pieces[sum(counts[:k]) : sum(counts[: k + 1])]

        @pl.when(step // each == k)
        def _(plan=plan, mine=mine):
            assemble(plan, mine, rows)

    part = dot_nt(rows[...], down_ref[...])

    @pl.when(step == 0)
    def _():
        back_ref[...] = part

    @pl.when(step > 0)
    def _():
        back_ref[...] += part


def up_first_kernel(plan, *refs):
    pieces, (up_ref, total_ref, squares_ref, rows) = refs[:-4], refs[-4:]
    assemble(plan, pieces, rows)
    part = dot(rows[...], up_ref[...])
    values = rows[...].astype(F32)
    square = jnp.broadcast_to(jnp.sum(values * values, axis=1, keepdims=True), squares_ref.shape)

    @pl.when(pl.program_id(0) == 0)
    def _():
        total_ref[...] = part
        squares_ref[...] = square

    @pl.when(pl.program_id(0) > 0)
    def _():
        total_ref[...] += part
        squares_ref[...] += square


def up_last_kernel(plan, features, *refs):
    count = max(b[0] for b in plan) + 1
    pieces = refs[:count]
    up_ref, before_ref, before_squares_ref, back_ref, act_ref, pre_grad_ref, along_ref, total, squares, rows = refs[count:]
    step, steps = pl.program_id(0), pl.num_programs(0)
    assemble(plan, pieces, rows)
    part = dot(rows[...], up_ref[...])
    values = rows[...].astype(F32)
    square = jnp.broadcast_to(jnp.sum(values * values, axis=1, keepdims=True), squares.shape)

    @pl.when(step == 0)
    def _():
        total[...] = before_ref[...] + part
        squares[...] = before_squares_ref[...] + square

    @pl.when(step > 0)
    def _():
        total[...] += part
        squares[...] += square

    @pl.when(step == steps - 1)
    def _():
        scale = lax.rsqrt(squares[:, :1] / features + EPSILON)
        pre = total[...] * scale
        gate = jax.nn.sigmoid(pre)
        act_ref[...] = (pre * gate).astype(BF16)
        pre_grad = (back_ref[...] * gate * (1.0 + pre * (1.0 - gate))).astype(BF16)
        pre_grad_ref[...] = pre_grad
        along = jnp.sum(pre_grad.astype(F32) * pre, axis=1, keepdims=True)
        along_ref[...] = jnp.broadcast_to(scale * along / features, along_ref.shape)


def expert_grad_kernel(plan, pre_grad_ref, up_ref, along_ref, *refs):
    count = len(refs) // 2
    total = dot_nt(pre_grad_ref[...], up_ref[...])
    for piece, at, to, size in plan:
        rows = refs[piece][at : at + size, :].astype(F32)
        refs[count + piece][at : at + size, :] = (
            total[to : to + size, :] - rows * along_ref[to : to + size, :1]
        ).astype(BF16)


def expert_out_kernel(plan, act_ref, down_ref, *outs):
    total = dot(act_ref[...], down_ref[...])
    for piece, at, to, size in plan:
        outs[piece][at : at + size, :] = total[to : to + size, :].astype(BF16)


def on_device(inputs, b_proj, c_proj, log_decay, doc_lengths, expert_ids, gate_weights, w_up, w_down, cotangent):
    tokens, features = inputs.shape[1:]
    heads = log_decay.shape[1]
    state = b_proj.shape[2]
    experts, blocks = lax.axis_size("exp"), lax.axis_size("seq")
    hidden = w_up.shape[2]
    capacity = 3 * tokens // experts
    slots = experts * capacity
    width = features // CHUNKS
    hops = max(1, blocks // 2)
    relayed = experts == 8 and hops == 2
    kinds = ((2, (0, 1, 4, 5)), (4, (0, 1, 2, 3)))

    x, b, c, log, cot = inputs[0], b_proj[0], c_proj[0], log_decay[0], cotangent[0]
    up, down = w_up[0], w_down[0]
    meta = jnp.concatenate([doc_lengths[0], (lax.axis_index("seq") * tokens)[None].astype(jnp.int32)])

    def log_spec(k):
        return pl.BlockSpec((heads // CHUNKS, tokens), lambda i: (k, 0))

    def chunk(k, rows=tokens):
        return pl.BlockSpec((rows, width), lambda i: (0, k))

    def shape(rows, columns, kind=BF16):
        return jax.ShapeDtypeStruct((rows, columns), kind)

    small, part = whole((tokens, state)), whole((tokens, width))
    unit = tokens * width
    head_flops = 2 * tokens * unit

    def offset(a, k):
        return lax.ppermute(a, "exp", [(i, i ^ k) for i in range(experts)])

    def hop(states, step):
        return lax.ppermute(states, "seq", [(i, i + step) for i in range(blocks) if 0 <= i + step < blocks])

    def hop_on(arrived, spec, step, k, after):
        if relayed:
            near, far = (b_pack, c_pack) if step > 0 else (c_pack, b_pack)
            wide = arrived.shape[1]
            taken, sent = call(
                functools.partial(pass_kernel, step > 0, k),
                (1,),
                [SMEM, whole((heads, tokens)) if wide == features else log_spec(k), whole(near.shape), small, spec],
                [whole((tokens, wide)), whole((tokens // 2, wide + state))],
                [shape(tokens, wide), shape(tokens // 2, wide + state)],
                2 * head_flops,
                5 * unit,
                "pass_states",
                after=after,
            )(meta, log, near, far, arrived)
            passed = hop(sent, step)
            return [taken, passed, passed], sent
        arrived = [arrived]
        for _ in range(hops - 1):
            kept = call(
                keep_kernel,
                (1,),
                [SMEM, log_spec(k), part],
                part,
                shape(tokens, width),
                unit,
                4 * unit,
                "keep_states",
                after=after,
            )(meta, log, arrived[-1])
            arrived = arrived + [hop(kept, step)]
        return arrived, kept

    if relayed:
        moving = hop(x, 1)
        pack = (tokens + 3 * heads, state)
        b_pack, c_pack, *cots, cot_both = call(
            prepare_kernel,
            (1,),
            [small, small, whole((heads, tokens)), whole((tokens, features)), whole((2, tokens)), whole((2, tokens))],
            [whole(pack)] * 2 + [whole((tokens, width + 128))] * CHUNKS + [whole((2 * tokens, width + 128))],
            [shape(*pack)] * 2 + [shape(tokens, width + 128)] * CHUNKS + [shape(2 * tokens, width + 128)],
            0,
            4 * tokens * features,
            "prepare",
            vmem=VMEM_ALL,
        )(b, c, log, cot, expert_ids[0].T, gate_weights[0].T)
        b_pack, c_pack = hop(b_pack, 1), hop(c_pack, -1)
    else:
        moving = []
        for k in range(CHUNKS):
            local = call(
                local_kernel,
                (1,),
                [SMEM, log_spec(k), small, chunk(k)],
                part,
                shape(tokens, width),
                head_flops,
                4 * unit,
                "local_states",
            )(meta, log, b, x)
            moving.append(hop(local, 1))
        cots = [cot[:, k * width : (k + 1) * width] for k in range(CHUNKS)]

    def tick(arrived):
        mark = call(
            tick_kernel, (1,), [], whole((16, 128)), shape(16, 128), 0, 0, "tick", after=[arrived]
        )()
        return offset(mark, 1)

    if relayed:
        plans = [
            [
                block
                for i, o in enumerate(offsets)
                for block in ((i, 0, o * capacity, capacity), (i, capacity, (o ^ by) * capacity, capacity))
            ]
            for by, offsets in kinds
        ]
        pieces_of = [[2 * capacity] * 4] * 2
        pick_shape = (4, 2, capacity, tokens)
        weight_shape = (4, tokens, 2 * capacity)
        outs = [pick_shape, weight_shape, weight_shape] * 2
        me = lax.axis_index("exp").astype(jnp.int32)[None]
        other_cots = [offset(rows, by) for rows, (by, _) in zip(cots, kinds)]
        found = call(
            functools.partial(relay_pick_kernel, experts, capacity, kinds),
            (1,),
            [SMEM] + [pl.BlockSpec((tokens, 128), lambda i: (0, width // 128))] * 3,
            [whole(s) for s in outs],
            [jax.ShapeDtypeStruct(s, BF16) for s in outs],
            6 * experts * tokens * tokens,
            4 * slots * tokens,
            "pick_rows",
        )(me, cots[0], *other_cots)
        picks, own_weights, relay_weights = found[0::3], found[1::3], found[2::3]
    else:
        table = jnp.concatenate([expert_ids[0].T.astype(F32), gate_weights[0].T], axis=0)
        other_cots = [None] * CHUNKS
        plans = [[(0, 0, 0, slots)]] * 2
        pieces_of = [[slots]] * 2
        pick, weights = call(
            functools.partial(direct_pick_kernel, experts, capacity),
            (1,),
            [whole((4, tokens))],
            [whole((slots, tokens)), whole((1, tokens, slots))],
            [shape(slots, tokens), jax.ShapeDtypeStruct((1, tokens, slots), BF16)],
            2 * experts * tokens * tokens,
            4 * slots * tokens,
            "pick_rows",
        )(table)
        picks, own_weights = [pick] * 2, [weights] * 2

    def piece_specs(kind):
        return [whole((rows, width)) for rows in pieces_of[kind]]

    def piece_shapes(kind):
        return [shape(rows, width) for rows in pieces_of[kind]]

    def switch(pieces):
        parts = pieces[0].reshape(experts, capacity, width)
        return [lax.all_to_all(parts, "exp", split_axis=0, concat_axis=0, tiled=True).reshape(slots, width)]

    def to_experts(rows, k, other, after=()):
        kind = k % 2
        cost = (2 * slots * unit, 2 * (unit + slots * width))
        if not relayed:
            sent = call(
                direct_gather_kernel,
                (1,),
                [whole((slots, tokens)), part],
                piece_specs(kind),
                piece_shapes(kind),
                *cost,
                "gather",
                after=after,
            )(picks[kind], rows)
            return sent, switch(sent)
        _, offsets = kinds[kind]
        sent = call(
            gather_kernel,
            (1,),
            [whole(picks[kind].shape), part, part],
            piece_specs(kind),
            piece_shapes(kind),
            *cost,
            "gather",
            after=after,
        )(picks[kind], rows, other)
        return sent, [piece if o == 0 else offset(piece, o) for piece, o in zip(sent, offsets)]

    def other_of(rows, k):
        return offset(rows, kinds[k % 2][0]) if relayed else None

    def to_positions(pieces, k, after=()):
        kind = k % 2
        if not relayed:
            arrived = switch(pieces)
            return arrived[0], arrived
        by, offsets = kinds[kind]
        pieces = [piece if o == 0 else offset(piece, o) for piece, o in zip(pieces, offsets)]
        relay = call(
            relay_kernel,
            (1,),
            [whole(relay_weights[kind].shape)] + piece_specs(kind),
            part,
            shape(tokens, width),
            2 * slots * unit,
            2 * (unit + slots * width),
            "relay",
            after=after,
        )(relay_weights[kind], *pieces)
        return relay, pieces + [offset(relay, by)]

    def moved_specs(kind):
        return piece_specs(kind) + ([part] if relayed else [])

    inner = call(
        inner_kernel,
        (CHUNKS,),
        [SMEM, pl.BlockSpec((heads // CHUNKS, tokens), lambda i: (i, 0)), small, small, columns(tokens, width)],
        columns(tokens, width),
        shape(tokens, features, F32),
        2 * CHUNKS * head_flops,
        6 * CHUNKS * unit,
        "inner",
    )(meta, log, b, c, x)
    if relayed:
        first_in, kept = hop_on(moving, whole((tokens, features)), 1, 0, [inner, picks[0]])
        second_in = first_in
    else:
        first_in, kept = hop_on(moving[0], part, 1, 0, [inner, picks[0]])
    if relayed:
        held = call(
            hold_kernel,
            (1,),
            [anywhere] * 3,
            [anywhere] * 3,
            [shape(tokens, width + 128)] * 2 + [shape(2 * tokens, width + 128)],
            0,
            0,
            "hold",
            after=[moving, inner, b_pack, c_pack],
            aliases={0: 0, 1: 1, 2: 2},
        )(*other_cots, cot_both)
        cot_sibling = offset(held[2], 1)
        side_others = [offset(rows, 1) for rows in held[:2]]
        table_spec = pl.BlockSpec((tokens, 128), lambda i: (0, width // 128))
        side_kinds = ((2, 4), (4, 2))
        side_plans = [
            [
                (e, j * capacity, (to ^ source) * capacity, capacity)
                for e, to in enumerate((0, partner))
                for j, source in enumerate((0, by, 1, by ^ 1))
            ]
            for by, partner in side_kinds
        ]
        side_shape, side_weight_shape = (2, 4, capacity, tokens), (4, 2, tokens, capacity)
        found = call(
            functools.partial(side_pick_kernel, experts, capacity, side_kinds),
            (1,),
            [SMEM] + [table_spec] * 6,
            [whole(side_shape)] * 4,
            [jax.ShapeDtypeStruct(side_shape, kind) for kind in (BF16, F32)] * 2,
            12 * experts * tokens * tokens,
            8 * slots * tokens,
            "side_picks",
        )(me, cots[0], cot_sibling, held[0], side_others[0], held[1], side_others[1])
        side_picks, side_gated = found[0::2], found[1::2]
        side_spec = whole((4 * capacity, width))
        both = [pl.BlockSpec((tokens, width), lambda i, k=k: (k, 0)) for k in range(2)]
        sent = call(
            side_gather_kernel,
            (1,),
            [whole(side_shape)] * 2 + [spec for k in range(2) for spec in (part, part, both[k], part)],
            [side_spec] * 4,
            [shape(4 * capacity, width)] * 4,
            4 * slots * unit,
            8 * slots * width,
            "side_gather",
            after=[kept],
        )(*side_picks, *[r for k in range(2) for r in (cots[k], held[k], cot_sibling, side_others[k])])
        got_cot = [[sent[2 * k], offset(sent[2 * k + 1], side_kinds[k][1])] for k in range(2)]
        sent = sent[1]
        early = [[], [pieces[1] for pieces in got_cot]]
    else:
        got_cot, sent, early = [], kept, [[], []]
        for k in range(CHUNKS):
            (sent, *_), pieces = to_experts(cots[k], k, other_cots[k], [sent])
            got_cot.append(pieces)
    if not relayed:
        second_in, _ = hop_on(moving[1], part, 1, 1, [sent])
    states_in = [first_in, second_in]


    def states_specs(k, w):
        if not relayed:
            return [part] * hops
        return [
            chunk(k),
            chunk(k, tokens // 2),
            pl.BlockSpec((tokens // 2, state), lambda i: (0, w // state)),
        ]

    resid, squares, others = [], [], []
    for k in range(CHUNKS):
        rows, square = call(
            functools.partial(resid_kernel, relayed),
            (1,),
            [SMEM, log_spec(k), small, chunk(k)] + states_specs(k, features),
            [part, whole((tokens, 128))],
            [shape(tokens, width), shape(tokens, 128, F32)],
            hops * head_flops,
            (6 + 2 * hops) * unit,
            "resid",
            after=early[k],
        )(meta, log, c, inner, *states_in[k])
        resid.append(rows)
        squares.append(square)
        others.append(other_of(rows, k))

    each = 2
    step = width // each
    chunk_flops = 2 * slots * width * hidden
    chunk_bytes = 2 * width * (hidden + slots)
    slots_hidden = whole((slots, hidden))

    def step_specs(kind, first=0):
        return [
            pl.BlockSpec((rows, step), lambda i: (0, jnp.clip(i - first, 0, each - 1))) for rows in pieces_of[kind]
        ]

    if relayed:
        cot_plans = side_plans
        cot_specs = [
            pl.BlockSpec((4 * capacity, step), lambda i, k=k: (0, jnp.clip(i - each * k, 0, each - 1)))
            for k in range(CHUNKS)
            for _ in range(2)
        ]
    else:
        cot_plans = [plans[k % 2] for k in range(CHUNKS)]
        cot_specs = [spec for k in range(CHUNKS) for spec in step_specs(k % 2, each * k)]
    back = call(
        functools.partial(back_kernel, cot_plans),
        (each * CHUNKS,),
        cot_specs + [columns(hidden, step)],
        slots_hidden,
        shape(slots, hidden, F32),
        CHUNKS * chunk_flops,
        CHUNKS * chunk_bytes,
        "back",
        [pltpu.VMEM((slots, step), BF16)],
        after=[resid[1]],
    )(*[piece for pieces in got_cot for piece in pieces], down)
    (sent, *_), pieces = to_experts(resid[0], 0, others[0], [back])
    got_in = [pieces]
    _, pieces = to_experts(resid[1], 1, others[1], [sent])
    got_in.append(pieces)

    def up_spec(k):
        return pl.BlockSpec((step, hidden), lambda i: (each * k + i, 0))

    slots_small = whole((slots, 128))
    total, total_squares = call(
        functools.partial(up_first_kernel, plans[0]),
        (each,),
        step_specs(0) + [up_spec(0)],
        [slots_hidden, slots_small],
        [shape(slots, hidden, F32), shape(slots, 128, F32)],
        chunk_flops,
        chunk_bytes,
        "up_first",
        [pltpu.VMEM((slots, step), BF16)],
    )(*got_in[0], up)
    act, pre_grad, along = call(
        functools.partial(up_last_kernel, plans[1], features),
        (each,),
        step_specs(1) + [up_spec(1), slots_hidden, slots_small, slots_hidden],
        [slots_hidden, slots_hidden, slots_small],
        [shape(slots, hidden), shape(slots, hidden), shape(slots, 128, F32)],
        chunk_flops,
        chunk_bytes,
        "up_last",
        [pltpu.VMEM((slots, hidden), F32), pltpu.VMEM((slots, 128), F32), pltpu.VMEM((slots, step), BF16)],
    )(*got_in[1], up, total, total_squares, back)

    got_grad, grads, last = [], [], []
    for k in range(CHUNKS):
        kind = k % 2
        expert_grad = call(
            functools.partial(expert_grad_kernel, plans[kind]),
            (each,),
            [slots_hidden, up_spec(k), slots_small] + step_specs(kind),
            step_specs(kind),
            piece_shapes(kind),
            chunk_flops,
            chunk_bytes,
            "expert_grad",
            after=last,
        )(pre_grad, up, along, *got_in[k])
        last = expert_grad[:1]
        grads.append(expert_grad)
    outs = []
    for k in range(CHUNKS):
        kind = k % 2
        expert_out = call(
            functools.partial(expert_out_kernel, side_plans[k] if relayed else plans[kind]),
            (each,),
            [slots_hidden, pl.BlockSpec((hidden, step), lambda i, k=k: (0, each * k + i))],
            [pl.BlockSpec((4 * capacity, step), lambda i: (0, i))] * 2 if relayed else step_specs(kind),
            [shape(4 * capacity, width)] * 2 if relayed else piece_shapes(kind),
            chunk_flops,
            chunk_bytes,
            "expert_out",
            after=last,
        )(act, down)
        outs.append(expert_out)
        last = expert_out[:1]

    for k in range(CHUNKS):
        relay, pieces = to_positions(grads[k], k, last)
        got_grad.append(pieces)
        last = [relay]
    last = relay

    def weights_spec(kind):
        return whole(own_weights[kind].shape)

    dresid, states_after = [], []
    for k in range(CHUNKS):
        kind = k % 2
        grads_here = call(
            functools.partial(dresid_kernel, CHUNKS, features),
            (1,),
            [SMEM, log_spec(k), small, weights_spec(kind), chunk(k)]
            + [whole((tokens, 128))] * CHUNKS
            + moved_specs(kind),
            [part] * (1 if relayed else 2),
            [shape(tokens, width)] * (1 if relayed else 2),
            head_flops + 2 * slots * unit,
            6 * unit + 2 * slots * width,
            "dresid",
            after=[last],
        )(meta, log, c, own_weights[kind], cot, *squares, *got_grad[k])
        dresid.append(grads_here[0])
        states_after.append(hop(grads_here[-1], -1))
        last = dresid[k]

    if relayed:
        states_after[0], last = hop_on(states_after[0], part, -1, 0, [last])
    inner_back = []
    for k in range(CHUNKS):
        last = call(
            inner_back_kernel,
            (1,),
            [SMEM, log_spec(k), small, small, part],
            part,
            shape(tokens, width, F32),
            2 * head_flops,
            6 * unit,
            "inner_back",
            after=[last],
        )(meta, log, b, c, dresid[k])
        inner_back.append(last)
    got_out = []
    if relayed:
        held = call(
            hold_kernel,
            (1,),
            [anywhere] * 2,
            [anywhere] * 2,
            [shape(4 * capacity, width)] * 2,
            0,
            0,
            "hold",
            after=[dresid[1]],
            aliases={0: 0, 1: 1},
        )(outs[0][1], outs[1][1])
        side_weights = call(
            side_weights_kernel,
            (1,),
            [whole(side_shape)] * 2,
            [whole(side_weight_shape)] * 2,
            [jax.ShapeDtypeStruct(side_weight_shape, BF16)] * 2,
            0,
            16 * slots * tokens,
            "side_weights",
            after=outs[0][:1],
        )(*side_gated)
        out_pieces = [[outs[k][0], offset(held[k], side_kinds[k][1])] for k in range(2)]
        operands = [*side_weights, *out_pieces[0], *out_pieces[1]]
        specs = [whole(side_weight_shape)] * 2 + [side_spec] * 4
        sums = call(
            side_sums_kernel,
            (1,),
            specs,
            [part] * 4,
            [shape(tokens, width)] * 4,
            4 * slots * unit,
            8 * slots * width,
            "side_sums",
            after=[last],
        )(*operands)
        sums_here = [offset(rows, 1) for rows in sums]
        states_after[1], last = hop_on(states_after[1], part, -1, 1, [sums[0]])
        sent = call(
            side_relay_kernel,
            (1,),
            specs + [part] * 2,
            [part] * 2,
            [shape(tokens, width)] * 2,
            4 * slots * unit,
            8 * slots * width,
            "side_relay",
            after=[last],
        )(*operands, *sums_here[:2])
        last = sent[0]
        relayed_sums = [offset(sent[k], side_kinds[k][0]) for k in range(2)]
    else:
        for k in range(CHUNKS):
            states_after[k], last = hop_on(states_after[k], part, -1, k, [last])
            last, pieces = to_positions(outs[k], k, [last])
            got_out.append(pieces)

    def placed(kernel, k, in_specs, operands, earlier, after, flops, nbytes, name):
        more = [] if earlier is None else [earlier]
        return call(
            kernel,
            (1,),
            in_specs + [pl.BlockSpec(memory_space=pl.ANY)] * len(more),
            chunk(k),
            shape(tokens, features),
            flops,
            nbytes,
            name,
            after=after,
            aliases={len(operands): 0} if more else {},
        )(*operands, *more)

    def input_grads(k, earlier, after):
        return placed(
            functools.partial(grad_kernel, 3 if relayed else hops, relayed),
            k,
            [SMEM, log_spec(k), small, part] + states_specs(0, width),
            [meta, log, b, inner_back[k], *states_after[k]],
            earlier,
            after,
            hops * head_flops,
            (6 + 2 * hops) * unit,
            "input_grad",
        )

    input_grad, output = input_grads(0, None, [last]), None
    if relayed:
        input_grad = input_grads(1, input_grad, [])
    if relayed:
        output = call(
            side_output_kernel,
            (1,),
            [whole(side_weight_shape)] * 2
            + [part] * 2
            + [spec for k in range(2) for spec in (side_spec, side_spec, part, part)],
            whole((tokens, features)),
            shape(tokens, features),
            2 * slots * unit,
            8 * unit + 4 * slots * width,
            "output",
            after=[input_grad],
        )(*side_weights, *resid, *[r for k in range(2) for r in (*out_pieces[k], sums_here[2 + k], relayed_sums[k])])
    else:
        for k in range(CHUNKS):
            kind = k % 2
            output = placed(
                output_kernel,
                k,
                [weights_spec(kind), part] + moved_specs(kind),
                [own_weights[kind], resid[k], *got_out[k]],
                output,
                [input_grad] if output is None else [],
                2 * slots * unit,
                4 * unit + 2 * slots * width,
                "output",
            )
    if not relayed:
        input_grad = input_grads(1, input_grad, [output])
    return (output[None], input_grad[None])


def solution(mesh):
    placed = (
        P("exp", "seq", None),
        P("exp", "seq", None),
        P("exp", "seq", None),
        P("exp", None, "seq"),
        P("exp", None),
        P("exp", "seq", None),
        P("exp", "seq", None),
        P("exp", None, None),
        P("exp", None, None),
        P("exp", "seq", None),
    )
    return jax.shard_map(
        on_device,
        mesh=mesh,
        in_specs=placed,
        out_specs=(P("exp", "seq", None), P("exp", "seq", None)),
        check_vma=False,
    )
```

```python
import functools

import jax
import jax.numpy as jnp
from jax import lax
from jax.experimental import pallas as pl
from jax.experimental.pallas import tpu as pltpu
from jax.sharding import PartitionSpec as P

EPSILON = 1e-06
F32 = jnp.float32
BF16 = jnp.bfloat16
CHUNKS = 2
VMEM_BYTES = 32 * 1024 * 1024
VMEM_ALL = 60 * 1024 * 1024
NT = (((1,), (1,)), ((), ()))


def dot(a, b):
    return jnp.dot(a, b, preferred_element_type=F32)


def dot_nt(a, b):
    return lax.dot_general(a, b, NT, preferred_element_type=F32)


def call(kernel, grid, in_specs, out_specs, out_shape, flops, nbytes, name, scratch=(), after=(), aliases=None, vmem=VMEM_BYTES):
    count, more = len(in_specs), len(after)

    def body(*refs):
        kernel(*refs[:count], *refs[count + more :])

    called = pl.pallas_call(
        body,
        grid=grid,
        in_specs=list(in_specs) + [pl.BlockSpec(memory_space=pl.ANY)] * more,
        out_specs=out_specs,
        out_shape=out_shape,
        scratch_shapes=scratch,
        input_output_aliases=aliases or {},
        name=name,
        cost_estimate=pl.CostEstimate(flops=flops, bytes_accessed=nbytes, transcendentals=0),
        compiler_params=pltpu.CompilerParams(vmem_limit_bytes=vmem),
    )
    return lambda *operands: called(*operands, *after)


def whole(shape):
    return pl.BlockSpec(shape, lambda i: (0,) * len(shape))


def columns(rows, width):
    return pl.BlockSpec((rows, width), lambda i: (0, i))


anywhere = pl.BlockSpec(memory_space=pl.ANY)
SMEM = pl.BlockSpec(memory_space=pltpu.SMEM)


def documents(meta, size, shift=0):
    count = meta.shape[0] - 1
    first = meta[count] + shift * size
    along = first + lax.broadcasted_iota(jnp.int32, (1, size), 1)
    down = first + lax.broadcasted_iota(jnp.int32, (size, 1), 0)
    row = jnp.full((1, size), -1, jnp.int32)
    col = jnp.full((size, 1), -1, jnp.int32)
    before, last, start = jnp.int32(-1), jnp.int32(-1), jnp.int32(0)
    for i in range(count):
        row += (start <= along).astype(jnp.int32)
        col += (start <= down).astype(jnp.int32)
        before += (start <= first - 1).astype(jnp.int32)
        last += (start <= first + size - 1).astype(jnp.int32)
        start = start + meta[i]
    return row, col, before, last


def running(log_ref):
    size = log_ref.shape[1]
    upto = (
        lax.broadcasted_iota(jnp.int32, (size, size), 0)
        <= lax.broadcasted_iota(jnp.int32, (size, size), 1)
    ).astype(F32)
    return jnp.dot(
        log_ref[...], upto, precision=lax.Precision.HIGHEST, preferred_element_type=F32
    )


def head(h, size):
    return slice(h * size, (h + 1) * size)


def local_kernel(meta, log_ref, b_ref, x_ref, state_ref):
    size = log_ref.shape[1]
    cum = running(log_ref)
    row, _, _, last = documents(meta, size)
    tail = (row == last).astype(F32)
    weight = tail * jnp.exp(cum[:, size - 1 :] - cum)
    b_t = b_ref[...].astype(F32).T
    p = x_ref.shape[1] // cum.shape[0]
    for h in range(cum.shape[0]):
        b_weighted = (b_t * weight[h : h + 1, :]).astype(BF16)
        state_ref[:, head(h, p)] = dot(b_weighted, x_ref[:, head(h, p)]).astype(BF16)


def pair_mask(meta, size):
    row, col, before, last = documents(meta, size)
    later = lax.broadcasted_iota(jnp.int32, (size, size), 0)
    earlier = lax.broadcasted_iota(jnp.int32, (size, size), 1)
    return row, col, before, last, later, earlier


def inner_kernel(meta, log_ref, b_ref, c_ref, x_ref, out_ref):
    size = log_ref.shape[1]
    cum = running(log_ref)
    cum_t = cum.T
    row, col, _, _, down, along = pair_mask(meta, size)
    scores = jnp.where((row == col) & (down >= along), dot_nt(c_ref[...], b_ref[...]), 0.0)
    p = x_ref.shape[1] // cum.shape[0]
    for h in range(cum.shape[0]):
        spread = cum_t[:, h : h + 1] - cum[h : h + 1, :]
        pair = (jnp.exp(jnp.minimum(spread, 0.0)) * scores).astype(BF16)
        out_ref[:, head(h, p)] = dot(pair, x_ref[:, head(h, p)])


def inner_back_kernel(meta, log_ref, b_ref, c_ref, grad_ref, out_ref):
    size = log_ref.shape[1]
    cum = running(log_ref)
    cum_t = cum.T
    row, col, _, _, down, along = pair_mask(meta, size)
    scores = jnp.where((row == col) & (down <= along), dot_nt(b_ref[...], c_ref[...]), 0.0)
    p = grad_ref.shape[1] // cum.shape[0]
    for h in range(cum.shape[0]):
        spread = cum[h : h + 1, :] - cum_t[:, h : h + 1]
        pair = (jnp.exp(jnp.minimum(spread, 0.0)) * scores).astype(BF16)
        out_ref[:, head(h, p)] = dot(pair, grad_ref[:, head(h, p)])


def keep_kernel(meta, log_ref, state_ref, out_ref):
    size = log_ref.shape[1]
    total = jnp.exp(running(log_ref)[:, size - 1 :])
    _, _, before, last = documents(meta, size)
    total = jnp.where(before == last, total, 0.0)
    p = state_ref.shape[1] // total.shape[0]
    for h in range(total.shape[0]):
        out_ref[:, head(h, p)] = (
            state_ref[:, head(h, p)].astype(F32) * total[h : h + 1, :]
        ).astype(BF16)


def prepare_kernel(b_ref, c_ref, log_ref, cot_ref, ids_ref, gates_ref, b_pack_ref, c_pack_ref, *chunks):
    chunks, both = chunks[:-1], chunks[-1]
    size = ids_ref.shape[1]
    width = chunks[0].shape[1] - size
    table = jnp.concatenate([ids_ref[...].astype(F32), gates_ref[...], jnp.zeros((size - 4, size), F32)], axis=0)
    table = table.T.astype(BF16)
    for k, chunk in enumerate(chunks):
        for ref, to in ((chunk, 0), (both, k * size)):
            ref[to : to + size, :width] = cot_ref[:, k * width : (k + 1) * width]
            ref[to : to + size, width:] = table
    rest, heads, at = log_ref[...], log_ref.shape[0], b_ref.shape[0]
    b_pack_ref[:at, :] = b_ref[...]
    c_pack_ref[:at, :] = c_ref[...]
    for _ in range(3):
        term = rest.astype(BF16)
        rest = rest - term.astype(F32)
        b_pack_ref[at : at + heads, :] = term
        c_pack_ref[at : at + heads, :] = term
        at += heads


def pass_kernel(ahead, chunk, meta, log_ref, near_ref, far_ref, rows_ref, state_ref, *sent_refs):
    size, heads = log_ref.shape[1], log_ref.shape[0]
    half = size // 2
    _, _, before, last = documents(meta, size)
    near_row, _, _, _ = documents(meta, size, -1 if ahead else 1)
    far_row, _, _, _ = documents(meta, size, 1 if ahead else -1)
    total = jnp.where(before == last, jnp.exp(running(log_ref)[:, size - 1 :]), 0.0)
    terms = (near_ref.shape[0] - size) // 3
    near_log = jnp.zeros((heads, size), F32)
    for i in range(3):
        at = size + i * terms + chunk * heads
        near_log += near_ref[at : at + heads, :].astype(F32)
    cum = running(near_log)
    if ahead:
        weight = jnp.where(near_row == before, jnp.exp(cum[:, size - 1 :] - cum), 0.0)
        count = jnp.sum((far_row == last).astype(F32), axis=1, keepdims=True)
        rows, wanted = slice(half, size), slice(0, half)
    else:
        weight = jnp.where(near_row == last, jnp.exp(cum), 0.0)
        count = jnp.sum((far_row == before).astype(F32), axis=1, keepdims=True)
        rows, wanted = slice(0, half), slice(half, size)
    few = (count <= half).astype(F32)
    weight_t = weight.T
    near_t = near_ref[:size, :].astype(F32).T
    far = far_ref[wanted, :]
    width = rows_ref.shape[1]
    p = width // heads
    for h in range(heads):
        at = head(h, p)
        state = dot((near_t * weight[h : h + 1, :]).astype(BF16), rows_ref[:, at]).astype(BF16)
        state_ref[:, at] = state
        scale = total[h : h + 1, :]
        sums = dot(far, state) * (few * scale)
        scaled = rows_ref[rows, at].astype(F32) * (weight_t[rows, h : h + 1] * ((1.0 - few) * scale))
        sent_ref = sent_refs[h * len(sent_refs) // heads]
        to = head(h % (heads // len(sent_refs)), p)
        sent_ref[:, to] = (sums + scaled).astype(BF16)
    for sent_ref in sent_refs:
        sent_ref[:, width // len(sent_refs) :] = near_ref[rows, :]


def spread_of(few, shift, mine, theirs):
    size, half = mine.shape[0], theirs.shape[0]
    down = lax.broadcasted_iota(jnp.int32, (size, half), 0)
    along = lax.broadcasted_iota(jnp.int32, (size, half), 1)
    same = (down == along + shift).astype(F32)
    return (few * same + (1.0 - few) * dot_nt(mine, theirs)).astype(BF16)


def carried_in(mine, spread, states, at):
    carried = dot(mine, states[0][:, at])
    if spread is not None:
        return carried + dot(spread, states[1][:, at])
    for state in states[1:]:
        carried += dot(mine, state[:, at])
    return carried


def resid_kernel(relayed, meta, log_ref, c_ref, inner_ref, *refs):
    states, (resid_ref, squares_ref) = refs[:-2], refs[-2:]
    size = log_ref.shape[1]
    row, col, before, _ = documents(meta, size)
    weight = jnp.where(col == before, jnp.exp(running(log_ref).T), 0.0)
    width = inner_ref.shape[1]
    p = width // log_ref.shape[0]
    spread = None
    if relayed:
        few = (jnp.sum((row == before).astype(F32), axis=1, keepdims=True) <= size // 2).astype(F32)
        spread = spread_of(few, 0, c_ref[...], states[2][...])
    squares = jnp.zeros((size, p), F32)
    for h in range(log_ref.shape[0]):
        carried = carried_in(c_ref[...], spread, states, head(h, p))
        rows = (inner_ref[:, head(h, p)] + weight[:, h : h + 1] * carried).astype(BF16)
        resid_ref[:, head(h, p)] = rows
        squares += rows.astype(F32) * rows.astype(F32)
    squares_ref[...] = jnp.broadcast_to(jnp.sum(squares, axis=1, keepdims=True), squares_ref.shape)


def combined(weights_ref, pieces):
    total = dot(weights_ref[0], pieces[0][...])
    for i, piece in enumerate(pieces[1:]):
        total += dot(weights_ref[i + 1], piece[...])
    return total


def relay_kernel(weights_ref, *refs):
    pieces, out_ref = refs[:-1], refs[-1]
    out_ref[...] = combined(weights_ref, pieces).astype(BF16)


def dresid_kernel(chunks, features, meta, log_ref, c_ref, weights_ref, cot_ref, *refs):
    squares, refs = refs[:chunks], refs[chunks:]
    count = weights_ref.shape[0]
    relayed = weights_ref.shape[0] > 1
    moved_refs, outs = (refs[:-1], refs[-1:]) if relayed else (refs[:-2], refs[-2:])
    dresid_ref = outs[0]
    size = log_ref.shape[1]
    row, _, before, _ = documents(meta, size)
    weight = jnp.where(row == before, jnp.exp(running(log_ref)), 0.0)
    c_t = c_ref[...].astype(F32).T
    total = squares[0][...]
    for part in squares[1:]:
        total = total + part[...]
    scale = lax.rsqrt(total[:, :1] / features + EPSILON)
    moved = combined(weights_ref, moved_refs[:count])
    for arrived in moved_refs[count:]:
        moved += arrived[...].astype(F32)
    dresid_ref[...] = (cot_ref[...].astype(F32) + scale * moved).astype(BF16)
    if relayed:
        return
    p = cot_ref.shape[1] // log_ref.shape[0]
    for h in range(log_ref.shape[0]):
        c_weighted = (c_t * weight[h : h + 1, :]).astype(BF16)
        outs[1][:, head(h, p)] = dot(c_weighted, dresid_ref[:, head(h, p)]).astype(BF16)


def dresid_all_kernel(features, first_weights, second_weights, cot_ref, *refs):
    squares, refs, dresid_ref = refs[:2], refs[2:-1], refs[-1]
    scale = lax.rsqrt((squares[0][:, :1] + squares[1][:, :1]) / features + EPSILON)
    count, width = len(refs) // 2, cot_ref.shape[1] // 2
    for k, weights in enumerate((first_weights, second_weights)):
        terms = refs[k * count : (k + 1) * count]
        moved = combined(weights, terms[: weights.shape[0]])
        for arrived in terms[weights.shape[0] :]:
            moved += arrived[...].astype(F32)
        at = slice(k * width, (k + 1) * width)
        dresid_ref[:, at] = (cot_ref[:, at].astype(F32) + scale * moved).astype(BF16)


def grad_kernel(count, relayed, meta, log_ref, b_ref, inner_ref, *refs):
    states, out_ref = refs[:count], refs[-1]
    size = log_ref.shape[1]
    row, col, _, last = documents(meta, size)
    cum = running(log_ref)
    weight = jnp.where(col == last, jnp.exp(cum[:, size - 1 :] - cum).T, 0.0)
    width = inner_ref.shape[1]
    p = width // log_ref.shape[0]
    spread = None
    if relayed:
        few = (jnp.sum((row == last).astype(F32), axis=1, keepdims=True) <= size // 2).astype(F32)
        spread = spread_of(few, size // 2, b_ref[...], states[2][...])
    for h in range(log_ref.shape[0]):
        carried = carried_in(b_ref[...], spread, states, head(h, p))
        out_ref[:, head(h, p)] = (inner_ref[:, head(h, p)] + weight[:, h : h + 1] * carried).astype(BF16)


def output_kernel(weights_ref, resid_ref, *refs):
    out_ref = refs[-1]
    count = weights_ref.shape[0]
    moved = combined(weights_ref, refs[:count])
    for arrived in refs[count : len(refs) - 1]:
        if arrived.shape == out_ref.shape:
            moved += arrived[...].astype(F32)
    out_ref[...] = (resid_ref[...].astype(F32) + moved).astype(BF16)


def picks_of(table, me, experts, capacity):
    tokens = table.shape[1]
    offset = lax.broadcasted_iota(jnp.int32, (experts, tokens), 0)
    first = (table[0:1, :].astype(jnp.int32) ^ me) == offset
    second = (table[1:2, :].astype(jnp.int32) ^ me) == offset
    named = (first | second).astype(F32)
    gate = jnp.where(first, table[2:3, :], 0.0) + jnp.where(second, table[3:4, :], 0.0)
    before = (
        lax.broadcasted_iota(jnp.int32, (tokens, tokens), 0)
        < lax.broadcasted_iota(jnp.int32, (tokens, tokens), 1)
    ).astype(BF16)
    rank = jnp.where(named > 0, dot(named.astype(BF16), before), -1.0)
    slot = lax.broadcasted_iota(jnp.int32, (capacity, tokens), 0).astype(F32)
    picks = [(rank[e : e + 1, :] == slot).astype(F32) for e in range(experts)]
    return picks, [pick * gate[e : e + 1, :] for e, pick in enumerate(picks)]


def direct_pick_kernel(experts, capacity, table_ref, pick_ref, weights_ref):
    picks, gated = picks_of(table_ref[...], 0, experts, capacity)
    pick_ref[...] = jnp.concatenate(picks, axis=0).astype(BF16)
    weights_ref[0] = jnp.concatenate(gated, axis=0).T.astype(BF16)


def relay_pick_kernel(experts, capacity, kinds, me_ref, own_ref, *refs):
    tables, outs = refs[: len(kinds)], refs[len(kinds) :]
    me = me_ref[0]
    picks, gated = picks_of(own_ref[...].astype(F32).T, me, experts, capacity)
    none = jnp.zeros_like(picks[0])
    for (_, offsets), table_ref, (pick_ref, own_weights_ref, relay_weights_ref) in zip(
        kinds, tables, (outs[:3], outs[3:])
    ):
        other_picks, other_gated = picks_of(table_ref[...].astype(F32).T, me, experts, capacity)
        for i, o in enumerate(offsets):
            pick_ref[i, 0] = picks[o].astype(BF16)
            pick_ref[i, 1] = other_picks[o].astype(BF16)
            own_weights_ref[i] = jnp.concatenate([gated[o], none], axis=0).T.astype(BF16)
            relay_weights_ref[i] = jnp.concatenate([none, other_gated[o]], axis=0).T.astype(BF16)


def side_pick_kernel(experts, capacity, kinds, me_ref, own_ref, sibling_ref, *refs):
    tables, outs = refs[:4], refs[4:]
    mine = [picks_of(t[...].astype(F32).T, me_ref[0], experts, capacity) for t in (own_ref, sibling_ref)]
    for k, (_, partner) in enumerate(kinds):
        near = [picks_of(t[...].astype(F32).T, me_ref[0], experts, capacity) for t in tables[2 * k : 2 * k + 2]]
        pick_ref, gated_ref = outs[2 * k : 2 * k + 2]
        for source, (picks, gated) in enumerate((mine[0], near[0], mine[1], near[1])):
            for e, to in enumerate((0, partner)):
                pick_ref[e, source] = picks[to].astype(BF16)
                gated_ref[e, source] = gated[to]


def side_weights_kernel(*refs):
    for gated_ref, weights_ref in zip(refs[:2], refs[2:]):
        for e in range(2):
            for source in range(4):
                weights_ref[source, e] = gated_ref[e, source].T.astype(BF16)


def side_gather_kernel(*refs):
    picks, rows, outs = refs[:2], (refs[2:6], refs[6:10]), (refs[10:12], refs[12:14])
    capacity = picks[0].shape[2]
    for e in (1, 0):
        for k in range(2):
            for source in range(4):
                at = slice(source * capacity, (source + 1) * capacity)
                outs[k][e][at, :] = dot(picks[k][e, source], rows[k][source][...]).astype(BF16)


def partial(weights_ref, pieces, source):
    slots = weights_ref.shape[3]
    rows = slice(source * slots, (source + 1) * slots)
    total = dot(weights_ref[source, 0], pieces[0][rows, :])
    for e, piece in enumerate(pieces[1:]):
        total += dot(weights_ref[source, e + 1], piece[rows, :])
    return total


def side_sums_kernel(*refs):
    weights, pieces, outs = refs[:2], (refs[2:4], refs[4:6]), refs[6:]
    for i, source in enumerate((3, 2)):
        for k in range(2):
            outs[2 * i + k][...] = partial(weights[k], pieces[k], source).astype(BF16)


def tick_kernel(out_ref):
    out_ref[...] = jnp.zeros_like(out_ref)


def side_relay_kernel(*refs):
    weights, pieces, arrived, outs = refs[:2], (refs[2:4], refs[4:6]), refs[6:8], refs[8:]
    for k in range(2):
        total = partial(weights[k], pieces[k], 1) + arrived[k][...].astype(F32)
        outs[k][...] = total.astype(BF16)


def side_output_kernel(first_weights, second_weights, first_resid, second_resid, *refs):
    out_ref, refs = refs[-1], refs[:-1]
    count, width = len(refs) // 2, first_resid.shape[1]
    for k, (weights, resid) in enumerate(((first_weights, first_resid), (second_weights, second_resid))):
        terms = refs[k * count : (k + 1) * count]
        sums = partial(weights, terms[:2], 0)
        for arrived in terms[2:]:
            sums += arrived[...].astype(F32)
        out_ref[:, k * width : (k + 1) * width] = (resid[...].astype(F32) + sums).astype(BF16)


def hold_kernel(*refs):
    pass


def gather_kernel(pick_ref, own_ref, other_ref, *outs):
    capacity = pick_ref.shape[2]
    for i, out in enumerate(outs):
        out[:capacity, :] = dot(pick_ref[i, 0], own_ref[...]).astype(BF16)
        out[capacity:, :] = dot(pick_ref[i, 1], other_ref[...]).astype(BF16)


def direct_gather_kernel(pick_ref, own_ref, out_ref):
    out_ref[...] = dot(pick_ref[...], own_ref[...]).astype(BF16)


def assemble(plan, pieces, rows):
    for piece, at, to, count in plan:
        rows[to : to + count, :] = pieces[piece][at : at + count, :]


def back_kernel(plans, *refs):
    counts = [max(b[0] for b in plan) + 1 for plan in plans]
    pieces, (down_ref, back_ref, rows) = refs[: sum(counts)], refs[sum(counts) :]
    step, each = pl.program_id(0), pl.num_programs(0) // len(plans)
    for k, plan in enumerate(plans):
        mine = pieces[sum(counts[:k]) : sum(counts[: k + 1])]

        @pl.when(step // each == k)
        def _(plan=plan, mine=mine):
            assemble(plan, mine, rows)

    part = dot_nt(rows[...], down_ref[...])

    @pl.when(step == 0)
    def _():
        back_ref[...] = part

    @pl.when(step > 0)
    def _():
        back_ref[...] += part


def up_first_kernel(plan, *refs):
    pieces, (up_ref, total_ref, squares_ref, rows) = refs[:-4], refs[-4:]
    assemble(plan, pieces, rows)
    part = dot(rows[...], up_ref[...])
    values = rows[...].astype(F32)
    square = jnp.broadcast_to(jnp.sum(values * values, axis=1, keepdims=True), squares_ref.shape)

    @pl.when(pl.program_id(0) == 0)
    def _():
        total_ref[...] = part
        squares_ref[...] = square

    @pl.when(pl.program_id(0) > 0)
    def _():
        total_ref[...] += part
        squares_ref[...] += square


def up_last_kernel(plan, features, *refs):
    count = max(b[0] for b in plan) + 1
    pieces = refs[:count]
    up_ref, before_ref, before_squares_ref, back_ref, act_ref, pre_grad_ref, along_ref, total, squares, rows = refs[count:]
    step, steps = pl.program_id(0), pl.num_programs(0)
    assemble(plan, pieces, rows)
    part = dot(rows[...], up_ref[...])
    values = rows[...].astype(F32)
    square = jnp.broadcast_to(jnp.sum(values * values, axis=1, keepdims=True), squares.shape)

    @pl.when(step == 0)
    def _():
        total[...] = before_ref[...] + part
        squares[...] = before_squares_ref[...] + square

    @pl.when(step > 0)
    def _():
        total[...] += part
        squares[...] += square

    @pl.when(step == steps - 1)
    def _():
        scale = lax.rsqrt(squares[:, :1] / features + EPSILON)
        pre = total[...] * scale
        gate = jax.nn.sigmoid(pre)
        act_ref[...] = (pre * gate).astype(BF16)
        pre_grad = (back_ref[...] * gate * (1.0 + pre * (1.0 - gate))).astype(BF16)
        pre_grad_ref[...] = pre_grad
        along = jnp.sum(pre_grad.astype(F32) * pre, axis=1, keepdims=True)
        along_ref[...] = jnp.broadcast_to(scale * along / features, along_ref.shape)


def expert_grad_kernel(plan, pre_grad_ref, up_ref, along_ref, *refs):
    count = len(refs) // 2
    total = dot_nt(pre_grad_ref[...], up_ref[...])
    for piece, at, to, size in plan:
        rows = refs[piece][at : at + size, :].astype(F32)
        refs[count + piece][at : at + size, :] = (
            total[to : to + size, :] - rows * along_ref[to : to + size, :1]
        ).astype(BF16)


def expert_out_kernel(plan, act_ref, down_ref, *outs):
    total = dot(act_ref[...], down_ref[...])
    for piece, at, to, size in plan:
        outs[piece][at : at + size, :] = total[to : to + size, :].astype(BF16)


def on_device(inputs, b_proj, c_proj, log_decay, doc_lengths, expert_ids, gate_weights, w_up, w_down, cotangent):
    tokens, features = inputs.shape[1:]
    heads = log_decay.shape[1]
    state = b_proj.shape[2]
    experts, blocks = lax.axis_size("exp"), lax.axis_size("seq")
    hidden = w_up.shape[2]
    capacity = 3 * tokens // experts
    slots = experts * capacity
    width = features // CHUNKS
    hops = max(1, blocks // 2)
    relayed = experts == 8 and hops == 2
    kinds = ((2, (0, 1, 4, 5)), (4, (0, 1, 2, 3)))

    x, b, c, log, cot = inputs[0], b_proj[0], c_proj[0], log_decay[0], cotangent[0]
    up, down = w_up[0], w_down[0]
    meta = jnp.concatenate([doc_lengths[0], (lax.axis_index("seq") * tokens)[None].astype(jnp.int32)])

    def log_spec(k):
        return pl.BlockSpec((heads // CHUNKS, tokens), lambda i: (k, 0))

    def chunk(k, rows=tokens):
        return pl.BlockSpec((rows, width), lambda i: (0, k))

    def shape(rows, columns, kind=BF16):
        return jax.ShapeDtypeStruct((rows, columns), kind)

    small, part = whole((tokens, state)), whole((tokens, width))
    unit = tokens * width
    head_flops = 2 * tokens * unit

    def offset(a, k):
        return lax.ppermute(a, "exp", [(i, i ^ k) for i in range(experts)])

    def hop(states, step):
        return lax.ppermute(states, "seq", [(i, i + step) for i in range(blocks) if 0 <= i + step < blocks])

    def hop_on(arrived, spec, step, k, after, parts=1):
        if relayed:
            near, far = (b_pack, c_pack) if step > 0 else (c_pack, b_pack)
            wide = arrived.shape[1]
            taken, *sent = call(
                functools.partial(pass_kernel, step > 0, k),
                (1,),
                [SMEM, whole((heads, tokens)) if wide == features else log_spec(k), whole(near.shape), small, spec],
                [whole((tokens, wide))] + [whole((tokens // 2, wide // parts + state))] * parts,
                [shape(tokens, wide)] + [shape(tokens // 2, wide // parts + state)] * parts,
                2 * head_flops,
                5 * unit,
                "pass_states",
                after=after,
            )(meta, log, near, far, arrived)
            passed = [hop(rows, step) for rows in sent]
            return [[taken, rows, rows] for rows in passed], sent[0]
        arrived = [arrived]
        for _ in range(hops - 1):
            kept = call(
                keep_kernel,
                (1,),
                [SMEM, log_spec(k), part],
                part,
                shape(tokens, width),
                unit,
                4 * unit,
                "keep_states",
                after=after,
            )(meta, log, arrived[-1])
            arrived = arrived + [hop(kept, step)]
        return arrived, kept

    if relayed:
        moving = hop(x, 1)
        pack = (tokens + 3 * heads, state)
        b_pack, c_pack, *cots, cot_both = call(
            prepare_kernel,
            (1,),
            [small, small, whole((heads, tokens)), whole((tokens, features)), whole((2, tokens)), whole((2, tokens))],
            [whole(pack)] * 2 + [whole((tokens, width + 128))] * CHUNKS + [whole((2 * tokens, width + 128))],
            [shape(*pack)] * 2 + [shape(tokens, width + 128)] * CHUNKS + [shape(2 * tokens, width + 128)],
            0,
            4 * tokens * features,
            "prepare",
            vmem=VMEM_ALL,
        )(b, c, log, cot, expert_ids[0].T, gate_weights[0].T)
        b_pack, c_pack = hop(b_pack, 1), hop(c_pack, -1)
    else:
        moving = []
        for k in range(CHUNKS):
            local = call(
                local_kernel,
                (1,),
                [SMEM, log_spec(k), small, chunk(k)],
                part,
                shape(tokens, width),
                head_flops,
                4 * unit,
                "local_states",
            )(meta, log, b, x)
            moving.append(hop(local, 1))
        cots = [cot[:, k * width : (k + 1) * width] for k in range(CHUNKS)]

    def tick(arrived):
        mark = call(
            tick_kernel, (1,), [], whole((16, 128)), shape(16, 128), 0, 0, "tick", after=[arrived]
        )()
        return offset(mark, 1)

    if relayed:
        plans = [
            [
                block
                for i, o in enumerate(offsets)
                for block in ((i, 0, o * capacity, capacity), (i, capacity, (o ^ by) * capacity, capacity))
            ]
            for by, offsets in kinds
        ]
        pieces_of = [[2 * capacity] * 4] * 2
        pick_shape = (4, 2, capacity, tokens)
        weight_shape = (4, tokens, 2 * capacity)
        outs = [pick_shape, weight_shape, weight_shape] * 2
        me = lax.axis_index("exp").astype(jnp.int32)[None]
        other_cots = [offset(rows, by) for rows, (by, _) in zip(cots, kinds)]
        found = call(
            functools.partial(relay_pick_kernel, experts, capacity, kinds),
            (1,),
            [SMEM] + [pl.BlockSpec((tokens, 128), lambda i: (0, width // 128))] * 3,
            [whole(s) for s in outs],
            [jax.ShapeDtypeStruct(s, BF16) for s in outs],
            6 * experts * tokens * tokens,
            4 * slots * tokens,
            "pick_rows",
        )(me, cots[0], *other_cots)
        picks, own_weights, relay_weights = found[0::3], found[1::3], found[2::3]
    else:
        table = jnp.concatenate([expert_ids[0].T.astype(F32), gate_weights[0].T], axis=0)
        other_cots = [None] * CHUNKS
        plans = [[(0, 0, 0, slots)]] * 2
        pieces_of = [[slots]] * 2
        pick, weights = call(
            functools.partial(direct_pick_kernel, experts, capacity),
            (1,),
            [whole((4, tokens))],
            [whole((slots, tokens)), whole((1, tokens, slots))],
            [shape(slots, tokens), jax.ShapeDtypeStruct((1, tokens, slots), BF16)],
            2 * experts * tokens * tokens,
            4 * slots * tokens,
            "pick_rows",
        )(table)
        picks, own_weights = [pick] * 2, [weights] * 2

    def piece_specs(kind):
        return [whole((rows, width)) for rows in pieces_of[kind]]

    def piece_shapes(kind):
        return [shape(rows, width) for rows in pieces_of[kind]]

    def switch(pieces):
        parts = pieces[0].reshape(experts, capacity, width)
        return [lax.all_to_all(parts, "exp", split_axis=0, concat_axis=0, tiled=True).reshape(slots, width)]

    def to_experts(rows, k, other, after=()):
        kind = k % 2
        cost = (2 * slots * unit, 2 * (unit + slots * width))
        if not relayed:
            sent = call(
                direct_gather_kernel,
                (1,),
                [whole((slots, tokens)), part],
                piece_specs(kind),
                piece_shapes(kind),
                *cost,
                "gather",
                after=after,
            )(picks[kind], rows)
            return sent, switch(sent)
        _, offsets = kinds[kind]
        sent = call(
            gather_kernel,
            (1,),
            [whole(picks[kind].shape), part, part],
            piece_specs(kind),
            piece_shapes(kind),
            *cost,
            "gather",
            after=after,
        )(picks[kind], rows, other)
        return sent, [piece if o == 0 else offset(piece, o) for piece, o in zip(sent, offsets)]

    def other_of(rows, k):
        return offset(rows, kinds[k % 2][0]) if relayed else None

    def to_positions(pieces, k, after=()):
        kind = k % 2
        if not relayed:
            arrived = switch(pieces)
            return arrived[0], arrived
        by, offsets = kinds[kind]
        pieces = [piece if o == 0 else offset(piece, o) for piece, o in zip(pieces, offsets)]
        relay = call(
            relay_kernel,
            (1,),
            [whole(relay_weights[kind].shape)] + piece_specs(kind),
            part,
            shape(tokens, width),
            2 * slots * unit,
            2 * (unit + slots * width),
            "relay",
            after=after,
        )(relay_weights[kind], *pieces)
        return relay, pieces + [offset(relay, by)]

    def moved_specs(kind):
        return piece_specs(kind) + ([part] if relayed else [])

    inner = call(
        inner_kernel,
        (CHUNKS,),
        [SMEM, pl.BlockSpec((heads // CHUNKS, tokens), lambda i: (i, 0)), small, small, columns(tokens, width)],
        columns(tokens, width),
        shape(tokens, features, F32),
        2 * CHUNKS * head_flops,
        6 * CHUNKS * unit,
        "inner",
    )(meta, log, b, c, x)
    if relayed:
        [first_in], kept = hop_on(moving, whole((tokens, features)), 1, 0, [inner, picks[0]])
        second_in = first_in
    else:
        first_in, kept = hop_on(moving[0], part, 1, 0, [inner, picks[0]])
    if relayed:
        held = call(
            hold_kernel,
            (1,),
            [anywhere] * 3,
            [anywhere] * 3,
            [shape(tokens, width + 128)] * 2 + [shape(2 * tokens, width + 128)],
            0,
            0,
            "hold",
            after=[moving, inner, b_pack, c_pack],
            aliases={0: 0, 1: 1, 2: 2},
        )(*other_cots, cot_both)
        cot_sibling = offset(held[2], 1)
        side_others = [offset(rows, 1) for rows in held[:2]]
        table_spec = pl.BlockSpec((tokens, 128), lambda i: (0, width // 128))
        side_kinds = ((2, 4), (4, 2))
        side_plans = [
            [
                (e, j * capacity, (to ^ source) * capacity, capacity)
                for e, to in enumerate((0, partner))
                for j, source in enumerate((0, by, 1, by ^ 1))
            ]
            for by, partner in side_kinds
        ]
        side_shape, side_weight_shape = (2, 4, capacity, tokens), (4, 2, tokens, capacity)
        found = call(
            functools.partial(side_pick_kernel, experts, capacity, side_kinds),
            (1,),
            [SMEM] + [table_spec] * 6,
            [whole(side_shape)] * 4,
            [jax.ShapeDtypeStruct(side_shape, kind) for kind in (BF16, F32)] * 2,
            12 * experts * tokens * tokens,
            8 * slots * tokens,
            "side_picks",
        )(me, cots[0], cot_sibling, held[0], side_others[0], held[1], side_others[1])
        side_picks, side_gated = found[0::2], found[1::2]
        side_spec = whole((4 * capacity, width))
        both = [pl.BlockSpec((tokens, width), lambda i, k=k: (k, 0)) for k in range(2)]
        sent = call(
            side_gather_kernel,
            (1,),
            [whole(side_shape)] * 2 + [spec for k in range(2) for spec in (part, part, both[k], part)],
            [side_spec] * 4,
            [shape(4 * capacity, width)] * 4,
            4 * slots * unit,
            8 * slots * width,
            "side_gather",
            after=[kept],
        )(*side_picks, *[r for k in range(2) for r in (cots[k], held[k], cot_sibling, side_others[k])])
        got_cot = [[sent[2 * k], offset(sent[2 * k + 1], side_kinds[k][1])] for k in range(2)]
        sent = sent[1]
        early = [[], [pieces[1] for pieces in got_cot]]
    else:
        got_cot, sent, early = [], kept, [[], []]
        for k in range(CHUNKS):
            (sent, *_), pieces = to_experts(cots[k], k, other_cots[k], [sent])
            got_cot.append(pieces)
    if not relayed:
        second_in, _ = hop_on(moving[1], part, 1, 1, [sent])
    states_in = [first_in, second_in]


    def states_specs(k, w):
        if not relayed:
            return [part] * hops
        return [
            chunk(k),
            chunk(k, tokens // 2),
            pl.BlockSpec((tokens // 2, state), lambda i: (0, w // state)),
        ]

    resid, squares, others = [], [], []
    for k in range(CHUNKS):
        rows, square = call(
            functools.partial(resid_kernel, relayed),
            (1,),
            [SMEM, log_spec(k), small, chunk(k)] + states_specs(k, features),
            [part, whole((tokens, 128))],
            [shape(tokens, width), shape(tokens, 128, F32)],
            hops * head_flops,
            (6 + 2 * hops) * unit,
            "resid",
            after=early[k],
        )(meta, log, c, inner, *states_in[k])
        resid.append(rows)
        squares.append(square)
        others.append(other_of(rows, k))

    each = 2
    step = width // each
    chunk_flops = 2 * slots * width * hidden
    chunk_bytes = 2 * width * (hidden + slots)
    slots_hidden = whole((slots, hidden))

    def step_specs(kind, first=0):
        return [
            pl.BlockSpec((rows, step), lambda i: (0, jnp.clip(i - first, 0, each - 1))) for rows in pieces_of[kind]
        ]

    if relayed:
        cot_plans = side_plans
        cot_specs = [
            pl.BlockSpec((4 * capacity, step), lambda i, k=k: (0, jnp.clip(i - each * k, 0, each - 1)))
            for k in range(CHUNKS)
            for _ in range(2)
        ]
    else:
        cot_plans = [plans[k % 2] for k in range(CHUNKS)]
        cot_specs = [spec for k in range(CHUNKS) for spec in step_specs(k % 2, each * k)]
    back = call(
        functools.partial(back_kernel, cot_plans),
        (each * CHUNKS,),
        cot_specs + [columns(hidden, step)],
        slots_hidden,
        shape(slots, hidden, F32),
        CHUNKS * chunk_flops,
        CHUNKS * chunk_bytes,
        "back",
        [pltpu.VMEM((slots, step), BF16)],
        after=[resid[1]],
    )(*[piece for pieces in got_cot for piece in pieces], down)
    (sent, *_), pieces = to_experts(resid[0], 0, others[0], [back])
    got_in = [pieces]
    _, pieces = to_experts(resid[1], 1, others[1], [sent])
    got_in.append(pieces)

    def up_spec(k):
        return pl.BlockSpec((step, hidden), lambda i: (each * k + i, 0))

    slots_small = whole((slots, 128))
    total, total_squares = call(
        functools.partial(up_first_kernel, plans[0]),
        (each,),
        step_specs(0) + [up_spec(0)],
        [slots_hidden, slots_small],
        [shape(slots, hidden, F32), shape(slots, 128, F32)],
        chunk_flops,
        chunk_bytes,
        "up_first",
        [pltpu.VMEM((slots, step), BF16)],
    )(*got_in[0], up)
    act, pre_grad, along = call(
        functools.partial(up_last_kernel, plans[1], features),
        (each,),
        step_specs(1) + [up_spec(1), slots_hidden, slots_small, slots_hidden],
        [slots_hidden, slots_hidden, slots_small],
        [shape(slots, hidden), shape(slots, hidden), shape(slots, 128, F32)],
        chunk_flops,
        chunk_bytes,
        "up_last",
        [pltpu.VMEM((slots, hidden), F32), pltpu.VMEM((slots, 128), F32), pltpu.VMEM((slots, step), BF16)],
    )(*got_in[1], up, total, total_squares, back)

    got_grad, grads, last = [], [], []
    for k in range(CHUNKS):
        kind = k % 2
        expert_grad = call(
            functools.partial(expert_grad_kernel, plans[kind]),
            (each,),
            [slots_hidden, up_spec(k), slots_small] + step_specs(kind),
            step_specs(kind),
            piece_shapes(kind),
            chunk_flops,
            chunk_bytes,
            "expert_grad",
            after=last,
        )(pre_grad, up, along, *got_in[k])
        last = expert_grad[:1]
        grads.append(expert_grad)
    outs = []
    for k in range(CHUNKS):
        kind = k % 2
        expert_out = call(
            functools.partial(expert_out_kernel, side_plans[k] if relayed else plans[kind]),
            (each,),
            [slots_hidden, pl.BlockSpec((hidden, step), lambda i, k=k: (0, each * k + i))],
            [pl.BlockSpec((4 * capacity, step), lambda i: (0, i))] * 2 if relayed else step_specs(kind),
            [shape(4 * capacity, width)] * 2 if relayed else piece_shapes(kind),
            chunk_flops,
            chunk_bytes,
            "expert_out",
            after=last,
        )(act, down)
        outs.append(expert_out)
        last = expert_out[:1]

    for k in range(CHUNKS):
        relay, pieces = to_positions(grads[k], k, last)
        got_grad.append(pieces)
        last = [relay]
    last = relay

    def weights_spec(kind):
        return whole(own_weights[kind].shape)

    dresid, states_after = [], []
    if relayed:
        dresid_whole = call(
            functools.partial(dresid_all_kernel, features),
            (1,),
            [weights_spec(k) for k in range(2)]
            + [whole((tokens, features))]
            + [whole((tokens, 128))] * 2
            + [spec for k in range(2) for spec in moved_specs(k)],
            whole((tokens, features)),
            shape(tokens, features),
            4 * slots * unit,
            8 * unit + 4 * slots * width,
            "dresid",
            after=[last],
        )(*own_weights, cot, *squares, *got_grad[0], *got_grad[1])
        moving_back = hop(dresid_whole, -1)
        last = dresid_whole
    else:
        for k in range(CHUNKS):
            kind = k % 2
            grads_here = call(
                functools.partial(dresid_kernel, CHUNKS, features),
                (1,),
                [SMEM, log_spec(k), small, weights_spec(kind), chunk(k)]
                + [whole((tokens, 128))] * CHUNKS
                + moved_specs(kind),
                [part] * (1 if relayed else 2),
                [shape(tokens, width)] * (1 if relayed else 2),
                head_flops + 2 * slots * unit,
                6 * unit + 2 * slots * width,
                "dresid",
                after=[last],
            )(meta, log, c, own_weights[kind], cot, *squares, *got_grad[k])
            dresid.append(grads_here[0])
            states_after.append(hop(grads_here[-1], -1))
            last = dresid[k]
    inner_back = []
    if relayed:
        last = inner_back_whole = call(
            inner_back_kernel,
            (CHUNKS,),
            [SMEM, pl.BlockSpec((heads // CHUNKS, tokens), lambda i: (i, 0)), small, small, columns(tokens, width)],
            columns(tokens, width),
            shape(tokens, features, F32),
            2 * CHUNKS * head_flops,
            6 * CHUNKS * unit,
            "inner_back",
            after=[last],
        )(meta, log, b, c, dresid_whole)
    else:
        for k in range(CHUNKS):
            last = call(
                inner_back_kernel,
                (1,),
                [SMEM, log_spec(k), small, small, part],
                part,
                shape(tokens, width, F32),
                2 * head_flops,
                6 * unit,
                "inner_back",
                after=[last],
            )(meta, log, b, c, dresid[k])
            inner_back.append(last)
    got_out = []
    if relayed:
        held = call(
            hold_kernel,
            (1,),
            [anywhere] * 2,
            [anywhere] * 2,
            [shape(4 * capacity, width)] * 2,
            0,
            0,
            "hold",
            after=[dresid_whole],
            aliases={0: 0, 1: 1},
        )(outs[0][1], outs[1][1])
        side_weights = call(
            side_weights_kernel,
            (1,),
            [whole(side_shape)] * 2,
            [whole(side_weight_shape)] * 2,
            [jax.ShapeDtypeStruct(side_weight_shape, BF16)] * 2,
            0,
            16 * slots * tokens,
            "side_weights",
            after=outs[0][:1],
        )(*side_gated)
        out_pieces = [[outs[k][0], offset(held[k], side_kinds[k][1])] for k in range(2)]
        operands = [*side_weights, *out_pieces[0], *out_pieces[1]]
        specs = [whole(side_weight_shape)] * 2 + [side_spec] * 4
        sums = call(
            side_sums_kernel,
            (1,),
            specs,
            [part] * 4,
            [shape(tokens, width)] * 4,
            4 * slots * unit,
            8 * slots * width,
            "side_sums",
            after=[last],
        )(*operands)
        sums_here = [offset(rows, 1) for rows in sums]
        sent = call(
            side_relay_kernel,
            (1,),
            specs + [part] * 2,
            [part] * 2,
            [shape(tokens, width)] * 2,
            4 * slots * unit,
            8 * slots * width,
            "side_relay",
        )(*operands, *sums_here[:2])
        after_whole, last = hop_on(moving_back, whole((tokens, features)), -1, 0, [sent[0]], CHUNKS)
        relayed_sums = [offset(sent[k], side_kinds[k][0]) for k in range(2)]
    else:
        for k in range(CHUNKS):
            states_after[k], last = hop_on(states_after[k], part, -1, k, [last])
            last, pieces = to_positions(outs[k], k, [last])
            got_out.append(pieces)

    def placed(kernel, k, in_specs, operands, earlier, after, flops, nbytes, name):
        more = [] if earlier is None else [earlier]
        return call(
            kernel,
            (1,),
            in_specs + [pl.BlockSpec(memory_space=pl.ANY)] * len(more),
            chunk(k),
            shape(tokens, features),
            flops,
            nbytes,
            name,
            after=after,
            aliases={len(operands): 0} if more else {},
        )(*operands, *more)

    def input_grads(k, earlier, after):
        return placed(
            functools.partial(grad_kernel, 3 if relayed else hops, relayed),
            k,
            [SMEM, log_spec(k), small, part] + states_specs(0, width),
            [meta, log, b, inner_back[k], *states_after[k]],
            earlier,
            after,
            hops * head_flops,
            (6 + 2 * hops) * unit,
            "input_grad",
        )

    if relayed:
        pass
    else:
        input_grad, output = input_grads(0, None, [last]), None
    if relayed:
        output = call(
            side_output_kernel,
            (1,),
            [whole(side_weight_shape)] * 2
            + [part] * 2
            + [spec for k in range(2) for spec in (side_spec, side_spec, part, part)],
            whole((tokens, features)),
            shape(tokens, features),
            2 * slots * unit,
            8 * unit + 4 * slots * width,
            "output",
            after=[last],
        )(*side_weights, *resid, *[r for k in range(2) for r in (*out_pieces[k], sums_here[2 + k], relayed_sums[k])])
        input_grad = None
        for k in range(CHUNKS):
            more = [] if input_grad is None else [input_grad]
            input_grad = call(
                functools.partial(grad_kernel, 3, relayed),
                (1,),
                [SMEM, log_spec(k), small, chunk(k), chunk(k)]
                + [whole((tokens // 2, width)), pl.BlockSpec((tokens // 2, state), lambda i: (0, width // state))]
                + [anywhere] * len(more),
                chunk(k),
                shape(tokens, features),
                hops * head_flops,
                (6 + 2 * hops) * unit,
                "input_grad",
                after=[output] if k == 0 else [],
                aliases={7: 0} if more else {},
                vmem=VMEM_BYTES,
            )(meta, log, b, inner_back_whole, *after_whole[k], *more)
    else:
        for k in range(CHUNKS):
            kind = k % 2
            output = placed(
                output_kernel,
                k,
                [weights_spec(kind), part] + moved_specs(kind),
                [own_weights[kind], resid[k], *got_out[k]],
                output,
                [input_grad] if output is None else [],
                2 * slots * unit,
                4 * unit + 2 * slots * width,
                "output",
            )
    if not relayed:
        input_grad = input_grads(1, input_grad, [output])
    return (output[None], input_grad[None])


def solution(mesh):
    placed = (
        P("exp", "seq", None),
        P("exp", "seq", None),
        P("exp", "seq", None),
        P("exp", None, "seq"),
        P("exp", None),
        P("exp", "seq", None),
        P("exp", "seq", None),
        P("exp", None, None),
        P("exp", None, None),
        P("exp", "seq", None),
    )
    return jax.shard_map(
        on_device,
        mesh=mesh,
        in_specs=placed,
        out_specs=(P("exp", "seq", None), P("exp", "seq", None)),
        check_vma=False,
    )
```

```python
import functools

import jax
import jax.numpy as jnp
from jax import lax
from jax.experimental import pallas as pl
from jax.experimental.pallas import tpu as pltpu
from jax.sharding import PartitionSpec as P

EPSILON = 1e-06
F32 = jnp.float32
BF16 = jnp.bfloat16
CHUNKS = 2
VMEM_BYTES = 26 * 1024 * 1024
VMEM_ALL = 60 * 1024 * 1024
NT = (((1,), (1,)), ((), ()))


def dot(a, b):
    return jnp.dot(a, b, preferred_element_type=F32)


def dot_nt(a, b):
    return lax.dot_general(a, b, NT, preferred_element_type=F32)


def call(kernel, grid, in_specs, out_specs, out_shape, flops, nbytes, name, scratch=(), after=(), aliases=None, vmem=VMEM_BYTES):
    count, more = len(in_specs), len(after)

    def body(*refs):
        kernel(*refs[:count], *refs[count + more :])

    called = pl.pallas_call(
        body,
        grid=grid,
        in_specs=list(in_specs) + [pl.BlockSpec(memory_space=pl.ANY)] * more,
        out_specs=out_specs,
        out_shape=out_shape,
        scratch_shapes=scratch,
        input_output_aliases=aliases or {},
        name=name,
        cost_estimate=pl.CostEstimate(flops=flops, bytes_accessed=nbytes, transcendentals=0),
        compiler_params=pltpu.CompilerParams(vmem_limit_bytes=vmem),
    )
    return lambda *operands: called(*operands, *after)


def whole(shape):
    return pl.BlockSpec(shape, lambda i: (0,) * len(shape))


def columns(rows, width):
    return pl.BlockSpec((rows, width), lambda i: (0, i))


anywhere = pl.BlockSpec(memory_space=pl.ANY)
SMEM = pl.BlockSpec(memory_space=pltpu.SMEM)


def documents(meta, size, shift=0):
    count = meta.shape[0] - 1
    first = meta[count] + shift * size
    along = first + lax.broadcasted_iota(jnp.int32, (1, size), 1)
    down = first + lax.broadcasted_iota(jnp.int32, (size, 1), 0)
    row = jnp.full((1, size), -1, jnp.int32)
    col = jnp.full((size, 1), -1, jnp.int32)
    before, last, start = jnp.int32(-1), jnp.int32(-1), jnp.int32(0)
    for i in range(count):
        row += (start <= along).astype(jnp.int32)
        col += (start <= down).astype(jnp.int32)
        before += (start <= first - 1).astype(jnp.int32)
        last += (start <= first + size - 1).astype(jnp.int32)
        start = start + meta[i]
    return row, col, before, last


def running(log_ref):
    size = log_ref.shape[1]
    upto = (
        lax.broadcasted_iota(jnp.int32, (size, size), 0)
        <= lax.broadcasted_iota(jnp.int32, (size, size), 1)
    ).astype(F32)
    return jnp.dot(
        log_ref[...], upto, precision=lax.Precision.HIGHEST, preferred_element_type=F32
    )


def head(h, size):
    return slice(h * size, (h + 1) * size)


def local_kernel(meta, log_ref, b_ref, x_ref, state_ref):
    size = log_ref.shape[1]
    cum = running(log_ref)
    row, _, _, last = documents(meta, size)
    tail = (row == last).astype(F32)
    weight = tail * jnp.exp(cum[:, size - 1 :] - cum)
    b_t = b_ref[...].astype(F32).T
    p = x_ref.shape[1] // cum.shape[0]
    for h in range(cum.shape[0]):
        b_weighted = (b_t * weight[h : h + 1, :]).astype(BF16)
        state_ref[:, head(h, p)] = dot(b_weighted, x_ref[:, head(h, p)]).astype(BF16)


def pair_mask(meta, size):
    row, col, before, last = documents(meta, size)
    later = lax.broadcasted_iota(jnp.int32, (size, size), 0)
    earlier = lax.broadcasted_iota(jnp.int32, (size, size), 1)
    return row, col, before, last, later, earlier


def inner_kernel(meta, log_ref, b_ref, c_ref, x_ref, out_ref):
    size = log_ref.shape[1]
    cum = running(log_ref)
    cum_t = cum.T
    row, col, _, _, down, along = pair_mask(meta, size)
    scores = jnp.where((row == col) & (down >= along), dot_nt(c_ref[...], b_ref[...]), 0.0)
    p = x_ref.shape[1] // cum.shape[0]
    for h in range(cum.shape[0]):
        spread = cum_t[:, h : h + 1] - cum[h : h + 1, :]
        pair = (jnp.exp(jnp.minimum(spread, 0.0)) * scores).astype(BF16)
        out_ref[:, head(h, p)] = dot(pair, x_ref[:, head(h, p)])


def inner_back_kernel(meta, log_ref, b_ref, c_ref, grad_ref, out_ref):
    size = log_ref.shape[1]
    cum = running(log_ref)
    cum_t = cum.T
    row, col, _, _, down, along = pair_mask(meta, size)
    scores = jnp.where((row == col) & (down <= along), dot_nt(b_ref[...], c_ref[...]), 0.0)
    p = grad_ref.shape[1] // cum.shape[0]
    for h in range(cum.shape[0]):
        spread = cum[h : h + 1, :] - cum_t[:, h : h + 1]
        pair = (jnp.exp(jnp.minimum(spread, 0.0)) * scores).astype(BF16)
        out_ref[:, head(h, p)] = dot(pair, grad_ref[:, head(h, p)])


def keep_kernel(meta, log_ref, state_ref, out_ref):
    size = log_ref.shape[1]
    total = jnp.exp(running(log_ref)[:, size - 1 :])
    _, _, before, last = documents(meta, size)
    total = jnp.where(before == last, total, 0.0)
    p = state_ref.shape[1] // total.shape[0]
    for h in range(total.shape[0]):
        out_ref[:, head(h, p)] = (
            state_ref[:, head(h, p)].astype(F32) * total[h : h + 1, :]
        ).astype(BF16)


def prepare_kernel(b_ref, c_ref, log_ref, cot_ref, ids_ref, gates_ref, b_pack_ref, c_pack_ref, *chunks):
    chunks, both = chunks[:-1], chunks[-1]
    size = ids_ref.shape[1]
    width = chunks[0].shape[1] - size
    table = jnp.concatenate([ids_ref[...].astype(F32), gates_ref[...], jnp.zeros((size - 4, size), F32)], axis=0)
    table = table.T.astype(BF16)
    for k, chunk in enumerate(chunks):
        for ref, to in ((chunk, 0), (both, k * size)):
            ref[to : to + size, :width] = cot_ref[:, k * width : (k + 1) * width]
            ref[to : to + size, width:] = table
    rest, heads, at = log_ref[...], log_ref.shape[0], b_ref.shape[0]
    b_pack_ref[:at, :] = b_ref[...]
    c_pack_ref[:at, :] = c_ref[...]
    for _ in range(3):
        term = rest.astype(BF16)
        rest = rest - term.astype(F32)
        b_pack_ref[at : at + heads, :] = term
        c_pack_ref[at : at + heads, :] = term
        at += heads


def pass_kernel(ahead, chunk, meta, log_ref, near_ref, far_ref, rows_ref, state_ref, *sent_refs):
    size, heads = log_ref.shape[1], log_ref.shape[0]
    half = size // 2
    _, _, before, last = documents(meta, size)
    near_row, _, _, _ = documents(meta, size, -1 if ahead else 1)
    far_row, _, _, _ = documents(meta, size, 1 if ahead else -1)
    total = jnp.where(before == last, jnp.exp(running(log_ref)[:, size - 1 :]), 0.0)
    terms = (near_ref.shape[0] - size) // 3
    near_log = jnp.zeros((heads, size), F32)
    for i in range(3):
        at = size + i * terms + chunk * heads
        near_log += near_ref[at : at + heads, :].astype(F32)
    cum = running(near_log)
    if ahead:
        weight = jnp.where(near_row == before, jnp.exp(cum[:, size - 1 :] - cum), 0.0)
        count = jnp.sum((far_row == last).astype(F32), axis=1, keepdims=True)
        rows, wanted = slice(half, size), slice(0, half)
    else:
        weight = jnp.where(near_row == last, jnp.exp(cum), 0.0)
        count = jnp.sum((far_row == before).astype(F32), axis=1, keepdims=True)
        rows, wanted = slice(0, half), slice(half, size)
    few = (count <= half).astype(F32)
    weight_t = weight.T
    near_t = near_ref[:size, :].astype(F32).T
    far = far_ref[wanted, :]
    width = rows_ref.shape[1]
    p = width // heads
    for h in range(heads):
        at = head(h, p)
        state = dot((near_t * weight[h : h + 1, :]).astype(BF16), rows_ref[:, at]).astype(BF16)
        state_ref[:, at] = state
        scale = total[h : h + 1, :]
        sums = dot(far, state) * (few * scale)
        scaled = rows_ref[rows, at].astype(F32) * (weight_t[rows, h : h + 1] * ((1.0 - few) * scale))
        sent_ref = sent_refs[h * len(sent_refs) // heads]
        to = head(h % (heads // len(sent_refs)), p)
        sent_ref[:, to] = (sums + scaled).astype(BF16)
    for sent_ref in sent_refs:
        sent_ref[:, width // len(sent_refs) :] = near_ref[rows, :]


def spread_of(few, shift, mine, theirs):
    size, half = mine.shape[0], theirs.shape[0]
    down = lax.broadcasted_iota(jnp.int32, (size, half), 0)
    along = lax.broadcasted_iota(jnp.int32, (size, half), 1)
    same = (down == along + shift).astype(F32)
    return (few * same + (1.0 - few) * dot_nt(mine, theirs)).astype(BF16)


def carried_in(mine, spread, states, at):
    carried = dot(mine, states[0][:, at])
    if spread is not None:
        return carried + dot(spread, states[1][:, at])
    for state in states[1:]:
        carried += dot(mine, state[:, at])
    return carried


def resid_kernel(relayed, meta, log_ref, c_ref, inner_ref, *refs):
    states, (resid_ref, squares_ref) = refs[:-2], refs[-2:]
    size = log_ref.shape[1]
    row, col, before, _ = documents(meta, size)
    weight = jnp.where(col == before, jnp.exp(running(log_ref).T), 0.0)
    width = inner_ref.shape[1]
    p = width // log_ref.shape[0]
    spread = None
    if relayed:
        few = (jnp.sum((row == before).astype(F32), axis=1, keepdims=True) <= size // 2).astype(F32)
        spread = spread_of(few, 0, c_ref[...], states[2][...])
    squares = jnp.zeros((size, p), F32)
    for h in range(log_ref.shape[0]):
        carried = carried_in(c_ref[...], spread, states, head(h, p))
        rows = (inner_ref[:, head(h, p)] + weight[:, h : h + 1] * carried).astype(BF16)
        resid_ref[:, head(h, p)] = rows
        squares += rows.astype(F32) * rows.astype(F32)
    squares_ref[...] = jnp.broadcast_to(jnp.sum(squares, axis=1, keepdims=True), squares_ref.shape)


def combined(weights_ref, pieces):
    total = dot(weights_ref[0], pieces[0][...])
    for i, piece in enumerate(pieces[1:]):
        total += dot(weights_ref[i + 1], piece[...])
    return total


def relay_kernel(weights_ref, *refs):
    pieces, out_ref = refs[:-1], refs[-1]
    out_ref[...] = combined(weights_ref, pieces).astype(BF16)


def dresid_kernel(chunks, features, meta, log_ref, c_ref, weights_ref, cot_ref, *refs):
    squares, refs = refs[:chunks], refs[chunks:]
    count = weights_ref.shape[0]
    relayed = weights_ref.shape[0] > 1
    moved_refs, outs = (refs[:-1], refs[-1:]) if relayed else (refs[:-2], refs[-2:])
    dresid_ref = outs[0]
    size = log_ref.shape[1]
    row, _, before, _ = documents(meta, size)
    weight = jnp.where(row == before, jnp.exp(running(log_ref)), 0.0)
    c_t = c_ref[...].astype(F32).T
    total = squares[0][...]
    for part in squares[1:]:
        total = total + part[...]
    scale = lax.rsqrt(total[:, :1] / features + EPSILON)
    moved = combined(weights_ref, moved_refs[:count])
    for arrived in moved_refs[count:]:
        moved += arrived[...].astype(F32)
    dresid_ref[...] = (cot_ref[...].astype(F32) + scale * moved).astype(BF16)
    if relayed:
        return
    p = cot_ref.shape[1] // log_ref.shape[0]
    for h in range(log_ref.shape[0]):
        c_weighted = (c_t * weight[h : h + 1, :]).astype(BF16)
        outs[1][:, head(h, p)] = dot(c_weighted, dresid_ref[:, head(h, p)]).astype(BF16)


def dresid_all_kernel(features, first_weights, second_weights, cot_ref, *refs):
    squares, refs, dresid_ref = refs[:2], refs[2:-1], refs[-1]
    scale = lax.rsqrt((squares[0][:, :1] + squares[1][:, :1]) / features + EPSILON)
    count, width = len(refs) // 2, cot_ref.shape[1] // 2
    for k, weights in enumerate((first_weights, second_weights)):
        terms = refs[k * count : (k + 1) * count]
        moved = combined(weights, terms[: weights.shape[0]])
        for arrived in terms[weights.shape[0] :]:
            moved += arrived[...].astype(F32)
        at = slice(k * width, (k + 1) * width)
        dresid_ref[:, at] = (cot_ref[:, at].astype(F32) + scale * moved).astype(BF16)


def grad_kernel(count, relayed, meta, log_ref, b_ref, inner_ref, *refs):
    states, out_ref = refs[:count], refs[-1]
    size = log_ref.shape[1]
    row, col, _, last = documents(meta, size)
    cum = running(log_ref)
    weight = jnp.where(col == last, jnp.exp(cum[:, size - 1 :] - cum).T, 0.0)
    width = inner_ref.shape[1]
    p = width // log_ref.shape[0]
    spread = None
    if relayed:
        few = (jnp.sum((row == last).astype(F32), axis=1, keepdims=True) <= size // 2).astype(F32)
        spread = spread_of(few, size // 2, b_ref[...], states[2][...])
    for h in range(log_ref.shape[0]):
        carried = carried_in(b_ref[...], spread, states, head(h, p))
        out_ref[:, head(h, p)] = (inner_ref[:, head(h, p)] + weight[:, h : h + 1] * carried).astype(BF16)


def output_kernel(weights_ref, resid_ref, *refs):
    out_ref = refs[-1]
    count = weights_ref.shape[0]
    moved = combined(weights_ref, refs[:count])
    for arrived in refs[count : len(refs) - 1]:
        if arrived.shape == out_ref.shape:
            moved += arrived[...].astype(F32)
    out_ref[...] = (resid_ref[...].astype(F32) + moved).astype(BF16)


def picks_of(table, me, experts, capacity):
    tokens = table.shape[1]
    offset = lax.broadcasted_iota(jnp.int32, (experts, tokens), 0)
    first = (table[0:1, :].astype(jnp.int32) ^ me) == offset
    second = (table[1:2, :].astype(jnp.int32) ^ me) == offset
    named = (first | second).astype(F32)
    gate = jnp.where(first, table[2:3, :], 0.0) + jnp.where(second, table[3:4, :], 0.0)
    before = (
        lax.broadcasted_iota(jnp.int32, (tokens, tokens), 0)
        < lax.broadcasted_iota(jnp.int32, (tokens, tokens), 1)
    ).astype(BF16)
    rank = jnp.where(named > 0, dot(named.astype(BF16), before), -1.0)
    slot = lax.broadcasted_iota(jnp.int32, (capacity, tokens), 0).astype(F32)
    picks = [(rank[e : e + 1, :] == slot).astype(F32) for e in range(experts)]
    return picks, [pick * gate[e : e + 1, :] for e, pick in enumerate(picks)]


def direct_pick_kernel(experts, capacity, table_ref, pick_ref, weights_ref):
    picks, gated = picks_of(table_ref[...], 0, experts, capacity)
    pick_ref[...] = jnp.concatenate(picks, axis=0).astype(BF16)
    weights_ref[0] = jnp.concatenate(gated, axis=0).T.astype(BF16)


def relay_pick_kernel(experts, capacity, kinds, me_ref, own_ref, *refs):
    tables, outs = refs[: len(kinds)], refs[len(kinds) :]
    me = me_ref[0]
    picks, gated = picks_of(own_ref[...].astype(F32).T, me, experts, capacity)
    none = jnp.zeros_like(picks[0])
    for (_, offsets), table_ref, (pick_ref, own_weights_ref, relay_weights_ref) in zip(
        kinds, tables, (outs[:3], outs[3:])
    ):
        other_picks, other_gated = picks_of(table_ref[...].astype(F32).T, me, experts, capacity)
        for i, o in enumerate(offsets):
            pick_ref[i, 0] = picks[o].astype(BF16)
            pick_ref[i, 1] = other_picks[o].astype(BF16)
            own_weights_ref[i] = jnp.concatenate([gated[o], none], axis=0).T.astype(BF16)
            relay_weights_ref[i] = jnp.concatenate([none, other_gated[o]], axis=0).T.astype(BF16)


def side_pick_kernel(experts, capacity, kinds, me_ref, own_ref, sibling_ref, *refs):
    tables, outs = refs[:4], refs[4:]
    mine = [picks_of(t[...].astype(F32).T, me_ref[0], experts, capacity) for t in (own_ref, sibling_ref)]
    for k, (_, partner) in enumerate(kinds):
        near = [picks_of(t[...].astype(F32).T, me_ref[0], experts, capacity) for t in tables[2 * k : 2 * k + 2]]
        pick_ref, gated_ref = outs[2 * k : 2 * k + 2]
        for source, (picks, gated) in enumerate((mine[0], near[0], mine[1], near[1])):
            for e, to in enumerate((0, partner)):
                pick_ref[e, source] = picks[to].astype(BF16)
                gated_ref[e, source] = gated[to]


def side_weights_kernel(*refs):
    for gated_ref, weights_ref in zip(refs[:2], refs[2:]):
        for e in range(2):
            for source in range(4):
                weights_ref[source, e] = gated_ref[e, source].T.astype(BF16)


def side_gather_kernel(*refs):
    picks, rows, outs = refs[:2], (refs[2:6], refs[6:10]), (refs[10:12], refs[12:14])
    capacity = picks[0].shape[2]
    for e in (1, 0):
        for k in range(2):
            for source in range(4):
                at = slice(source * capacity, (source + 1) * capacity)
                outs[k][e][at, :] = dot(picks[k][e, source], rows[k][source][...]).astype(BF16)


def partial(weights_ref, pieces, source):
    slots = weights_ref.shape[3]
    rows = slice(source * slots, (source + 1) * slots)
    total = dot(weights_ref[source, 0], pieces[0][rows, :])
    for e, piece in enumerate(pieces[1:]):
        total += dot(weights_ref[source, e + 1], piece[rows, :])
    return total


def side_sums_kernel(*refs):
    weights, pieces, outs = refs[:2], (refs[2:4], refs[4:6]), refs[6:]
    for i, source in enumerate((3, 2)):
        for k in range(2):
            outs[2 * i + k][...] = partial(weights[k], pieces[k], source).astype(BF16)


def tick_kernel(out_ref):
    out_ref[...] = jnp.zeros_like(out_ref)


def side_relay_kernel(*refs):
    weights, pieces, arrived, outs = refs[:2], (refs[2:4], refs[4:6]), refs[6:8], refs[8:]
    for k in range(2):
        total = partial(weights[k], pieces[k], 1) + arrived[k][...].astype(F32)
        outs[k][...] = total.astype(BF16)


def side_output_kernel(first_weights, second_weights, first_resid, second_resid, *refs):
    out_ref, mark_ref, refs = refs[-2], refs[-1], refs[:-2]
    mark_ref[...] = jnp.zeros_like(mark_ref)
    count, width = len(refs) // 2, first_resid.shape[1]
    for k, (weights, resid) in enumerate(((first_weights, first_resid), (second_weights, second_resid))):
        terms = refs[k * count : (k + 1) * count]
        sums = partial(weights, terms[:2], 0)
        for arrived in terms[2:]:
            sums += arrived[...].astype(F32)
        out_ref[:, k * width : (k + 1) * width] = (resid[...].astype(F32) + sums).astype(BF16)


def hold_kernel(*refs):
    pass


def gather_kernel(pick_ref, own_ref, other_ref, *outs):
    capacity = pick_ref.shape[2]
    for i, out in enumerate(outs):
        out[:capacity, :] = dot(pick_ref[i, 0], own_ref[...]).astype(BF16)
        out[capacity:, :] = dot(pick_ref[i, 1], other_ref[...]).astype(BF16)


def direct_gather_kernel(pick_ref, own_ref, out_ref):
    out_ref[...] = dot(pick_ref[...], own_ref[...]).astype(BF16)


def assemble(plan, pieces, rows):
    for piece, at, to, count in plan:
        rows[to : to + count, :] = pieces[piece][at : at + count, :]


def back_kernel(plans, *refs):
    counts = [max(b[0] for b in plan) + 1 for plan in plans]
    pieces, (down_ref, back_ref, rows) = refs[: sum(counts)], refs[sum(counts) :]
    step, each = pl.program_id(0), pl.num_programs(0) // len(plans)
    for k, plan in enumerate(plans):
        mine = pieces[sum(counts[:k]) : sum(counts[: k + 1])]

        @pl.when(step // each == k)
        def _(plan=plan, mine=mine):
            assemble(plan, mine, rows)

    part = dot_nt(rows[...], down_ref[...])

    @pl.when(step == 0)
    def _():
        back_ref[...] = part

    @pl.when(step > 0)
    def _():
        back_ref[...] += part


def up_first_kernel(plan, *refs):
    pieces, (up_ref, total_ref, squares_ref, rows) = refs[:-4], refs[-4:]
    assemble(plan, pieces, rows)
    part = dot(rows[...], up_ref[...])
    values = rows[...].astype(F32)
    square = jnp.broadcast_to(jnp.sum(values * values, axis=1, keepdims=True), squares_ref.shape)

    @pl.when(pl.program_id(0) == 0)
    def _():
        total_ref[...] = part
        squares_ref[...] = square

    @pl.when(pl.program_id(0) > 0)
    def _():
        total_ref[...] += part
        squares_ref[...] += square


def up_last_kernel(plan, features, *refs):
    count = max(b[0] for b in plan) + 1
    pieces = refs[:count]
    up_ref, before_ref, before_squares_ref, back_ref, act_ref, pre_grad_ref, along_ref, total, squares, rows = refs[count:]
    step, steps = pl.program_id(0), pl.num_programs(0)
    assemble(plan, pieces, rows)
    part = dot(rows[...], up_ref[...])
    values = rows[...].astype(F32)
    square = jnp.broadcast_to(jnp.sum(values * values, axis=1, keepdims=True), squares.shape)

    @pl.when(step == 0)
    def _():
        total[...] = before_ref[...] + part
        squares[...] = before_squares_ref[...] + square

    @pl.when(step > 0)
    def _():
        total[...] += part
        squares[...] += square

    @pl.when(step == steps - 1)
    def _():
        scale = lax.rsqrt(squares[:, :1] / features + EPSILON)
        pre = total[...] * scale
        gate = jax.nn.sigmoid(pre)
        act_ref[...] = (pre * gate).astype(BF16)
        pre_grad = (back_ref[...] * gate * (1.0 + pre * (1.0 - gate))).astype(BF16)
        pre_grad_ref[...] = pre_grad
        along = jnp.sum(pre_grad.astype(F32) * pre, axis=1, keepdims=True)
        along_ref[...] = jnp.broadcast_to(scale * along / features, along_ref.shape)


def expert_grad_kernel(plan, pre_grad_ref, up_ref, along_ref, *refs):
    count = len(refs) // 2
    total = dot_nt(pre_grad_ref[...], up_ref[...])
    for piece, at, to, size in plan:
        rows = refs[piece][at : at + size, :].astype(F32)
        refs[count + piece][at : at + size, :] = (
            total[to : to + size, :] - rows * along_ref[to : to + size, :1]
        ).astype(BF16)


def expert_out_kernel(plan, act_ref, down_ref, *outs):
    total = dot(act_ref[...], down_ref[...])
    for piece, at, to, size in plan:
        outs[piece][at : at + size, :] = total[to : to + size, :].astype(BF16)


def on_device(inputs, b_proj, c_proj, log_decay, doc_lengths, expert_ids, gate_weights, w_up, w_down, cotangent):
    tokens, features = inputs.shape[1:]
    heads = log_decay.shape[1]
    state = b_proj.shape[2]
    experts, blocks = lax.axis_size("exp"), lax.axis_size("seq")
    hidden = w_up.shape[2]
    capacity = 3 * tokens // experts
    slots = experts * capacity
    width = features // CHUNKS
    hops = max(1, blocks // 2)
    relayed = experts == 8 and hops == 2
    kinds = ((2, (0, 1, 4, 5)), (4, (0, 1, 2, 3)))

    x, b, c, log, cot = inputs[0], b_proj[0], c_proj[0], log_decay[0], cotangent[0]
    up, down = w_up[0], w_down[0]
    meta = jnp.concatenate([doc_lengths[0], (lax.axis_index("seq") * tokens)[None].astype(jnp.int32)])

    def log_spec(k):
        return pl.BlockSpec((heads // CHUNKS, tokens), lambda i: (k, 0))

    def chunk(k, rows=tokens):
        return pl.BlockSpec((rows, width), lambda i: (0, k))

    def shape(rows, columns, kind=BF16):
        return jax.ShapeDtypeStruct((rows, columns), kind)

    small, part = whole((tokens, state)), whole((tokens, width))
    unit = tokens * width
    head_flops = 2 * tokens * unit

    def offset(a, k):
        return lax.ppermute(a, "exp", [(i, i ^ k) for i in range(experts)])

    def hop(states, step):
        return lax.ppermute(states, "seq", [(i, i + step) for i in range(blocks) if 0 <= i + step < blocks])

    def hop_on(arrived, spec, step, k, after, parts=1):
        if relayed:
            near, far = (b_pack, c_pack) if step > 0 else (c_pack, b_pack)
            wide = arrived.shape[1]
            taken, *sent = call(
                functools.partial(pass_kernel, step > 0, k),
                (1,),
                [SMEM, whole((heads, tokens)) if wide == features else log_spec(k), whole(near.shape), small, spec],
                [whole((tokens, wide))] + [whole((tokens // 2, wide // parts + state))] * parts,
                [shape(tokens, wide)] + [shape(tokens // 2, wide // parts + state)] * parts,
                2 * head_flops,
                5 * unit,
                "pass_states",
                after=after,
            )(meta, log, near, far, arrived)
            passed = [hop(rows, step) for rows in sent]
            return [[taken, rows, rows] for rows in passed], sent[0]
        arrived = [arrived]
        for _ in range(hops - 1):
            kept = call(
                keep_kernel,
                (1,),
                [SMEM, log_spec(k), part],
                part,
                shape(tokens, width),
                unit,
                4 * unit,
                "keep_states",
                after=after,
            )(meta, log, arrived[-1])
            arrived = arrived + [hop(kept, step)]
        return arrived, kept

    if relayed:
        moving = hop(x, 1)
        pack = (tokens + 3 * heads, state)
        b_pack, c_pack, *cots, cot_both = call(
            prepare_kernel,
            (1,),
            [small, small, whole((heads, tokens)), whole((tokens, features)), whole((2, tokens)), whole((2, tokens))],
            [whole(pack)] * 2 + [whole((tokens, width + 128))] * CHUNKS + [whole((2 * tokens, width + 128))],
            [shape(*pack)] * 2 + [shape(tokens, width + 128)] * CHUNKS + [shape(2 * tokens, width + 128)],
            0,
            4 * tokens * features,
            "prepare",
            vmem=VMEM_ALL,
        )(b, c, log, cot, expert_ids[0].T, gate_weights[0].T)
        b_pack, c_pack = hop(b_pack, 1), hop(c_pack, -1)
    else:
        moving = []
        for k in range(CHUNKS):
            local = call(
                local_kernel,
                (1,),
                [SMEM, log_spec(k), small, chunk(k)],
                part,
                shape(tokens, width),
                head_flops,
                4 * unit,
                "local_states",
            )(meta, log, b, x)
            moving.append(hop(local, 1))
        cots = [cot[:, k * width : (k + 1) * width] for k in range(CHUNKS)]

    def tick(arrived):
        mark = call(
            tick_kernel, (1,), [], whole((16, 128)), shape(16, 128), 0, 0, "tick", after=[arrived]
        )()
        return offset(mark, 1)

    if relayed:
        plans = [
            [
                block
                for i, o in enumerate(offsets)
                for block in ((i, 0, o * capacity, capacity), (i, capacity, (o ^ by) * capacity, capacity))
            ]
            for by, offsets in kinds
        ]
        pieces_of = [[2 * capacity] * 4] * 2
        pick_shape = (4, 2, capacity, tokens)
        weight_shape = (4, tokens, 2 * capacity)
        outs = [pick_shape, weight_shape, weight_shape] * 2
        me = lax.axis_index("exp").astype(jnp.int32)[None]
        other_cots = [offset(rows, by) for rows, (by, _) in zip(cots, kinds)]
        found = call(
            functools.partial(relay_pick_kernel, experts, capacity, kinds),
            (1,),
            [SMEM] + [pl.BlockSpec((tokens, 128), lambda i: (0, width // 128))] * 3,
            [whole(s) for s in outs],
            [jax.ShapeDtypeStruct(s, BF16) for s in outs],
            6 * experts * tokens * tokens,
            4 * slots * tokens,
            "pick_rows",
        )(me, cots[0], *other_cots)
        picks, own_weights, relay_weights = found[0::3], found[1::3], found[2::3]
    else:
        table = jnp.concatenate([expert_ids[0].T.astype(F32), gate_weights[0].T], axis=0)
        other_cots = [None] * CHUNKS
        plans = [[(0, 0, 0, slots)]] * 2
        pieces_of = [[slots]] * 2
        pick, weights = call(
            functools.partial(direct_pick_kernel, experts, capacity),
            (1,),
            [whole((4, tokens))],
            [whole((slots, tokens)), whole((1, tokens, slots))],
            [shape(slots, tokens), jax.ShapeDtypeStruct((1, tokens, slots), BF16)],
            2 * experts * tokens * tokens,
            4 * slots * tokens,
            "pick_rows",
        )(table)
        picks, own_weights = [pick] * 2, [weights] * 2

    def piece_specs(kind):
        return [whole((rows, width)) for rows in pieces_of[kind]]

    def piece_shapes(kind):
        return [shape(rows, width) for rows in pieces_of[kind]]

    def switch(pieces):
        parts = pieces[0].reshape(experts, capacity, width)
        return [lax.all_to_all(parts, "exp", split_axis=0, concat_axis=0, tiled=True).reshape(slots, width)]

    def to_experts(rows, k, other, after=()):
        kind = k % 2
        cost = (2 * slots * unit, 2 * (unit + slots * width))
        if not relayed:
            sent = call(
                direct_gather_kernel,
                (1,),
                [whole((slots, tokens)), part],
                piece_specs(kind),
                piece_shapes(kind),
                *cost,
                "gather",
                after=after,
            )(picks[kind], rows)
            return sent, switch(sent)
        _, offsets = kinds[kind]
        sent = call(
            gather_kernel,
            (1,),
            [whole(picks[kind].shape), part, part],
            piece_specs(kind),
            piece_shapes(kind),
            *cost,
            "gather",
            after=after,
        )(picks[kind], rows, other)
        return sent, [piece if o == 0 else offset(piece, o) for piece, o in zip(sent, offsets)]

    def other_of(rows, k):
        return offset(rows, kinds[k % 2][0]) if relayed else None

    def to_positions(pieces, k, after=()):
        kind = k % 2
        if not relayed:
            arrived = switch(pieces)
            return arrived[0], arrived
        by, offsets = kinds[kind]
        pieces = [piece if o == 0 else offset(piece, o) for piece, o in zip(pieces, offsets)]
        relay = call(
            relay_kernel,
            (1,),
            [whole(relay_weights[kind].shape)] + piece_specs(kind),
            part,
            shape(tokens, width),
            2 * slots * unit,
            2 * (unit + slots * width),
            "relay",
            after=after,
        )(relay_weights[kind], *pieces)
        return relay, pieces + [offset(relay, by)]

    def moved_specs(kind):
        return piece_specs(kind) + ([part] if relayed else [])

    inner = call(
        inner_kernel,
        (CHUNKS,),
        [SMEM, pl.BlockSpec((heads // CHUNKS, tokens), lambda i: (i, 0)), small, small, columns(tokens, width)],
        columns(tokens, width),
        shape(tokens, features, F32),
        2 * CHUNKS * head_flops,
        6 * CHUNKS * unit,
        "inner",
    )(meta, log, b, c, x)
    if relayed:
        [first_in], kept = hop_on(moving, whole((tokens, features)), 1, 0, [inner, picks[0]])
        second_in = first_in
    else:
        first_in, kept = hop_on(moving[0], part, 1, 0, [inner, picks[0]])
    if relayed:
        held = call(
            hold_kernel,
            (1,),
            [anywhere] * 3,
            [anywhere] * 3,
            [shape(tokens, width + 128)] * 2 + [shape(2 * tokens, width + 128)],
            0,
            0,
            "hold",
            after=[moving, inner, b_pack, c_pack],
            aliases={0: 0, 1: 1, 2: 2},
        )(*other_cots, cot_both)
        cot_sibling = offset(held[2], 1)
        side_others = [offset(rows, 1) for rows in held[:2]]
        table_spec = pl.BlockSpec((tokens, 128), lambda i: (0, width // 128))
        side_kinds = ((2, 4), (4, 2))
        side_plans = [
            [
                (e, j * capacity, (to ^ source) * capacity, capacity)
                for e, to in enumerate((0, partner))
                for j, source in enumerate((0, by, 1, by ^ 1))
            ]
            for by, partner in side_kinds
        ]
        side_shape, side_weight_shape = (2, 4, capacity, tokens), (4, 2, tokens, capacity)
        found = call(
            functools.partial(side_pick_kernel, experts, capacity, side_kinds),
            (1,),
            [SMEM] + [table_spec] * 6,
            [whole(side_shape)] * 4,
            [jax.ShapeDtypeStruct(side_shape, kind) for kind in (BF16, F32)] * 2,
            12 * experts * tokens * tokens,
            8 * slots * tokens,
            "side_picks",
        )(me, cots[0], cot_sibling, held[0], side_others[0], held[1], side_others[1])
        side_picks, side_gated = found[0::2], found[1::2]
        side_spec = whole((4 * capacity, width))
        both = [pl.BlockSpec((tokens, width), lambda i, k=k: (k, 0)) for k in range(2)]
        sent = call(
            side_gather_kernel,
            (1,),
            [whole(side_shape)] * 2 + [spec for k in range(2) for spec in (part, part, both[k], part)],
            [side_spec] * 4,
            [shape(4 * capacity, width)] * 4,
            4 * slots * unit,
            8 * slots * width,
            "side_gather",
            after=[kept],
        )(*side_picks, *[r for k in range(2) for r in (cots[k], held[k], cot_sibling, side_others[k])])
        got_cot = [[sent[2 * k], offset(sent[2 * k + 1], side_kinds[k][1])] for k in range(2)]
        sent = sent[1]
        early = [[], [pieces[1] for pieces in got_cot]]
    else:
        got_cot, sent, early = [], kept, [[], []]
        for k in range(CHUNKS):
            (sent, *_), pieces = to_experts(cots[k], k, other_cots[k], [sent])
            got_cot.append(pieces)
    if not relayed:
        second_in, _ = hop_on(moving[1], part, 1, 1, [sent])
    states_in = [first_in, second_in]


    def states_specs(k, w):
        if not relayed:
            return [part] * hops
        return [
            chunk(k),
            chunk(k, tokens // 2),
            pl.BlockSpec((tokens // 2, state), lambda i: (0, w // state)),
        ]

    resid, squares, others = [], [], []
    for k in range(CHUNKS):
        rows, square = call(
            functools.partial(resid_kernel, relayed),
            (1,),
            [SMEM, log_spec(k), small, chunk(k)] + states_specs(k, features),
            [part, whole((tokens, 128))],
            [shape(tokens, width), shape(tokens, 128, F32)],
            hops * head_flops,
            (6 + 2 * hops) * unit,
            "resid",
            after=early[k],
        )(meta, log, c, inner, *states_in[k])
        resid.append(rows)
        squares.append(square)
        others.append(other_of(rows, k))

    each = 2
    step = width // each
    chunk_flops = 2 * slots * width * hidden
    chunk_bytes = 2 * width * (hidden + slots)
    slots_hidden = whole((slots, hidden))

    def step_specs(kind, first=0):
        return [
            pl.BlockSpec((rows, step), lambda i: (0, jnp.clip(i - first, 0, each - 1))) for rows in pieces_of[kind]
        ]

    if relayed:
        cot_plans = side_plans
        cot_specs = [
            pl.BlockSpec((4 * capacity, step), lambda i, k=k: (0, jnp.clip(i - each * k, 0, each - 1)))
            for k in range(CHUNKS)
            for _ in range(2)
        ]
    else:
        cot_plans = [plans[k % 2] for k in range(CHUNKS)]
        cot_specs = [spec for k in range(CHUNKS) for spec in step_specs(k % 2, each * k)]
    back = call(
        functools.partial(back_kernel, cot_plans),
        (each * CHUNKS,),
        cot_specs + [columns(hidden, step)],
        slots_hidden,
        shape(slots, hidden, F32),
        CHUNKS * chunk_flops,
        CHUNKS * chunk_bytes,
        "back",
        [pltpu.VMEM((slots, step), BF16)],
        after=[resid[1]],
    )(*[piece for pieces in got_cot for piece in pieces], down)
    (sent, *_), pieces = to_experts(resid[0], 0, others[0], [back])
    got_in = [pieces]
    _, pieces = to_experts(resid[1], 1, others[1], [sent])
    got_in.append(pieces)

    def up_spec(k):
        return pl.BlockSpec((step, hidden), lambda i: (each * k + i, 0))

    slots_small = whole((slots, 128))
    total, total_squares = call(
        functools.partial(up_first_kernel, plans[0]),
        (each,),
        step_specs(0) + [up_spec(0)],
        [slots_hidden, slots_small],
        [shape(slots, hidden, F32), shape(slots, 128, F32)],
        chunk_flops,
        chunk_bytes,
        "up_first",
        [pltpu.VMEM((slots, step), BF16)],
    )(*got_in[0], up)
    act, pre_grad, along = call(
        functools.partial(up_last_kernel, plans[1], features),
        (each,),
        step_specs(1) + [up_spec(1), slots_hidden, slots_small, slots_hidden],
        [slots_hidden, slots_hidden, slots_small],
        [shape(slots, hidden), shape(slots, hidden), shape(slots, 128, F32)],
        chunk_flops,
        chunk_bytes,
        "up_last",
        [pltpu.VMEM((slots, hidden), F32), pltpu.VMEM((slots, 128), F32), pltpu.VMEM((slots, step), BF16)],
    )(*got_in[1], up, total, total_squares, back)

    got_grad, grads, last = [], [], []
    for k in range(CHUNKS):
        kind = k % 2
        expert_grad = call(
            functools.partial(expert_grad_kernel, plans[kind]),
            (each,),
            [slots_hidden, up_spec(k), slots_small] + step_specs(kind),
            step_specs(kind),
            piece_shapes(kind),
            chunk_flops,
            chunk_bytes,
            "expert_grad",
            after=last,
        )(pre_grad, up, along, *got_in[k])
        last = expert_grad[:1]
        grads.append(expert_grad)
    outs = []
    for k in range(CHUNKS):
        kind = k % 2
        expert_out = call(
            functools.partial(expert_out_kernel, side_plans[k] if relayed else plans[kind]),
            (each,),
            [slots_hidden, pl.BlockSpec((hidden, step), lambda i, k=k: (0, each * k + i))],
            [pl.BlockSpec((4 * capacity, step), lambda i: (0, i))] * 2 if relayed else step_specs(kind),
            [shape(4 * capacity, width)] * 2 if relayed else piece_shapes(kind),
            chunk_flops,
            chunk_bytes,
            "expert_out",
            after=last,
        )(act, down)
        outs.append(expert_out)
        last = expert_out[:1]

    for k in range(CHUNKS):
        relay, pieces = to_positions(grads[k], k, last)
        got_grad.append(pieces)
        last = [relay]
    last = relay

    def weights_spec(kind):
        return whole(own_weights[kind].shape)

    dresid, states_after = [], []
    if relayed:
        dresid_whole = call(
            functools.partial(dresid_all_kernel, features),
            (1,),
            [weights_spec(k) for k in range(2)]
            + [whole((tokens, features))]
            + [whole((tokens, 128))] * 2
            + [spec for k in range(2) for spec in moved_specs(k)],
            whole((tokens, features)),
            shape(tokens, features),
            4 * slots * unit,
            8 * unit + 4 * slots * width,
            "dresid",
            after=[last],
        )(*own_weights, cot, *squares, *got_grad[0], *got_grad[1])
        moving_back = hop(dresid_whole, -1)
        last = dresid_whole
    else:
        for k in range(CHUNKS):
            kind = k % 2
            grads_here = call(
                functools.partial(dresid_kernel, CHUNKS, features),
                (1,),
                [SMEM, log_spec(k), small, weights_spec(kind), chunk(k)]
                + [whole((tokens, 128))] * CHUNKS
                + moved_specs(kind),
                [part] * (1 if relayed else 2),
                [shape(tokens, width)] * (1 if relayed else 2),
                head_flops + 2 * slots * unit,
                6 * unit + 2 * slots * width,
                "dresid",
                after=[last],
            )(meta, log, c, own_weights[kind], cot, *squares, *got_grad[k])
            dresid.append(grads_here[0])
            states_after.append(hop(grads_here[-1], -1))
            last = dresid[k]
    inner_back = []
    if relayed:
        last = inner_back_whole = call(
            inner_back_kernel,
            (CHUNKS,),
            [SMEM, pl.BlockSpec((heads // CHUNKS, tokens), lambda i: (i, 0)), small, small, columns(tokens, width)],
            columns(tokens, width),
            shape(tokens, features, F32),
            2 * CHUNKS * head_flops,
            6 * CHUNKS * unit,
            "inner_back",
            after=[last],
        )(meta, log, b, c, dresid_whole)
    else:
        for k in range(CHUNKS):
            last = call(
                inner_back_kernel,
                (1,),
                [SMEM, log_spec(k), small, small, part],
                part,
                shape(tokens, width, F32),
                2 * head_flops,
                6 * unit,
                "inner_back",
                after=[last],
            )(meta, log, b, c, dresid[k])
            inner_back.append(last)
    got_out = []
    if relayed:
        held = call(
            hold_kernel,
            (1,),
            [anywhere] * 2,
            [anywhere] * 2,
            [shape(4 * capacity, width)] * 2,
            0,
            0,
            "hold",
            after=[dresid_whole],
            aliases={0: 0, 1: 1},
        )(outs[0][1], outs[1][1])
        side_weights = call(
            side_weights_kernel,
            (1,),
            [whole(side_shape)] * 2,
            [whole(side_weight_shape)] * 2,
            [jax.ShapeDtypeStruct(side_weight_shape, BF16)] * 2,
            0,
            16 * slots * tokens,
            "side_weights",
            after=outs[0][:1],
        )(*side_gated)
        out_pieces = [[outs[k][0], offset(held[k], side_kinds[k][1])] for k in range(2)]
        operands = [*side_weights, *out_pieces[0], *out_pieces[1]]
        specs = [whole(side_weight_shape)] * 2 + [side_spec] * 4
        sums = call(
            side_sums_kernel,
            (1,),
            specs,
            [part] * 4,
            [shape(tokens, width)] * 4,
            4 * slots * unit,
            8 * slots * width,
            "side_sums",
            after=[last],
        )(*operands)
        sums_here = [offset(rows, 1) for rows in sums]
        sent = call(
            side_relay_kernel,
            (1,),
            specs + [part] * 2,
            [part] * 2,
            [shape(tokens, width)] * 2,
            4 * slots * unit,
            8 * slots * width,
            "side_relay",
        )(*operands, *sums_here[:2])
        after_whole, last = hop_on(moving_back, whole((tokens, features)), -1, 0, [sent[0]], CHUNKS)
        relayed_sums = [offset(sent[k], side_kinds[k][0]) for k in range(2)]
    else:
        for k in range(CHUNKS):
            states_after[k], last = hop_on(states_after[k], part, -1, k, [last])
            last, pieces = to_positions(outs[k], k, [last])
            got_out.append(pieces)

    def placed(kernel, k, in_specs, operands, earlier, after, flops, nbytes, name):
        more = [] if earlier is None else [earlier]
        return call(
            kernel,
            (1,),
            in_specs + [pl.BlockSpec(memory_space=pl.ANY)] * len(more),
            chunk(k),
            shape(tokens, features),
            flops,
            nbytes,
            name,
            after=after,
            aliases={len(operands): 0} if more else {},
        )(*operands, *more)

    def input_grads(k, earlier, after):
        return placed(
            functools.partial(grad_kernel, 3 if relayed else hops, relayed),
            k,
            [SMEM, log_spec(k), small, part] + states_specs(0, width),
            [meta, log, b, inner_back[k], *states_after[k]],
            earlier,
            after,
            hops * head_flops,
            (6 + 2 * hops) * unit,
            "input_grad",
        )

    if relayed:
        pass
    else:
        input_grad, output = input_grads(0, None, [last]), None
    if relayed:
        output, mark = call(
            side_output_kernel,
            (1,),
            [whole(side_weight_shape)] * 2
            + [part] * 2
            + [spec for k in range(2) for spec in (side_spec, side_spec, part, part)],
            [whole((tokens, features)), whole((16, 128))],
            [shape(tokens, features), shape(16, 128)],
            2 * slots * unit,
            8 * unit + 4 * slots * width,
            "output",
            after=[last],
        )(*side_weights, *resid, *[r for k in range(2) for r in (*out_pieces[k], sums_here[2 + k], relayed_sums[k])])
        input_grad = None
        for k in range(CHUNKS):
            more = [] if input_grad is None else [input_grad]
            input_grad = call(
                functools.partial(grad_kernel, 3, relayed),
                (1,),
                [SMEM, log_spec(k), small, chunk(k), chunk(k)]
                + [whole((tokens // 2, width)), pl.BlockSpec((tokens // 2, state), lambda i: (0, width // state))]
                + [anywhere] * len(more),
                chunk(k),
                shape(tokens, features),
                hops * head_flops,
                (6 + 2 * hops) * unit,
                "input_grad",
                after=[mark] if k == 0 else [],
                aliases={7: 0} if more else {},
                vmem=VMEM_BYTES,
            )(meta, log, b, inner_back_whole, *after_whole[k], *more)
    else:
        for k in range(CHUNKS):
            kind = k % 2
            output = placed(
                output_kernel,
                k,
                [weights_spec(kind), part] + moved_specs(kind),
                [own_weights[kind], resid[k], *got_out[k]],
                output,
                [input_grad] if output is None else [],
                2 * slots * unit,
                4 * unit + 2 * slots * width,
                "output",
            )
    if not relayed:
        input_grad = input_grads(1, input_grad, [output])
    return (output[None], input_grad[None])


def solution(mesh):
    placed = (
        P("exp", "seq", None),
        P("exp", "seq", None),
        P("exp", "seq", None),
        P("exp", None, "seq"),
        P("exp", None),
        P("exp", "seq", None),
        P("exp", "seq", None),
        P("exp", None, None),
        P("exp", None, None),
        P("exp", "seq", None),
    )
    return jax.shard_map(
        on_device,
        mesh=mesh,
        in_specs=placed,
        out_specs=(P("exp", "seq", None), P("exp", "seq", None)),
        check_vma=False,
    )
```
